32 devices in a mesh: section: 4 (over y, x), dp: 8 (over z, core).
Axes of the slice: x: 2, y: 2, z: 4, core: 2. Of those that a mesh axis runs over, the one named last changes fastest.
Arguments:
- inputs: bfloat16 [48, 512, 768], P('dp'), may hold values from -6 to 6
- bucket: int32 [48], P('dp'), may hold values from 0 to 3, as said below
- padding: int32 [48, 512], P('dp'), may hold values from 0 to 1, as said below
- cotangent: bfloat16 [48, 512, 768], P('dp'), may hold values from -6 to 6
- down_weight: bfloat16 [4, 768, 64], P('section'), may hold values from -0.21875 to 0.21875
- down_bias: float32 [4, 64], P('section'), may hold values from -3 to 3
- up_weight: bfloat16 [4, 64, 768], P('section'), may hold values from -0.75 to 0.75
- up_bias: float32 [4, 768], P('section'), may hold values from -2 to 2
- ln_gain: float32 [4, 768], P('section'), may hold values from 0.1 to 1.9
- ln_beta: float32 [4, 768], P('section'), may hold values from -2 to 2
- qkv_weight: bfloat16 [2, 768, 2304], P(None, 'dp'), may hold values from -0.21875 to 0.21875
- query_bias: float32 [2, 768], replicated, may hold values from -2 to 2
- value_bias: float32 [2, 768], replicated, may hold values from -2 to 2
- attn_out_weight: bfloat16 [2, 768, 768], P(None, 'dp'), may hold values from -1.25 to 1.25
- attn_out_bias: float32 [2, 768], replicated, may hold values from -2 to 2
- ffn_in_weight: bfloat16 [2, 768, 3072], P(None, 'dp'), may hold values from -0.21875 to 0.21875
- ffn_in_bias: float32 [2, 3072], replicated, may hold values from -2 to 2
- ffn_out_weight: bfloat16 [2, 3072, 768], P(None, 'dp'), may hold values from -0.15625 to 0.15625
- ffn_out_bias: float32 [2, 768], replicated, may hold values from -2 to 2
Outputs:
- sub_outputs: bfloat16 [4, 48, 512, 768], P('section', 'dp')
- sub_input_grads: bfloat16 [4, 48, 512, 768], P('section', 'dp')
- grad_down_weight: float32 [4, 768, 64], P('section')
- grad_down_bias: float32 [4, 64], P('section')
- grad_up_weight: float32 [4, 64, 768], P('section')
- grad_up_bias: float32 [4, 768], P('section')
- grad_ln_gain: float32 [4, 768], P('section')
- grad_ln_beta: float32 [4, 768], P('section')
- ratios: float32 [4], P('section')
The draws below stay inside these ranges and needn't reach their ends.
Inputs may be any that keep to these rules, and one draw needn't show every extreme that they name: A row holds sequences of 64 * 2**bucket positions each, one after the other. `padding`: within each sequence of a row the ones come first, and each sequence has at least one.
All inputs are finite; a program needn't handle non-finite values.
Results may differ from the reference program's by a relative error of at most 0.024.
Values may be sent and summed in bfloat16 or wider, within the bound.
A program may use at most 320 MiB of HBM per device.

```python
import jax
import jax.numpy as jnp
from jax import lax

D = 768
HEADS = 12
HD = 64
FF = 3072
AD = 64
SUBS = 4
LAYERS = 2
SEG = 64
LEN = 512
SEQS = 48


def shared_rows(key):
    bucket_ids = jax.random.randint(jax.random.fold_in(key, 11), (SEQS,), 0, 4).astype(jnp.int32)
    seq_span = SEG * jnp.left_shift(jnp.int32(1), bucket_ids)
    raw_lengths = jax.random.randint(jax.random.fold_in(key, 12), (SEQS, 8), 0, 1 << 20).astype(jnp.int32)
    seq_lengths = 1 + raw_lengths % seq_span[:, None]
    places = jnp.arange(LEN, dtype=jnp.int32)
    which_seq = places[None, :] // seq_span[:, None]
    row_lengths = jnp.take_along_axis(seq_lengths, which_seq, 1)
    marks = (places[None, :] % seq_span[:, None] < row_lengths).astype(jnp.int32)
    return (bucket_ids, marks)


def draw_bucket(key, part):
    return shared_rows(key)[0]


def draw_padding(key, part):
    return shared_rows(key)[1]


def block_levels(stream_key, extent, pieces, low, largest):
    def one(axis_at, shards_of):
        draws = jax.random.uniform(jax.random.fold_in(jax.random.fold_in(stream_key, 6), axis_at), (shards_of,), jnp.float32, low / len(pieces), largest / len(pieces))
        return jnp.repeat(jnp.exp(draws), extent[axis_at] // shards_of).reshape((-1,) + (1,) * (len(extent) - axis_at - 1))

    factor_of = one(*pieces[0])
    for cut in pieces[1:]:
        factor_of = factor_of * one(*cut)
    return factor_of


def bell_draw(rng, shape, spread, most, shards=(), held_as=jnp.bfloat16):
    entries = jax.random.normal(rng, shape, jnp.float32) * spread
    if len(shards) > 0:
        entries = block_levels(rng, shape, shards, -0.22, 0.18) * entries
    return jnp.clip(entries, min=-most, max=most).astype(held_as)


def setup_inputs(seed: int = 0) -> dict:
    arg_keys = jax.random.split(jax.random.key(seed), 20)
    inputs = bell_draw(arg_keys[0], (SEQS, LEN, D), 1.0, 6.0, ((0, 8),))
    bucket = draw_bucket(jax.random.fold_in(arg_keys[19], 71), 0)
    padding = draw_padding(jax.random.fold_in(arg_keys[19], 71), 0)
    cotangent = bell_draw(arg_keys[3], (SEQS, LEN, D), 1.0, 6.0, ((0, 8),))
    down_weight = bell_draw(arg_keys[4], (SUBS, D, AD), D ** -0.5, 0.21875, ((0, 4),))
    down_bias = bell_draw(arg_keys[5], (SUBS, AD), 0.5, 3.0, ((0, 4),), jnp.float32)
    up_weight = bell_draw(arg_keys[6], (SUBS, AD, D), AD ** -0.5, 0.75, ((0, 4),))
    up_bias = bell_draw(arg_keys[7], (SUBS, D), 0.3, 2.0, ((0, 4),), jnp.float32)
    ln_gain = jnp.clip(1.0 + 0.18 * jax.random.normal(arg_keys[8], (SUBS, D), jnp.float32), 0.1, 1.9)
    ln_beta = bell_draw(arg_keys[9], (SUBS, D), 0.3, 2.0, ((0, 4),), jnp.float32)
    qkv_weight = bell_draw(arg_keys[10], (LAYERS, D, 3 * D), D ** -0.5, 0.21875, ((1, 8),))
    query_bias = bell_draw(arg_keys[11], (LAYERS, D), 0.3, 2.0, (), jnp.float32)
    value_bias = bell_draw(arg_keys[12], (LAYERS, D), 0.3, 2.0, (), jnp.float32)
    attn_out_weight = bell_draw(arg_keys[13], (LAYERS, D, D), (D // 32) ** -0.5, 1.25, ((1, 8),))
    attn_out_bias = bell_draw(arg_keys[14], (LAYERS, D), 0.3, 2.0, (), jnp.float32)
    ffn_in_weight = bell_draw(arg_keys[15], (LAYERS, D, FF), D ** -0.5, 0.21875, ((1, 8),))
    ffn_in_bias = bell_draw(arg_keys[16], (LAYERS, FF), 0.3, 2.0, (), jnp.float32)
    ffn_out_weight = bell_draw(arg_keys[17], (LAYERS, FF, D), (FF // 2) ** -0.5, 0.15625, ((1, 8),))
    ffn_out_bias = bell_draw(arg_keys[18], (LAYERS, D), 0.3, 2.0, (), jnp.float32)
    return dict(inputs=inputs, bucket=bucket, padding=padding, cotangent=cotangent, down_weight=down_weight, down_bias=down_bias, up_weight=up_weight, up_bias=up_bias, ln_gain=ln_gain, ln_beta=ln_beta, qkv_weight=qkv_weight, query_bias=query_bias, value_bias=value_bias, attn_out_weight=attn_out_weight, attn_out_bias=attn_out_bias, ffn_in_weight=ffn_in_weight, ffn_in_bias=ffn_in_bias, ffn_out_weight=ffn_out_weight, ffn_out_bias=ffn_out_bias)


HIGHEST = lax.Precision.HIGHEST
EPSILON = 1e-05
MASKED = -1e+30

@jax.custom_vjp
def low(v):
    return lax.optimization_barrier(v.astype(jnp.bfloat16)).astype(jnp.float32)

@jax.custom_vjp
def low_back(v):
    return v

def low_keep(v):
    return (low(v), None)

def low_pass(kept, grad):
    return (grad,)

def back_keep(v):
    return (v, None)

def back_low(kept, grad):
    return (low(grad),)
low.defvjp(low_keep, low_pass)
low_back.defvjp(back_keep, back_low)

def matmul(left, right):
    return jnp.dot(left, right, precision=HIGHEST)

def gelu(values):
    return jax.nn.gelu(values, approximate=False)

def layer_norm(resid, gain, beta):
    center = resid - lax.optimization_barrier(jnp.mean(resid, -1, keepdims=True))
    variance = lax.optimization_barrier(jnp.mean(center * center, -1, keepdims=True))
    return center * lax.rsqrt(variance + EPSILON) * gain + beta

def allowed_keys(bucket_row, pad_row):
    seq_span = SEG * jnp.left_shift(jnp.int32(1), bucket_row)
    places = jnp.arange(LEN, dtype=jnp.int32)
    same_piece = places[:, None] // seq_span == places[None, :] // seq_span
    return same_piece & (pad_row[None, :] == 1)

def split_heads(matrix):
    return matrix.reshape(LEN, HEADS, HD)

def attention_branch(hidden, allowed, qkv_mat, query_shift, value_shift, out_mat, out_shift):
    mixed = matmul(hidden, qkv_mat)
    query = low_back(low(mixed[:, :D] + query_shift))
    keys_part = low_back(low(mixed[:, D:2 * D]))
    values_part = low_back(low(mixed[:, 2 * D:] + value_shift))
    scores = jnp.einsum('qhd,khd->hqk', split_heads(query), split_heads(keys_part), precision=HIGHEST)
    scores = low_back(scores * HD ** (-0.5))
    scores = jnp.where(allowed[None], scores, MASKED)
    weights_soft = jax.nn.softmax(scores, axis=-1)
    attended = jnp.einsum('hqk,khd->qhd', low(weights_soft), split_heads(values_part), precision=HIGHEST)
    attended = low_back(low(attended.reshape(LEN, D)))
    return low_back(matmul(attended, out_mat) + out_shift)

def ffn_branch(hidden, in_mat, in_shift, out_mat, out_shift):
    pre_act = low_back(matmul(hidden, in_mat) + in_shift)
    return low_back(matmul(low(gelu(pre_act)), out_mat) + out_shift)

def row_forward(train_params, frozen, x_row, probe_row, bucket_row, pad_row):
    down_mats, down_shifts, lift_mats, lift_shifts, gains, betas = train_params
    qkv_all, query_all, value_all, attn_mats, attn_shifts, in_mats, in_shifts, out_mats, out_shifts = frozen
    allowed = allowed_keys(bucket_row, pad_row)
    valid_row = pad_row.astype(jnp.float32)
    hidden = x_row
    results = []
    square_sums = []
    for block_index in range(SUBS):
        hidden = hidden + probe_row[block_index]
        layer_index = block_index // 2
        if block_index % 2 == 0:
            branch = attention_branch(hidden, allowed, qkv_all[layer_index], query_all[layer_index], value_all[layer_index], attn_mats[layer_index], attn_shifts[layer_index])
        else:
            branch = ffn_branch(hidden, in_mats[layer_index], in_shifts[layer_index], out_mats[layer_index], out_shifts[layer_index])
        down_act = low_back(matmul(low(branch), down_mats[block_index]) + down_shifts[block_index])
        lifted = low_back(matmul(low(gelu(down_act)), lift_mats[block_index]) + lift_shifts[block_index])
        resid = hidden + branch + lifted
        output = low(layer_norm(resid, gains[block_index], betas[block_index]))
        square_sums.append(jnp.stack([jnp.sum(valid_row * lax.optimization_barrier(jnp.sum(lifted * lifted, -1))), jnp.sum(valid_row * lax.optimization_barrier(jnp.sum(hidden * hidden, -1)))]))
        results.append(output)
        hidden = low_back(output)
    return (jnp.stack(results), jnp.stack(square_sums))

def reference(inputs, bucket, padding, cotangent, down_weight, down_bias, up_weight, up_bias, ln_gain, ln_beta, qkv_weight, query_bias, value_bias, attn_out_weight, attn_out_bias, ffn_in_weight, ffn_in_bias, ffn_out_weight, ffn_out_bias):
    frozen = tuple((member.astype(jnp.float32) for member in (qkv_weight, query_bias, value_bias, attn_out_weight, attn_out_bias, ffn_in_weight, ffn_in_bias, ffn_out_weight, ffn_out_bias)))
    trainable = tuple((member.astype(jnp.float32) for member in (down_weight, down_bias, up_weight, up_bias, ln_gain, ln_beta)))
    probes = jnp.zeros((SEQS, SUBS, LEN, D), jnp.float32)
    rows_in = inputs.astype(jnp.float32)

    def primal(train_params, probe_all):

        def one_row(row_data):
            x_row, probe_row, bucket_row, pad_row = row_data
            return row_forward(train_params, frozen, x_row, probe_row, bucket_row, pad_row)
        return lax.map(jax.checkpoint(one_row), (rows_in, probe_all, bucket, padding))
    (outputs, sums_all), pullback = jax.vjp(primal, trainable, probes)
    start_grad = jnp.zeros_like(outputs).at[:, SUBS - 1].set(cotangent.astype(jnp.float32))
    grad_train, grad_probes = pullback((start_grad, jnp.zeros_like(sums_all)))
    totals = lax.optimization_barrier(jnp.sum(sums_all, 0))
    ratios = jnp.sqrt(totals[:, 0] / totals[:, 1])
    sub_outputs = jnp.transpose(outputs, (1, 0, 2, 3)).astype(jnp.bfloat16)
    sub_input_grads = jnp.transpose(grad_probes, (1, 0, 2, 3)).astype(jnp.bfloat16)
    return (sub_outputs, sub_input_grads, grad_train[0], grad_train[1], grad_train[2], grad_train[3], grad_train[4], grad_train[5], ratios)
```

```python
import functools
import jax
import jax.numpy as jnp
from jax import lax
from jax.experimental import pallas as pl
from jax.experimental.pallas import tpu as pltpu
from jax.sharding import PartitionSpec as P

HEADS = 12
HD = 64
SEG = 64
EPSILON = 1e-05
MASKED = -1e30
LOG_TOP = 24
VMEM_BYTES = 56 * 1024 * 1024
F32 = jnp.float32
BF16 = jnp.bfloat16


def dot(left, right):
    return jnp.dot(left, right, preferred_element_type=F32)


def dot_nt(left, right):
    return lax.dot_general(left, right, (((1,), (1,)), ((), ())), preferred_element_type=F32)


def dot_tn(left, right):
    return lax.dot_general(left, right, (((0,), (0,)), ((), ())), preferred_element_type=F32)


def gelu_both(v):
    bell = jnp.exp(v * v * -0.5)
    t = 1.0 / (1.0 + jnp.abs(v) * (0.3275911 * 0.7071067811865476))
    tail = t * (
        0.127414796
        + t * (-0.142248368 + t * (0.7107068705 + t * (-0.7265760135 + t * 0.5307027145)))
    )
    tail = tail * bell
    cdf = jnp.where(v >= 0, 1.0 - tail, tail)
    return (v * cdf, cdf + v * bell * 0.3989422804014327)


def lanes(rows):
    return lax.broadcasted_iota(jnp.int32, (rows, 128), 1)


def adapter_forward(hidden, branch, adapter_ref, vec_ref, base, stage, aux, valid):
    down_t = adapter_ref[0, stage, :64]
    lift = adapter_ref[0, stage, 64:]
    branch_low = branch.astype(BF16)
    down = dot_nt(branch_low, down_t) + vec_ref[0, base + 4 : base + 5, :64]
    act, _ = gelu_both(down)
    lifted = dot(act.astype(BF16), lift) + vec_ref[0, base + 1 : base + 2]
    hidden_float = hidden.astype(F32)
    resid = hidden_float + branch + lifted
    mean = jnp.mean(resid, -1, keepdims=True)
    center = resid - mean
    inverse = lax.rsqrt(jnp.mean(center * center, -1, keepdims=True) + EPSILON)
    normed = center * inverse
    output = (normed * vec_ref[0, base + 2 : base + 3] + vec_ref[0, base + 3 : base + 4]).astype(BF16)
    sums = (
        jnp.sum(lifted * lifted * valid, 0, keepdims=True),
        jnp.sum(hidden_float * hidden_float * valid, 0, keepdims=True),
    )
    return branch_low, down, output, normed.astype(BF16), inverse, sums


def column_copies(weight, kind, chunk, held, sem):
    return pltpu.make_async_copy(weight.at[:, chunk, kind], held.at[chunk], sem)


def row_copies(weight, kind, chunk, held, sem):
    span = held.shape[1]
    return pltpu.make_async_copy(weight.at[pl.ds(chunk * span, span), :, kind], held.at[chunk], sem)


def start_copies(choice, sources, order, sems):
    made = []
    for which, source in enumerate(sources):
        copies = [make(source[matrix][0], source[matrix][1], chunk, held, sems.at[i])
                  for i, (make, matrix, chunk, held) in enumerate(order)]
        made.append(copies)

        @pl.when(choice == which)
        def _():
            for copy in copies:
                copy.start()

    return made[0]


def square(held, chunk):
    width = held.shape[-1]
    return held[chunk].reshape(width, width)


def attention_pair_forward(p, start, size, qkv, keyb, att, aux):
    rows = pl.ds(start, size)
    width = att.shape[1]
    col = pl.multiple_of(p * 128, 128)
    lane = lanes(size)
    query = qkv[rows, pl.ds(col, 128)]
    key = qkv[rows, pl.ds(width + col, 128)]
    value = qkv[rows, pl.ds(2 * width + col, 128)]
    bias = keyb[rows]
    place = start + lax.broadcasted_iota(jnp.int32, (size, 128), 0)
    hot = jnp.where(lane % 64 == place // SEG, 1.0, 0.0).astype(BF16)
    query = query * jnp.asarray(HD ** -0.5, BF16)
    total = None
    for half in range(2):
        mine = (lane < 64) if half == 0 else (lane >= 64)
        scores = dot_nt(jnp.where(mine, query, hot), jnp.where(mine, key, bias))
        peak = jnp.max(scores, -1, keepdims=True)
        expo = jnp.exp(scores - peak)
        norm = jnp.sum(expo, -1, keepdims=True)
        part = dot(expo.astype(BF16), jnp.where(mine, value, jnp.zeros_like(value))) * (1.0 / norm)
        log_total = peak + jnp.log(norm)
        aux[rows] = jnp.where(lane == 80 + 2 * p + half, log_total, aux[rows])
        total = part if total is None else total + part
    att[rows, pl.ds(col, 128)] = total.astype(BF16)


def forward_kernel(
    sources, idx, hidden_ref, keyb_ref, adapter_ref, vec_ref, in_bias_ref,
    h1_ref, h2_ref, qkv_ref, att_ref, br1_ref, nh1_ref, aux1_ref, slope_ref, br2_ref, nh2_ref, aux2_ref, sums_ref,
    attn_v, in_v, out_v, acc, sems,
):
    bucket = idx[1]
    length, width = hidden_ref.shape
    chunks = in_v.shape[0]
    cols = [pl.ds(c * width, width) for c in range(chunks)]
    order = [(column_copies, 0, c, attn_v) for c in range(4)]
    for c in range(chunks):
        order.append((column_copies, 1, c, in_v))
        order.append((row_copies, 2, c, out_v))
    copies = start_copies(idx[2], sources, order, sems)
    hidden = hidden_ref[...]
    valid = keyb_ref[:, 16:17].astype(F32)
    for part in range(3):
        copies[part].wait()
        mixed = dot(hidden, square(attn_v, part))
        if part == 0:
            mixed = mixed + vec_ref[0, 5:6]
        if part == 2:
            mixed = mixed + vec_ref[0, 6:7]
        qkv_ref[:, cols[part]] = mixed.astype(BF16)
    aux1_ref[...] = jnp.zeros_like(aux1_ref)

    def heads(size):
        blocks = length // size

        def body(step, carry):
            p = step // blocks
            start = pl.multiple_of((step % blocks) * size, size)
            attention_pair_forward(p, start, size, qkv_ref, keyb_ref, att_ref, aux1_ref)
            return carry

        lax.fori_loop(0, (HEADS // 2) * blocks, body, 0)

    @pl.when(bucket >= 3)
    def _():
        heads(length)

    @pl.when(bucket < 3)
    def _():
        heads(length // 2)

    copies[3].wait()
    branch = dot(att_ref[...], square(attn_v, 3)) + vec_ref[0, 0:1]
    branch_low, down, output, normed, inverse, sums = adapter_forward(
        hidden, branch, adapter_ref, vec_ref, 0, 0, None, valid
    )
    br1_ref[...] = branch_low
    nh1_ref[...] = normed
    h1_ref[...] = output
    lane = lanes(length)
    aux1_ref[:, :64] = down
    aux1_ref[...] = jnp.where(lane == 64, inverse, aux1_ref[...])
    sums_ref[0:1] = sums[0]
    sums_ref[1:2] = sums[1]
    hidden = h1_ref[...]
    for c in range(chunks):
        copies[4 + 2 * c].wait()
        pre = dot(hidden, square(in_v, c)) + in_bias_ref[0, :, c * width : (c + 1) * width]
        act, slope = gelu_both(pre)
        slope_ref[:, cols[c]] = slope.astype(BF16)
        copies[5 + 2 * c].wait()
        term = dot(act.astype(BF16), square(out_v, c))
        if c == 0:
            acc[...] = term + vec_ref[0, 8:9]
        else:
            acc[...] += term
    branch_low, down, output, normed, inverse, sums = adapter_forward(
        hidden, acc[...], adapter_ref, vec_ref, 8, 1, None, valid
    )
    br2_ref[...] = branch_low
    nh2_ref[...] = normed
    h2_ref[...] = output
    aux2_ref[...] = jnp.where(lane == 64, inverse, jnp.zeros((length, 128), F32))
    aux2_ref[:, :64] = down
    sums_ref[2:3] = sums[0]
    sums_ref[3:4] = sums[1]
    sums_ref[4:8] = jnp.zeros_like(sums_ref[4:8])


def weight_plan(weights):
    arrays, places = [], []
    for layer in weights:
        spots = []
        for array, kind in layer:
            found = [i for i, other in enumerate(arrays) if other is array]
            if not found:
                arrays.append(array)
                found = [len(arrays) - 1]
            spots.append((found[0], kind))
        places.append(spots)
    return arrays, places


def weight_scratch(weights):
    attn, inner, outer = [array.shape for array, _ in weights[0]]
    width = attn[-1]
    span = width // (4 * outer[3])
    return [
        pltpu.VMEM((4, attn[0], attn[3], width), BF16),
        pltpu.VMEM((4, inner[0], inner[3], width), BF16),
        pltpu.VMEM((outer[0] // span, span, 4, outer[3], width), BF16),
    ]


def whole(shape):
    return pl.BlockSpec(shape, lambda i, s: (0,) * len(shape))


def by_layer(shape):
    return pl.BlockSpec((1,) + shape, lambda i, s: (s[0],) + (0,) * len(shape))


def call_with_weights(kernel, weights, blocks, outs, scratch, flops, name):
    arrays, places = weight_plan(weights)
    fixed = len(blocks)
    idx, rest = blocks[0], blocks[1:]

    def body(*refs):
        held = refs[fixed : fixed + len(arrays)]
        sources = [[(held[i], kind) for i, kind in spots] for spots in places]
        kernel(sources, *refs[:fixed], *refs[fixed + len(arrays) :])

    copies = 12
    return pl.pallas_call(
        body,
        grid_spec=pltpu.PrefetchScalarGridSpec(
            num_scalar_prefetch=1,
            grid=(1,),
            in_specs=[spec for _, spec in rest] + [pl.BlockSpec(memory_space=pl.ANY)] * len(arrays),
            out_specs=[whole(shape) for shape, _ in outs],
            scratch_shapes=weight_scratch(weights) + scratch + [pltpu.SemaphoreType.DMA((copies,))],
        ),
        out_shape=[jax.ShapeDtypeStruct(shape, dtype) for shape, dtype in outs],
        compiler_params=pltpu.CompilerParams(vmem_limit_bytes=VMEM_BYTES),
        cost_estimate=pl.CostEstimate(flops=flops, bytes_accessed=24_000_000, transcendentals=0),
        name=name,
    )(idx, *[array for array, _ in rest], *arrays)


def forward_pair(layer, choice, bucket, hidden, keyb, weights, adapters, vecs, in_bias):
    length, width = hidden.shape
    ffn = in_bias.shape[-1]
    idx = jnp.stack([layer, bucket, choice]).astype(jnp.int32)
    outs = [
        ((length, width), BF16), ((length, width), BF16), ((length, 3 * width), BF16), ((length, width), BF16),
        ((length, width), BF16), ((length, width), BF16), ((length, 128), F32), ((length, ffn), BF16),
        ((length, width), BF16), ((length, width), BF16), ((length, 128), F32), ((8, width), F32),
    ]
    blocks = [
        idx, (hidden, whole((length, width))), (keyb, whole((length, 128))), (adapters, by_layer((2, 128, width))),
        (vecs, by_layer((16, width))), (in_bias, by_layer((1, ffn))),
    ]
    scratch = [pltpu.VMEM((length, width), F32)]
    return call_with_weights(forward_kernel, weights, blocks, outs, scratch, 12_000_000_000, "forward_pair")


def adapter_backward(grad, normed, branch_low, aux, adapter_ref, vec_ref, base, stage, grads_ref):
    down_t = adapter_ref[0, stage, :64]
    lift = adapter_ref[0, stage, 64:]
    grad = grad.astype(F32)
    normed = normed.astype(F32)
    inverse = aux[:, 64:65]
    down = aux[:, :64]
    scaled = grad * vec_ref[0, base + 2 : base + 3]
    resid = inverse * (
        scaled
        - jnp.mean(scaled, -1, keepdims=True)
        - normed * jnp.mean(scaled * normed, -1, keepdims=True)
    )
    lift_grad = resid.astype(BF16)
    act, slope = gelu_both(down)
    down_grad = (dot_nt(lift_grad, lift) * slope).astype(BF16)
    grads_ref[stage, 0:64] = dot_tn(act.astype(BF16), lift_grad)
    grads_ref[stage, 64:128] = dot_tn(down_grad, branch_low)
    grads_ref[stage, 128:136] = jnp.zeros_like(grads_ref[stage, 128:136])
    grads_ref[stage, 128:129] = jnp.sum(lift_grad.astype(F32), 0, keepdims=True)
    grads_ref[stage, 129:130] = jnp.sum(normed * grad, 0, keepdims=True)
    grads_ref[stage, 130:131] = jnp.sum(grad, 0, keepdims=True)
    grads_ref[stage, 131:132, :64] = jnp.sum(down_grad.astype(F32), 0, keepdims=True)
    branch_grad = (resid + dot(down_grad, down_t)).astype(BF16)
    return resid, branch_grad


def split_low(column):
    high = column.astype(BF16).astype(F32)
    rest = column - high
    middle = rest.astype(BF16).astype(F32)
    return high, middle, rest - middle


def attention_pair_backward(p, start, size, qkv, keyb, att, aux, att_grad, dqkv):
    rows = pl.ds(start, size)
    width = att.shape[1]
    col = pl.multiple_of(p * 128, 128)
    lane = lanes(size)
    query = qkv[rows, pl.ds(col, 128)] * jnp.asarray(HD ** -0.5, BF16)
    key = qkv[rows, pl.ds(width + col, 128)]
    value = qkv[rows, pl.ds(2 * width + col, 128)]
    grad = att_grad[rows, pl.ds(col, 128)]
    product = grad.astype(F32) * att[rows, pl.ds(col, 128)].astype(F32)
    bias = keyb[rows]
    place = start + lax.broadcasted_iota(jnp.int32, (size, 128), 0)
    spot = lane % 64
    hot = jnp.where(spot == place // SEG, 1.0, 0.0)
    aux_rows = aux[rows]
    zero = jnp.zeros((size, 128), BF16)
    sums = [None, None, None]
    for half in range(2):
        mine = (lane < 64) if half == 0 else (lane >= 64)
        log_total = jnp.sum(jnp.where(lane == 80 + 2 * p + half, aux_rows, 0.0), -1, keepdims=True)
        parts = split_low(-log_total)
        extra = jnp.where(spot == LOG_TOP, parts[0], jnp.where(spot == LOG_TOP + 1, parts[1], jnp.where(spot == LOG_TOP + 2, parts[2], hot)))
        row_dot = jnp.sum(jnp.where(mine, product, 0.0), -1, keepdims=True)
        dots = split_low(-row_dot)
        extra_grad = jnp.where(spot == LOG_TOP, dots[0], jnp.where(spot == LOG_TOP + 1, dots[1], jnp.where(spot == LOG_TOP + 2, dots[2], 0.0)))
        key_side = jnp.where(mine, key, bias)
        value_side = jnp.where(mine, value, bias)
        probs = jnp.exp(dot_nt(key_side, jnp.where(mine, query, extra.astype(BF16))))
        centred = dot_nt(value_side, jnp.where(mine, grad, extra_grad.astype(BF16)))
        score_grad = (probs * centred).astype(BF16)
        terms = (
            dot_tn(score_grad, jnp.where(mine, key, zero)),
            dot(score_grad, jnp.where(mine, query, zero)),
            dot(probs.astype(BF16), jnp.where(mine, grad, zero)),
        )
        sums = [t if s is None else s + t for s, t in zip(sums, terms)]
    dqkv[rows, pl.ds(col, 128)] = (sums[0] * HD ** -0.5).astype(BF16)
    dqkv[rows, pl.ds(width + col, 128)] = sums[1].astype(BF16)
    dqkv[rows, pl.ds(2 * width + col, 128)] = sums[2].astype(BF16)


def backward_kernel(
    sources, idx, grad_ref, keyb_ref, qkv_ref, att_ref, br1_ref, nh1_ref, aux1_ref, slope_ref, br2_ref, nh2_ref,
    aux2_ref, adapter_ref, vec_ref,
    g2_ref, g1_ref, grads_ref,
    attn_v, in_v, out_v, acc, low, dqkv, sems,
):
    bucket = idx[1]
    length, width = grad_ref.shape
    chunks = in_v.shape[0]
    cols = [pl.ds(c * width, width) for c in range(chunks)]
    order = []
    for c in range(chunks):
        order.append((row_copies, 2, c, out_v))
        order.append((column_copies, 1, c, in_v))
    order += [(column_copies, 0, c, attn_v) for c in (3, 0, 1, 2)]
    copies = start_copies(idx[2], sources, order, sems)
    resid, branch_grad = adapter_backward(
        grad_ref[...], nh2_ref[...], br2_ref[...], aux2_ref[...], adapter_ref, vec_ref, 8, 1, grads_ref
    )
    acc[...] = resid
    low[...] = branch_grad
    for c in range(chunks):
        copies[2 * c].wait()
        act_grad = dot_nt(low[...], square(out_v, c))
        pre_grad = (act_grad * slope_ref[:, cols[c]].astype(F32)).astype(BF16)
        copies[2 * c + 1].wait()
        acc[...] += dot_nt(pre_grad, square(in_v, c))
    g2_ref[...] = acc[...].astype(BF16)
    resid, branch_grad = adapter_backward(
        g2_ref[...], nh1_ref[...], br1_ref[...], aux1_ref[...], adapter_ref, vec_ref, 0, 0, grads_ref
    )
    acc[...] = resid
    copies[2 * chunks].wait()
    low[...] = dot_nt(branch_grad, square(attn_v, 3)).astype(BF16)

    def heads(size):
        blocks = length // size

        def body(step, carry):
            p = step // blocks
            start = pl.multiple_of((step % blocks) * size, size)
            attention_pair_backward(p, start, size, qkv_ref, keyb_ref, att_ref, aux1_ref, low, dqkv)
            return carry

        lax.fori_loop(0, (HEADS // 2) * blocks, body, 0)

    @pl.when(bucket >= 3)
    def _():
        heads(length)

    @pl.when(bucket < 3)
    def _():
        heads(length // 2)

    for part in range(3):
        copies[2 * chunks + 1 + part].wait()
        acc[...] += dot_nt(dqkv[:, cols[part]], square(attn_v, part))
    g1_ref[...] = acc[...].astype(BF16)


def backward_pair(layer, choice, bucket, grad, keyb, saved, weights, adapters, vecs):
    length, width = grad.shape
    idx = jnp.stack([layer, bucket, choice]).astype(jnp.int32)
    outs = [((length, width), BF16), ((length, width), BF16), ((2, 136, width), F32)]
    blocks = [idx, (grad, whole((length, width))), (keyb, whole((length, 128)))]
    blocks += [(member, whole(member.shape)) for member in saved]
    blocks += [(adapters, by_layer((2, 128, width))), (vecs, by_layer((16, width)))]
    scratch = [
        pltpu.VMEM((length, width), F32),
        pltpu.VMEM((length, width), BF16),
        pltpu.VMEM((length, 3 * width), BF16),
    ]
    return call_with_weights(backward_kernel, weights, blocks, outs, scratch, 16_000_000_000, "backward_pair")


def key_table(bucket, padding):
    rows, length = padding.shape
    spot = jnp.arange(128, dtype=jnp.int32) % 64
    shift = 6 + bucket[:, None, None]
    place = jnp.arange(length, dtype=jnp.int32)
    same = (spot[None, None, :] * SEG) >> shift == place[None, :, None] >> shift
    real = (padding == 1)[:, :, None]
    table = jnp.where(same & real, 0.0, MASKED)
    ones = (spot >= LOG_TOP) & (spot < LOG_TOP + 3)
    table = jnp.where(spot < 8, table, jnp.where(spot == 16, real.astype(F32), jnp.where(ones, 1.0, 0.0)))
    return table.astype(BF16)


X_PAIRS = [(0, 1), (1, 0), (2, 3), (3, 2)]
Y_PAIRS = [(0, 2), (2, 0), (1, 3), (3, 1)]
CROSS = [(0, 3), (3, 0), (1, 2), (2, 1)]


def send(value, pairs, senders=(0, 1, 2, 3)):
    return lax.ppermute(value, "section", [pair for pair in pairs if pair[0] in senders])


def gather_weights(shards):
    section = lax.axis_index("section")
    quarter = lax.dynamic_index_in_dim(shards, section, 0, keepdims=False)
    full = lax.all_gather(quarter, ("dp", "section"), axis=0, tiled=False)
    count = lax.axis_size("dp")
    full = full.reshape((count, lax.axis_size("section")) + quarter.shape)
    return full


def in_quarters(matrix):
    rows, columns = matrix.shape
    return matrix.reshape(rows, 4, columns // 4).transpose(1, 0, 2)


def block_rows(full, kind, by_rows):
    if full.shape[3] % 16 == 0:
        return (full, kind)
    count, quarters, _, rows, width = full.shape
    one = full[:, :, kind]
    if by_rows:
        return (one.reshape(count * rows * quarters // width, quarters, 1, width // quarters, width), 0)
    return (one.transpose(1, 0, 2, 3).reshape(1, quarters, 1, count * rows, width), 0)


def on_device(
    inputs, bucket, padding, cotangent, down_weight, down_bias, up_weight, up_bias, ln_gain, ln_beta, qkv_weight,
    query_bias, value_bias, attn_out_weight, attn_out_bias, ffn_in_weight, ffn_in_bias, ffn_out_weight, ffn_out_bias,
):
    section = lax.axis_index("section")
    early = section < 2
    side = section % 2
    width = inputs.shape[2]
    adapter_width = down_weight.shape[2]
    layers = qkv_weight.shape[0]

    def layer_shards(layer):
        attn = jnp.concatenate([qkv_weight[layer], attn_out_weight[layer]], 1)
        outer = ffn_out_weight[layer]
        return (
            in_quarters(attn)[:, None],
            jnp.stack([in_quarters(ffn_in_weight[layer]), outer.reshape((4, -1) + outer.shape[1:])], 1),
        )

    weights = []
    for layer in range(layers):
        attn, inner = layer_shards(layer)
        if layer == 0:
            attn_full = gather_weights(attn)
            inner_full = gather_weights(inner)
            weights.append([block_rows(attn_full, 0, False), block_rows(inner_full, 0, False), block_rows(inner_full, 1, True)])
        else:
            full = gather_weights(jnp.concatenate([attn, inner], 1))
            weights.append([block_rows(full, 0, False), block_rows(full, 1, False), block_rows(full, 2, True)])

    zero_row = jnp.zeros((1, width), F32)
    own_vecs = jnp.concatenate(
        [zero_row, up_bias, ln_gain, ln_beta, jnp.pad(down_bias, ((0, 0), (0, width - adapter_width))), zero_row, zero_row, zero_row], 0
    )
    own_pack = jnp.concatenate([down_weight[0].T.astype(F32), up_weight[0].astype(F32), own_vecs], 0)
    packs = lax.all_gather(own_pack, "section", axis=0, tiled=False)
    adapters = packs[:, :128].astype(BF16).reshape(layers, 2, 128, width)
    vecs = packs[:, 128:].reshape(layers, 2, 8, width)
    vecs = vecs.at[:, 0, 0].set(attn_out_bias).at[:, 0, 5].set(query_bias).at[:, 0, 6].set(value_bias)
    vecs = vecs.at[:, 1, 0].set(ffn_out_bias).reshape(layers, 16, width)
    in_bias = ffn_in_bias[:, None, :]

    table = key_table(bucket, padding)
    own = section
    shared = 4 + side

    def row_of(array, row):
        return lax.dynamic_index_in_dim(array, row, 0, keepdims=False)

    def forward(row, hidden, layer, weights_used, choice):
        return forward_pair(
            layer, choice, row_of(bucket, row), hidden, row_of(table, row), weights_used, adapters, vecs, in_bias
        )

    def backward(row, grad, saved, layer, weights_used, choice):
        return backward_pair(
            layer, choice, row_of(bucket, row), grad, row_of(table, row), saved, weights_used, adapters, vecs
        )

    zero = jnp.int32(0)
    one = jnp.int32(1)
    late = 1 - early.astype(jnp.int32)
    first_row = jnp.where(early, shared, own)
    third_row = jnp.where(early, own, shared)

    f0 = forward(first_row, row_of(inputs, first_row), zero, weights[:1], zero)
    x0 = send(jnp.where(side == 0, f0[1], f0[0]), X_PAIRS, (0, 1))
    y0 = send(jnp.where(early | (side == 1), f0[1], f0[0]), Y_PAIRS)
    z0 = send(jnp.where(side == 0, f0[1], f0[0]), CROSS, (2, 3))
    hidden = jnp.where(early, row_of(inputs, own), f0[1])
    f1 = forward(own, hidden, late, weights, late)
    x1 = send(jnp.where(side == 0, f1[1], f1[0]), X_PAIRS)
    hidden = jnp.where(early, f1[1], y0)
    f2 = forward(third_row, hidden, one, weights[1:], zero)
    x2 = send(jnp.where(side == 0, f2[1], f2[0]), X_PAIRS, (2, 3))
    y2 = send(jnp.where(side == 1, f2[1], f2[0]), Y_PAIRS, (0, 1))
    z2 = send(jnp.where(side == 0, f2[1], f2[0]), CROSS, (0, 1))

    b3 = backward(third_row, row_of(cotangent, third_row), f2[2:11], one, weights[1:], zero)
    x3 = send(jnp.where(side == 0, b3[0], b3[1]), X_PAIRS, (2, 3))
    y3 = send(jnp.where(early & (side == 1), b3[0], b3[1]), Y_PAIRS)
    z3 = send(jnp.where(side == 0, b3[0], b3[1]), CROSS, (0, 1))
    grad = jnp.where(early, b3[1], row_of(cotangent, own))
    b4 = backward(own, grad, f1[2:11], late, weights, late)
    x4 = send(jnp.where(side == 0, b4[0], b4[1]), X_PAIRS)
    grad = jnp.where(early, y3, b4[1])
    b5 = backward(first_row, grad, f0[2:11], zero, weights[:1], zero)
    x5 = send(jnp.where(side == 0, b5[0], b5[1]), X_PAIRS, (0, 1))
    y5 = send(jnp.where(side == 1, b5[0], b5[1]), Y_PAIRS, (2, 3))
    z5 = send(jnp.where(side == 0, b5[0], b5[1]), CROSS, (2, 3))

    def assemble(parts):
        result = jnp.zeros(inputs.shape, BF16)
        for row, part in parts:
            result = lax.dynamic_update_index_in_dim(result, part, row, 0)
        return result

    other = section + 1 - 2 * side
    across = jnp.where(early, section + 2, section - 2)
    corner = 3 - section
    other_shared = 4 + 1 - side
    outputs = assemble(
        [
            (own, jnp.where(side == 0, f1[0], f1[1])),
            (other, x1),
            (across, jnp.where(early, y0, y2)),
            (corner, jnp.where(early, z0, z2)),
            (shared, jnp.where(early, jnp.where(side == 0, f0[0], f0[1]), jnp.where(side == 0, f2[0], f2[1]))),
            (other_shared, jnp.where(early, x0, x2)),
        ]
    )
    input_grads = assemble(
        [
            (own, jnp.where(side == 0, b4[1], b4[0])),
            (other, x4),
            (across, jnp.where(early, y5, y3)),
            (corner, jnp.where(early, z5, z3)),
            (shared, jnp.where(early, jnp.where(side == 0, b5[1], b5[0]), jnp.where(side == 0, b3[1], b3[0]))),
            (other_shared, jnp.where(early, x5, x3)),
        ]
    )

    def with_sums(grads, sums):
        squares = jnp.sum(sums[:4].reshape(2, 2, width), -1, keepdims=True)
        return grads.at[:, 132:134].set(jnp.broadcast_to(squares, (2, 2, width)))

    g3, g4, g5 = with_sums(b3[2], f2[11]), with_sums(b4[2], f1[11]), with_sums(b5[2], f0[11])
    low_layer = g5 + jnp.where(early, g4, 0.0)
    high_layer = g3 + jnp.where(early, 0.0, g4)
    mine = lax.psum_scatter(jnp.concatenate([low_layer, high_layer], 0), "section", scatter_dimension=0, tiled=False)
    total = lax.psum(mine, "dp")
    ratios = jnp.sqrt(total[132, 0] / total[133, 0])[None]
    return (
        outputs[None],
        input_grads[None],
        total[64:128].T[None],
        total[131, :adapter_width][None],
        total[0:64][None],
        total[128][None],
        total[129][None],
        total[130][None],
        ratios,
    )


def solution(mesh):
    in_specs = (
        P("dp", None, None),
        P("dp"),
        P("dp", None),
        P("dp", None, None),
        P("section", None, None),
        P("section", None),
        P("section", None, None),
        P("section", None),
        P("section", None),
        P("section", None),
        P(None, "dp", None),
        P(),
        P(),
        P(None, "dp", None),
        P(),
        P(None, "dp", None),
        P(),
        P(None, "dp", None),
        P(),
    )
    out_specs = (
        P("section", "dp", None, None),
        P("section", "dp", None, None),
        P("section", None, None),
        P("section", None),
        P("section", None, None),
        P("section", None),
        P("section", None),
        P("section", None),
        P("section"),
    )
    return jax.shard_map(
        on_device, mesh=mesh, in_specs=in_specs, out_specs=out_specs, check_vma=False
    )
```

```python
import functools
import jax
import jax.numpy as jnp
from jax import lax
from jax.experimental import pallas as pl
from jax.experimental.pallas import tpu as pltpu
from jax.sharding import PartitionSpec as P

HEADS = 12
HD = 64
SEG = 64
EPSILON = 1e-05
MASKED = -1e30
LOG_TOP = 24
VMEM_BYTES = 56 * 1024 * 1024
F32 = jnp.float32
BF16 = jnp.bfloat16


def dot(left, right):
    return jnp.dot(left, right, preferred_element_type=F32)


def dot_nt(left, right):
    return lax.dot_general(left, right, (((1,), (1,)), ((), ())), preferred_element_type=F32)


def dot_tn(left, right):
    return lax.dot_general(left, right, (((0,), (0,)), ((), ())), preferred_element_type=F32)


def gelu_both(v):
    bell = jnp.exp(v * v * -0.5)
    t = 1.0 / (1.0 + jnp.abs(v) * (0.3275911 * 0.7071067811865476))
    tail = t * (
        0.127414796
        + t * (-0.142248368 + t * (0.7107068705 + t * (-0.7265760135 + t * 0.5307027145)))
    )
    tail = tail * bell
    cdf = jnp.where(v >= 0, 1.0 - tail, tail)
    return (v * cdf, cdf + v * bell * 0.3989422804014327)


def lanes(rows):
    return lax.broadcasted_iota(jnp.int32, (rows, 128), 1)


def adapter_forward(hidden, branch, adapter_ref, vec_ref, base, stage, aux, valid):
    down_t = adapter_ref[0, stage, :64]
    lift = adapter_ref[0, stage, 64:]
    branch_low = branch.astype(BF16)
    down = dot_nt(branch_low, down_t) + vec_ref[0, base + 4 : base + 5, :64]
    act, _ = gelu_both(down)
    lifted = dot(act.astype(BF16), lift) + vec_ref[0, base + 1 : base + 2]
    hidden_float = hidden.astype(F32)
    resid = hidden_float + branch + lifted
    mean = jnp.mean(resid, -1, keepdims=True)
    center = resid - mean
    inverse = lax.rsqrt(jnp.mean(center * center, -1, keepdims=True) + EPSILON)
    normed = center * inverse
    output = (normed * vec_ref[0, base + 2 : base + 3] + vec_ref[0, base + 3 : base + 4]).astype(BF16)
    sums = (
        jnp.sum(lifted * lifted * valid, 0, keepdims=True),
        jnp.sum(hidden_float * hidden_float * valid, 0, keepdims=True),
    )
    return branch_low, down, output, normed.astype(BF16), inverse, sums


def column_copies(weight, kind, chunk, held, sem):
    return pltpu.make_async_copy(weight.at[:, chunk, kind], held.at[chunk], sem)


def row_copies(weight, kind, chunk, held, sem):
    span = held.shape[1]
    return pltpu.make_async_copy(weight.at[pl.ds(chunk * span, span), :, kind], held.at[chunk], sem)


def start_copies(choice, sources, order, sems):
    made = []
    for which, source in enumerate(sources):
        copies = [make(source[matrix][0], source[matrix][1], chunk, held, sems.at[i])
                  for i, (make, matrix, chunk, held) in enumerate(order)]
        made.append(copies)

        @pl.when(choice == which)
        def _():
            for copy in copies:
                copy.start()

    return made[0]


def square(held, chunk):
    width = held.shape[-1]
    return held[chunk].reshape(width, width)


def attention_pair_forward(p, start, size, qkv, keyb, att, aux):
    rows = pl.ds(start, size)
    width = att.shape[1]
    col = pl.multiple_of(p * 128, 128)
    lane = lanes(size)
    query = qkv[rows, pl.ds(col, 128)]
    key = qkv[rows, pl.ds(width + col, 128)]
    value = qkv[rows, pl.ds(2 * width + col, 128)]
    bias = keyb[rows]
    place = start + lax.broadcasted_iota(jnp.int32, (size, 128), 0)
    hot = jnp.where(lane % 64 == place // SEG, 1.0, 0.0).astype(BF16)
    query = query * jnp.asarray(HD ** -0.5, BF16)
    total = None
    for half in range(2):
        mine = (lane < 64) if half == 0 else (lane >= 64)
        scores = dot_nt(jnp.where(mine, query, hot), jnp.where(mine, key, bias))
        peak = jnp.max(scores, -1, keepdims=True)
        expo = jnp.exp(scores - peak)
        norm = jnp.sum(expo, -1, keepdims=True)
        part = dot(expo.astype(BF16), jnp.where(mine, value, jnp.zeros_like(value))) * (1.0 / norm)
        log_total = peak + jnp.log(norm)
        aux[rows] = jnp.where(lane == 80 + 2 * p + half, log_total, aux[rows])
        total = part if total is None else total + part
    att[rows, pl.ds(col, 128)] = total.astype(BF16)


def forward_kernel(
    sources, idx, hidden_ref, keyb_ref, adapter_ref, vec_ref, in_bias_ref,
    h1_ref, h2_ref, qkv_ref, att_ref, br1_ref, nh1_ref, aux1_ref, slope_ref, br2_ref, nh2_ref, aux2_ref, sums_ref,
    attn_v, in_v, out_v, acc, sems,
):
    bucket = idx[1]
    length, width = hidden_ref.shape
    chunks = in_v.shape[0]
    cols = [pl.ds(c * width, width) for c in range(chunks)]
    order = [(column_copies, 0, c, attn_v) for c in range(4)]
    for c in range(chunks):
        order.append((column_copies, 1, c, in_v))
        order.append((row_copies, 2, c, out_v))
    copies = start_copies(idx[2], sources, order, sems)
    hidden = hidden_ref[...]
    valid = keyb_ref[:, 16:17].astype(F32)
    for part in range(3):
        copies[part].wait()
        mixed = dot(hidden, square(attn_v, part))
        if part == 0:
            mixed = mixed + vec_ref[0, 5:6]
        if part == 2:
            mixed = mixed + vec_ref[0, 6:7]
        qkv_ref[:, cols[part]] = mixed.astype(BF16)
    aux1_ref[...] = jnp.zeros_like(aux1_ref)

    def heads(size):
        blocks = length // size

        def body(step, carry):
            p = step // blocks
            start = pl.multiple_of((step % blocks) * size, size)
            attention_pair_forward(p, start, size, qkv_ref, keyb_ref, att_ref, aux1_ref)
            return carry

        lax.fori_loop(0, (HEADS // 2) * blocks, body, 0)

    @pl.when(bucket >= 3)
    def _():
        heads(length)

    @pl.when(bucket < 3)
    def _():
        heads(length // 2)

    copies[3].wait()
    branch = dot(att_ref[...], square(attn_v, 3)) + vec_ref[0, 0:1]
    branch_low, down, output, normed, inverse, sums = adapter_forward(
        hidden, branch, adapter_ref, vec_ref, 0, 0, None, valid
    )
    br1_ref[...] = branch_low
    nh1_ref[...] = normed
    h1_ref[...] = output
    lane = lanes(length)
    aux1_ref[:, :64] = down
    aux1_ref[...] = jnp.where(lane == 64, inverse, aux1_ref[...])
    sums_ref[0:1] = sums[0]
    sums_ref[1:2] = sums[1]
    hidden = h1_ref[...]
    for c in range(chunks):
        copies[4 + 2 * c].wait()
        pre = dot(hidden, square(in_v, c)) + in_bias_ref[0, :, c * width : (c + 1) * width]
        act, slope = gelu_both(pre)
        slope_ref[:, cols[c]] = slope.astype(BF16)
        copies[5 + 2 * c].wait()
        term = dot(act.astype(BF16), square(out_v, c))
        if c == 0:
            acc[...] = term + vec_ref[0, 8:9]
        else:
            acc[...] += term
    branch_low, down, output, normed, inverse, sums = adapter_forward(
        hidden, acc[...], adapter_ref, vec_ref, 8, 1, None, valid
    )
    br2_ref[...] = branch_low
    nh2_ref[...] = normed
    h2_ref[...] = output
    aux2_ref[...] = jnp.where(lane == 64, inverse, jnp.zeros((length, 128), F32))
    aux2_ref[:, :64] = down
    sums_ref[2:3] = sums[0]
    sums_ref[3:4] = sums[1]
    sums_ref[4:8] = jnp.zeros_like(sums_ref[4:8])


def weight_plan(weights):
    arrays, places = [], []
    for layer in weights:
        spots = []
        for array, kind in layer:
            found = [i for i, other in enumerate(arrays) if other is array]
            if not found:
                arrays.append(array)
                found = [len(arrays) - 1]
            spots.append((found[0], kind))
        places.append(spots)
    return arrays, places


def weight_scratch(weights):
    attn, inner, outer = [array.shape for array, _ in weights[0]]
    width = attn[-1]
    span = width // (4 * outer[3])
    return [
        pltpu.VMEM((4, attn[0], attn[3], width), BF16),
        pltpu.VMEM((4, inner[0], inner[3], width), BF16),
        pltpu.VMEM((outer[0] // span, span, 4, outer[3], width), BF16),
    ]


def whole(shape):
    return pl.BlockSpec(shape, lambda i, s: (0,) * len(shape))


def by_layer(shape):
    return pl.BlockSpec((1,) + shape, lambda i, s: (s[0],) + (0,) * len(shape))


def call_with_weights(kernel, weights, blocks, outs, scratch, flops, name):
    arrays, places = weight_plan(weights)
    fixed = len(blocks)
    idx, rest = blocks[0], blocks[1:]

    def body(*refs):
        held = refs[fixed : fixed + len(arrays)]
        sources = [[(held[i], kind) for i, kind in spots] for spots in places]
        kernel(sources, *refs[:fixed], *refs[fixed + len(arrays) :])

    copies = 12
    return pl.pallas_call(
        body,
        grid_spec=pltpu.PrefetchScalarGridSpec(
            num_scalar_prefetch=1,
            grid=(1,),
            in_specs=[spec for _, spec in rest] + [pl.BlockSpec(memory_space=pl.ANY)] * len(arrays),
            out_specs=[whole(shape) for shape, _ in outs],
            scratch_shapes=weight_scratch(weights) + scratch + [pltpu.SemaphoreType.DMA((copies,))],
        ),
        out_shape=[jax.ShapeDtypeStruct(shape, dtype) for shape, dtype in outs],
        compiler_params=pltpu.CompilerParams(vmem_limit_bytes=VMEM_BYTES),
        cost_estimate=pl.CostEstimate(flops=flops, bytes_accessed=24_000_000, transcendentals=0),
        name=name,
    )(idx, *[array for array, _ in rest], *arrays)


def forward_pair(layer, choice, bucket, hidden, keyb, weights, adapters, vecs, in_bias):
    length, width = hidden.shape
    ffn = in_bias.shape[-1]
    idx = jnp.stack([layer, bucket, choice]).astype(jnp.int32)
    outs = [
        ((length, width), BF16), ((length, width), BF16), ((length, 3 * width), BF16), ((length, width), BF16),
        ((length, width), BF16), ((length, width), BF16), ((length, 128), F32), ((length, ffn), BF16),
        ((length, width), BF16), ((length, width), BF16), ((length, 128), F32), ((8, width), F32),
    ]
    blocks = [
        idx, (hidden, whole((length, width))), (keyb, whole((length, 128))), (adapters, by_layer((2, 128, width))),
        (vecs, by_layer((16, width))), (in_bias, by_layer((1, ffn))),
    ]
    scratch = [pltpu.VMEM((length, width), F32)]
    return call_with_weights(forward_kernel, weights, blocks, outs, scratch, 12_000_000_000, "forward_pair")


def adapter_backward(grad, normed, branch_low, aux, adapter_ref, vec_ref, base, stage, grads_ref):
    down_t = adapter_ref[0, stage, :64]
    lift = adapter_ref[0, stage, 64:]
    grad = grad.astype(F32)
    normed = normed.astype(F32)
    inverse = aux[:, 64:65]
    down = aux[:, :64]
    scaled = grad * vec_ref[0, base + 2 : base + 3]
    resid = inverse * (
        scaled
        - jnp.mean(scaled, -1, keepdims=True)
        - normed * jnp.mean(scaled * normed, -1, keepdims=True)
    )
    lift_grad = resid.astype(BF16)
    act, slope = gelu_both(down)
    down_grad = (dot_nt(lift_grad, lift) * slope).astype(BF16)
    grads_ref[stage, 0:64] = dot_tn(act.astype(BF16), lift_grad)
    grads_ref[stage, 64:128] = dot_tn(down_grad, branch_low)
    grads_ref[stage, 128:136] = jnp.zeros_like(grads_ref[stage, 128:136])
    grads_ref[stage, 128:129] = jnp.sum(lift_grad.astype(F32), 0, keepdims=True)
    grads_ref[stage, 129:130] = jnp.sum(normed * grad, 0, keepdims=True)
    grads_ref[stage, 130:131] = jnp.sum(grad, 0, keepdims=True)
    grads_ref[stage, 131:132, :64] = jnp.sum(down_grad.astype(F32), 0, keepdims=True)
    branch_grad = (resid + dot(down_grad, down_t)).astype(BF16)
    return resid, branch_grad


def split_low(column):
    high = column.astype(BF16).astype(F32)
    rest = column - high
    middle = rest.astype(BF16).astype(F32)
    return high, middle, rest - middle


def attention_pair_backward(p, start, size, qkv, keyb, att, aux, att_grad, dqkv):
    rows = pl.ds(start, size)
    width = att.shape[1]
    col = pl.multiple_of(p * 128, 128)
    lane = lanes(size)
    query = qkv[rows, pl.ds(col, 128)] * jnp.asarray(HD ** -0.5, BF16)
    key = qkv[rows, pl.ds(width + col, 128)]
    value = qkv[rows, pl.ds(2 * width + col, 128)]
    grad = att_grad[rows, pl.ds(col, 128)]
    product = grad.astype(F32) * att[rows, pl.ds(col, 128)].astype(F32)
    bias = keyb[rows]
    place = start + lax.broadcasted_iota(jnp.int32, (size, 128), 0)
    spot = lane % 64
    hot = jnp.where(spot == place // SEG, 1.0, 0.0)
    aux_rows = aux[rows]
    zero = jnp.zeros((size, 128), BF16)
    sums = [None, None, None]
    for half in range(2):
        mine = (lane < 64) if half == 0 else (lane >= 64)
        log_total = jnp.sum(jnp.where(lane == 80 + 2 * p + half, aux_rows, 0.0), -1, keepdims=True)
        parts = split_low(-log_total)
        extra = jnp.where(spot == LOG_TOP, parts[0], jnp.where(spot == LOG_TOP + 1, parts[1], jnp.where(spot == LOG_TOP + 2, parts[2], hot)))
        row_dot = jnp.sum(jnp.where(mine, product, 0.0), -1, keepdims=True)
        dots = split_low(-row_dot)
        extra_grad = jnp.where(spot == LOG_TOP, dots[0], jnp.where(spot == LOG_TOP + 1, dots[1], jnp.where(spot == LOG_TOP + 2, dots[2], 0.0)))
        key_side = jnp.where(mine, key, bias)
        value_side = jnp.where(mine, value, bias)
        probs = jnp.exp(dot_nt(key_side, jnp.where(mine, query, extra.astype(BF16))))
        centred = dot_nt(value_side, jnp.where(mine, grad, extra_grad.astype(BF16)))
        score_grad = (probs * centred).astype(BF16)
        terms = (
            dot_tn(score_grad, jnp.where(mine, key, zero)),
            dot(score_grad, jnp.where(mine, query, zero)),
            dot(probs.astype(BF16), jnp.where(mine, grad, zero)),
        )
        sums = [t if s is None else s + t for s, t in zip(sums, terms)]
    dqkv[rows, pl.ds(col, 128)] = (sums[0] * HD ** -0.5).astype(BF16)
    dqkv[rows, pl.ds(width + col, 128)] = sums[1].astype(BF16)
    dqkv[rows, pl.ds(2 * width + col, 128)] = sums[2].astype(BF16)


def backward_kernel(
    sources, idx, grad_ref, keyb_ref, qkv_ref, att_ref, br1_ref, nh1_ref, aux1_ref, slope_ref, br2_ref, nh2_ref,
    aux2_ref, adapter_ref, vec_ref,
    g2_ref, g1_ref, grads_ref,
    attn_v, in_v, out_v, acc, low, dqkv, sems,
):
    bucket = idx[1]
    length, width = grad_ref.shape
    chunks = in_v.shape[0]
    cols = [pl.ds(c * width, width) for c in range(chunks)]
    order = []
    for c in range(chunks):
        order.append((row_copies, 2, c, out_v))
        order.append((column_copies, 1, c, in_v))
    order += [(column_copies, 0, c, attn_v) for c in (3, 0, 1, 2)]
    copies = start_copies(idx[2], sources, order, sems)
    resid, branch_grad = adapter_backward(
        grad_ref[...], nh2_ref[...], br2_ref[...], aux2_ref[...], adapter_ref, vec_ref, 8, 1, grads_ref
    )
    acc[...] = resid
    low[...] = branch_grad
    for c in range(chunks):
        copies[2 * c].wait()
        act_grad = dot_nt(low[...], square(out_v, c))
        pre_grad = (act_grad * slope_ref[:, cols[c]].astype(F32)).astype(BF16)
        copies[2 * c + 1].wait()
        acc[...] += dot_nt(pre_grad, square(in_v, c))
    g2_ref[...] = acc[...].astype(BF16)
    resid, branch_grad = adapter_backward(
        g2_ref[...], nh1_ref[...], br1_ref[...], aux1_ref[...], adapter_ref, vec_ref, 0, 0, grads_ref
    )
    acc[...] = resid
    copies[2 * chunks].wait()
    low[...] = dot_nt(branch_grad, square(attn_v, 3)).astype(BF16)

    def heads(size):
        blocks = length // size

        def body(step, carry):
            p = step // blocks
            start = pl.multiple_of((step % blocks) * size, size)
            attention_pair_backward(p, start, size, qkv_ref, keyb_ref, att_ref, aux1_ref, low, dqkv)
            return carry

        lax.fori_loop(0, (HEADS // 2) * blocks, body, 0)

    @pl.when(bucket >= 3)
    def _():
        heads(length)

    @pl.when(bucket < 3)
    def _():
        heads(length // 2)

    for part in range(3):
        copies[2 * chunks + 1 + part].wait()
        acc[...] += dot_nt(dqkv[:, cols[part]], square(attn_v, part))
    g1_ref[...] = acc[...].astype(BF16)


def backward_pair(layer, choice, bucket, grad, keyb, saved, weights, adapters, vecs):
    length, width = grad.shape
    idx = jnp.stack([layer, bucket, choice]).astype(jnp.int32)
    outs = [((length, width), BF16), ((length, width), BF16), ((2, 136, width), F32)]
    blocks = [idx, (grad, whole((length, width))), (keyb, whole((length, 128)))]
    blocks += [(member, whole(member.shape)) for member in saved]
    blocks += [(adapters, by_layer((2, 128, width))), (vecs, by_layer((16, width)))]
    scratch = [
        pltpu.VMEM((length, width), F32),
        pltpu.VMEM((length, width), BF16),
        pltpu.VMEM((length, 3 * width), BF16),
    ]
    return call_with_weights(backward_kernel, weights, blocks, outs, scratch, 16_000_000_000, "backward_pair")


def key_table(bucket, padding):
    rows, length = padding.shape
    spot = jnp.arange(128, dtype=jnp.int32) % 64
    shift = 6 + bucket[:, None, None]
    place = jnp.arange(length, dtype=jnp.int32)
    same = (spot[None, None, :] * SEG) >> shift == place[None, :, None] >> shift
    real = (padding == 1)[:, :, None]
    table = jnp.where(same & real, 0.0, MASKED)
    ones = (spot >= LOG_TOP) & (spot < LOG_TOP + 3)
    table = jnp.where(spot < 8, table, jnp.where(spot == 16, real.astype(F32), jnp.where(ones, 1.0, 0.0)))
    return table.astype(BF16)


MESH = pl.DeviceIdType.MESH


def place_of(index):
    return index // 2, index % 2


class Gather:
    def __init__(self, full, sems):
        self.full = full
        self.sems = sems
        self.section = lax.axis_index("section")
        self.dp = lax.axis_index("dp")
        self.count = lax.axis_size("dp") // 2
        self.z, self.core = place_of(self.dp)
        self.x_side = self.section + 1 - 2 * (self.section % 2)
        self.y_side = lax.rem(self.section + 2, 4)
        self.corner = 3 - self.section
        self.sibling = self.dp + 1 - 2 * self.core

    def along(self, step):
        return lax.rem(self.z + step, self.count) * 2 + self.core

    def source(self, step):
        return lax.rem(self.z + self.count - step, self.count) * 2 + self.core

    def peers(self):
        steps = [(self.section, self.along(d)) for d in range(1, self.count)]
        near = [(other, self.dp) for other in (self.x_side, self.y_side, self.corner)]
        return steps + near + [(self.section, self.sibling)]

    def barrier(self):
        entry = pltpu.get_barrier_semaphore()
        peers = self.peers()
        for peer in peers:
            pl.semaphore_signal(entry, inc=1, device_id=peer, device_id_type=MESH)
        pl.semaphore_wait(entry, len(peers))

    def block(self, layer, group, shard, quarter, rows=None):
        kinds = pl.ds(0, 1) if group == 0 else pl.ds(1, 2)
        ref = self.full[layer].at[shard, quarter, kinds]
        return ref if rows is None else ref.at[:, rows]

    def copy(self, ref, name, spot, device):
        return pltpu.make_async_remote_copy(
            src_ref=ref, dst_ref=ref, send_sem=self.sems[name].at[(0,) + spot], recv_sem=self.sems[name].at[(1,) + spot],
            device_id=device, device_id_type=MESH,
        )

    def z_copy(self, layer, group, step):
        ref = self.block(layer, group, self.dp, self.section)
        return self.copy(ref, "z", (layer, group, step - 1), (self.section, self.along(step)))

    def side_copy(self, layer, group, step, way):
        ref = self.block(layer, group, self.source(step), self.section)
        device = (self.x_side if way == 0 else self.y_side, self.dp)
        return self.copy(ref, "side", (layer, group, step - 1, way), device)

    def corner_copy(self, layer, group, step, way):
        half = self.full[layer].shape[3] // 2
        quarter, target = (self.x_side, self.y_side) if way == 0 else (self.y_side, self.x_side)
        ref = self.block(layer, group, self.source(step), quarter, pl.ds(way * half, half))
        return self.copy(ref, "corner", (layer, group, step - 1, way), (target, self.dp))

    def core_copy(self, layer, group, step, which):
        quarter = (self.section, self.x_side, self.y_side, self.corner)[which]
        ref = self.block(layer, group, self.source(step), quarter)
        return self.copy(ref, "core", (layer, group, step, which), (self.section, self.sibling))

    def steps(self):
        return range(1, self.count)

    def start(self, layer, group):
        for step in self.steps():
            self.z_copy(layer, group, step).start()
        for which in range(4):
            self.core_copy(layer, group, 0, which).start()

    def spread(self, layer, group):
        for step in self.steps():
            self.z_copy(layer, group, step).wait_recv()
            for way in range(2):
                self.side_copy(layer, group, step, way).start()
            self.core_copy(layer, group, step, 0).start()

    def relay(self, layer, group):
        for step in self.steps():
            for way in range(2):
                self.side_copy(layer, group, step, way).wait_recv()
                self.corner_copy(layer, group, step, way).start()
                self.core_copy(layer, group, step, 1 + way).start()

    def close(self, layer, group):
        for step in self.steps():
            for way in range(2):
                self.corner_copy(layer, group, step, way).wait_recv()
            self.core_copy(layer, group, step, 3).start()

    def arrive(self, layer, group):
        for step in range(self.count):
            for which in range(4):
                self.core_copy(layer, group, step, which).wait_recv()

    def drain(self, layer, group):
        for step in self.steps():
            self.z_copy(layer, group, step).wait_send()
            for way in range(2):
                self.side_copy(layer, group, step, way).wait_send()
                self.corner_copy(layer, group, step, way).wait_send()
        for step in range(self.count):
            for which in range(4):
                self.core_copy(layer, group, step, which).wait_send()

    @staticmethod
    def semaphores(count):
        return {
            "z": pltpu.SemaphoreType.DMA((2, 2, 2, count - 1)),
            "side": pltpu.SemaphoreType.DMA((2, 2, 2, count - 1, 2)),
            "corner": pltpu.SemaphoreType.DMA((2, 2, 2, count - 1, 2)),
            "core": pltpu.SemaphoreType.DMA((2, 2, 2, count, 4)),
        }


def own_blocks(full, layer, shard, qkv_w, attn_w, in_w, out_w, sems):
    width = full.shape[-1]
    rows = full.shape[3]
    made = []
    for quarter in range(4):
        cols = pl.ds(quarter * width, width)
        first = qkv_w.at[layer, :, cols] if quarter < 3 else attn_w.at[layer]
        made.append(pltpu.make_async_copy(first, full.at[shard, quarter, 0], sems.at[layer, 3 * quarter]))
        made.append(pltpu.make_async_copy(in_w.at[layer, :, cols], full.at[shard, quarter, 1], sems.at[layer, 3 * quarter + 1]))
        made.append(
            pltpu.make_async_copy(
                out_w.at[layer, pl.ds(quarter * rows, rows)], full.at[shard, quarter, 2], sems.at[layer, 3 * quarter + 2]
            )
        )
    return made


def small_copies(gather, ref, sems, base):
    made = []
    for i, target in enumerate((gather.x_side, gather.y_side, gather.corner)):
        made.append(
            pltpu.make_async_remote_copy(
                src_ref=ref.at[gather.section], dst_ref=ref.at[gather.section], send_sem=sems.at[0, base + i],
                recv_sem=sems.at[1, base + i], device_id=(target, gather.dp), device_id_type=MESH,
            )
        )
    return made


def gather_kernel(
    qkv_w, attn_w, in_w, out_w, own_adapter, own_vec, full0, full1, adapters, vecs,
    z_sem, side_sem, corner_sem, core_sem, small_sem, local_sem,
):
    gather = Gather([full0, full1], {"z": z_sem, "side": side_sem, "corner": corner_sem, "core": core_sem})
    local = [own_blocks(full, layer, gather.dp, qkv_w, attn_w, in_w, out_w, local_sem) for layer, full in enumerate((full0, full1))]
    tiny = [
        pltpu.make_async_copy(own_adapter, adapters.at[gather.section], local_sem.at[2, 0]),
        pltpu.make_async_copy(own_vec, vecs.at[gather.section], local_sem.at[2, 1]),
    ]
    for copy in local[0] + tiny + local[1]:
        copy.start()
    gather.barrier()
    for copy in local[0] + tiny:
        copy.wait()
    gather.start(0, 0)
    small = small_copies(gather, adapters, small_sem, 0) + small_copies(gather, vecs, small_sem, 3)
    for copy in small:
        copy.start()
    gather.start(0, 1)
    gather.spread(0, 0)
    for copy in local[1]:
        copy.wait()
    gather.relay(0, 0)
    gather.spread(0, 1)
    gather.close(0, 0)
    gather.start(1, 0)
    gather.relay(0, 1)
    gather.spread(1, 0)
    gather.start(1, 1)
    gather.close(0, 1)
    gather.relay(1, 0)
    gather.spread(1, 1)
    gather.close(1, 0)
    gather.relay(1, 1)
    gather.close(1, 1)
    for copy in small:
        copy.wait()
    for layer in range(2):
        for group in range(2):
            gather.arrive(layer, group)
            gather.drain(layer, group)


def gather_everything(qkv_w, attn_w, in_w, out_w, own_adapter, own_vec):
    width = qkv_w.shape[2] // 3
    rows = qkv_w.shape[1]
    shards = lax.axis_size("dp")
    sections = lax.axis_size("section")
    anyspec = pl.BlockSpec(memory_space=pl.ANY)
    sems = Gather.semaphores(shards // 2)
    full = jax.ShapeDtypeStruct((shards, 4, 3, rows, width), BF16)
    return pl.pallas_call(
        gather_kernel,
        in_specs=[anyspec] * 6,
        out_specs=[anyspec] * 4,
        out_shape=[
            full, full, jax.ShapeDtypeStruct((sections,) + own_adapter.shape, BF16),
            jax.ShapeDtypeStruct((sections,) + own_vec.shape, F32),
        ],
        scratch_shapes=[
            sems["z"], sems["side"], sems["corner"], sems["core"], pltpu.SemaphoreType.DMA((2, 6)), pltpu.SemaphoreType.DMA((3, 12)),
        ],
        compiler_params=pltpu.CompilerParams(collective_id=1, has_side_effects=True),
        cost_estimate=pl.CostEstimate(flops=0, bytes_accessed=60_000_000, transcendentals=0),
        name="gather_weights",
    )(qkv_w, attn_w, in_w, out_w, own_adapter, own_vec)


X_PAIRS = [(0, 1), (1, 0), (2, 3), (3, 2)]
Y_PAIRS = [(0, 2), (2, 0), (1, 3), (3, 1)]
CROSS = [(0, 3), (3, 0), (1, 2), (2, 1)]


def send(value, pairs, senders=(0, 1, 2, 3)):
    return lax.ppermute(value, "section", [pair for pair in pairs if pair[0] in senders])


def gather_weights(shards):
    section = lax.axis_index("section")
    quarter = lax.dynamic_index_in_dim(shards, section, 0, keepdims=False)
    full = lax.all_gather(quarter, ("dp", "section"), axis=0, tiled=False)
    count = lax.axis_size("dp")
    full = full.reshape((count, lax.axis_size("section")) + quarter.shape)
    return full


def in_quarters(matrix):
    rows, columns = matrix.shape
    return matrix.reshape(rows, 4, columns // 4).transpose(1, 0, 2)


def block_rows(full, kind, by_rows):
    if full.shape[3] % 16 == 0:
        return (full, kind)
    count, quarters, _, rows, width = full.shape
    one = full[:, :, kind]
    if by_rows:
        return (one.reshape(count * rows * quarters // width, quarters, 1, width // quarters, width), 0)
    return (one.transpose(1, 0, 2, 3).reshape(1, quarters, 1, count * rows, width), 0)


def on_device(
    inputs, bucket, padding, cotangent, down_weight, down_bias, up_weight, up_bias, ln_gain, ln_beta, qkv_weight,
    query_bias, value_bias, attn_out_weight, attn_out_bias, ffn_in_weight, ffn_in_bias, ffn_out_weight, ffn_out_bias,
):
    section = lax.axis_index("section")
    early = section < 2
    side = section % 2
    width = inputs.shape[2]
    adapter_width = down_weight.shape[2]
    layers = qkv_weight.shape[0]

    def layer_shards(layer):
        attn = jnp.concatenate([qkv_weight[layer], attn_out_weight[layer]], 1)
        outer = ffn_out_weight[layer]
        return (
            in_quarters(attn)[:, None],
            jnp.stack([in_quarters(ffn_in_weight[layer]), outer.reshape((4, -1) + outer.shape[1:])], 1),
        )

    zero_row = jnp.zeros((1, width), F32)
    own_vec = jnp.concatenate(
        [zero_row, up_bias, ln_gain, ln_beta, jnp.pad(down_bias, ((0, 0), (0, width - adapter_width))), zero_row, zero_row, zero_row], 0
    )
    own_adapter = jnp.concatenate([down_weight[0].T, up_weight[0]], 0)
    if lax.axis_size("dp") == 8 and lax.axis_size("section") == 4:
        full0, full1, adapters, vecs = gather_everything(
            qkv_weight, attn_out_weight, ffn_in_weight, ffn_out_weight, own_adapter, own_vec
        )
        weights = [[(full, kind) for kind in range(3)] for full in (full0, full1)]
    else:
        weights = []
        for layer in range(layers):
            full = gather_weights(jnp.concatenate(layer_shards(layer), 1))
            weights.append([block_rows(full, 0, False), block_rows(full, 1, False), block_rows(full, 2, True)])
        adapters = lax.all_gather(own_adapter, "section", axis=0, tiled=False)
        vecs = lax.all_gather(own_vec, "section", axis=0, tiled=False)
    adapters = adapters.reshape(layers, 2, 128, width)
    vecs = vecs.reshape(layers, 2, 8, width)
    vecs = vecs.at[:, 0, 0].set(attn_out_bias).at[:, 0, 5].set(query_bias).at[:, 0, 6].set(value_bias)
    vecs = vecs.at[:, 1, 0].set(ffn_out_bias).reshape(layers, 16, width)
    in_bias = ffn_in_bias[:, None, :]

    table = key_table(bucket, padding)
    own = section
    shared = 4 + side

    def row_of(array, row):
        return lax.dynamic_index_in_dim(array, row, 0, keepdims=False)

    def forward(row, hidden, layer, weights_used, choice):
        return forward_pair(
            layer, choice, row_of(bucket, row), hidden, row_of(table, row), weights_used, adapters, vecs, in_bias
        )

    def backward(row, grad, saved, layer, weights_used, choice):
        return backward_pair(
            layer, choice, row_of(bucket, row), grad, row_of(table, row), saved, weights_used, adapters, vecs
        )

    zero = jnp.int32(0)
    one = jnp.int32(1)
    late = 1 - early.astype(jnp.int32)
    first_row = jnp.where(early, shared, own)
    third_row = jnp.where(early, own, shared)

    f0 = forward(first_row, row_of(inputs, first_row), zero, weights[:1], zero)
    x0 = send(jnp.where(side == 0, f0[1], f0[0]), X_PAIRS, (0, 1))
    y0 = send(jnp.where(early | (side == 1), f0[1], f0[0]), Y_PAIRS)
    z0 = send(jnp.where(side == 0, f0[1], f0[0]), CROSS, (2, 3))
    hidden = jnp.where(early, row_of(inputs, own), f0[1])
    f1 = forward(own, hidden, late, weights, late)
    x1 = send(jnp.where(side == 0, f1[1], f1[0]), X_PAIRS)
    hidden = jnp.where(early, f1[1], y0)
    f2 = forward(third_row, hidden, one, weights[1:], zero)
    x2 = send(jnp.where(side == 0, f2[1], f2[0]), X_PAIRS, (2, 3))
    y2 = send(jnp.where(side == 1, f2[1], f2[0]), Y_PAIRS, (0, 1))
    z2 = send(jnp.where(side == 0, f2[1], f2[0]), CROSS, (0, 1))

    b3 = backward(third_row, row_of(cotangent, third_row), f2[2:11], one, weights[1:], zero)
    x3 = send(jnp.where(side == 0, b3[0], b3[1]), X_PAIRS, (2, 3))
    y3 = send(jnp.where(early & (side == 1), b3[0], b3[1]), Y_PAIRS)
    z3 = send(jnp.where(side == 0, b3[0], b3[1]), CROSS, (0, 1))
    grad = jnp.where(early, b3[1], row_of(cotangent, own))
    b4 = backward(own, grad, f1[2:11], late, weights, late)
    x4 = send(jnp.where(side == 0, b4[0], b4[1]), X_PAIRS)
    grad = jnp.where(early, y3, b4[1])
    b5 = backward(first_row, grad, f0[2:11], zero, weights[:1], zero)
    x5 = send(jnp.where(side == 0, b5[0], b5[1]), X_PAIRS, (0, 1))
    y5 = send(jnp.where(side == 1, b5[0], b5[1]), Y_PAIRS, (2, 3))
    z5 = send(jnp.where(side == 0, b5[0], b5[1]), CROSS, (2, 3))

    def assemble(parts):
        result = jnp.zeros(inputs.shape, BF16)
        for row, part in parts:
            result = lax.dynamic_update_index_in_dim(result, part, row, 0)
        return result

    other = section + 1 - 2 * side
    across = jnp.where(early, section + 2, section - 2)
    corner = 3 - section
    other_shared = 4 + 1 - side
    outputs = assemble(
        [
            (own, jnp.where(side == 0, f1[0], f1[1])),
            (other, x1),
            (across, jnp.where(early, y0, y2)),
            (corner, jnp.where(early, z0, z2)),
            (shared, jnp.where(early, jnp.where(side == 0, f0[0], f0[1]), jnp.where(side == 0, f2[0], f2[1]))),
            (other_shared, jnp.where(early, x0, x2)),
        ]
    )
    input_grads = assemble(
        [
            (own, jnp.where(side == 0, b4[1], b4[0])),
            (other, x4),
            (across, jnp.where(early, y5, y3)),
            (corner, jnp.where(early, z5, z3)),
            (shared, jnp.where(early, jnp.where(side == 0, b5[1], b5[0]), jnp.where(side == 0, b3[1], b3[0]))),
            (other_shared, jnp.where(early, x5, x3)),
        ]
    )

    def with_sums(grads, sums):
        squares = jnp.sum(sums[:4].reshape(2, 2, width), -1, keepdims=True)
        return grads.at[:, 132:134].set(jnp.broadcast_to(squares, (2, 2, width)))

    g3, g4, g5 = with_sums(b3[2], f2[11]), with_sums(b4[2], f1[11]), with_sums(b5[2], f0[11])
    low_layer = g5 + jnp.where(early, g4, 0.0)
    high_layer = g3 + jnp.where(early, 0.0, g4)
    mine = lax.psum_scatter(jnp.concatenate([low_layer, high_layer], 0), "section", scatter_dimension=0, tiled=False)
    total = lax.psum(mine, "dp")
    ratios = jnp.sqrt(total[132, 0] / total[133, 0])[None]
    return (
        outputs[None],
        input_grads[None],
        total[64:128].T[None],
        total[131, :adapter_width][None],
        total[0:64][None],
        total[128][None],
        total[129][None],
        total[130][None],
        ratios,
    )


def solution(mesh):
    in_specs = (
        P("dp", None, None),
        P("dp"),
        P("dp", None),
        P("dp", None, None),
        P("section", None, None),
        P("section", None),
        P("section", None, None),
        P("section", None),
        P("section", None),
        P("section", None),
        P(None, "dp", None),
        P(),
        P(),
        P(None, "dp", None),
        P(),
        P(None, "dp", None),
        P(),
        P(None, "dp", None),
        P(),
    )
    out_specs = (
        P("section", "dp", None, None),
        P("section", "dp", None, None),
        P("section", None, None),
        P("section", None),
        P("section", None, None),
        P("section", None),
        P("section", None),
        P("section", None),
        P("section"),
    )
    return jax.shard_map(
        on_device, mesh=mesh, in_specs=in_specs, out_specs=out_specs, check_vma=False
    )
```

```python
import functools
import jax
import jax.numpy as jnp
from jax import lax
from jax.experimental import pallas as pl
from jax.experimental.pallas import tpu as pltpu
from jax.sharding import PartitionSpec as P

HEADS = 12
HD = 64
SEG = 64
EPSILON = 1e-05
MASKED = -1e30
LOG_TOP = 24
VMEM_BYTES = 56 * 1024 * 1024
F32 = jnp.float32
BF16 = jnp.bfloat16


def dot(left, right):
    return jnp.dot(left, right, preferred_element_type=F32)


def dot_nt(left, right):
    return lax.dot_general(left, right, (((1,), (1,)), ((), ())), preferred_element_type=F32)


def dot_tn(left, right):
    return lax.dot_general(left, right, (((0,), (0,)), ((), ())), preferred_element_type=F32)


def gelu_both(v):
    bell = jnp.exp(v * v * -0.5)
    t = 1.0 / (1.0 + jnp.abs(v) * (0.3275911 * 0.7071067811865476))
    tail = t * (
        0.127414796
        + t * (-0.142248368 + t * (0.7107068705 + t * (-0.7265760135 + t * 0.5307027145)))
    )
    tail = tail * bell
    cdf = jnp.where(v >= 0, 1.0 - tail, tail)
    return (v * cdf, cdf + v * bell * 0.3989422804014327)


def lanes(rows):
    return lax.broadcasted_iota(jnp.int32, (rows, 128), 1)


def adapter_forward(hidden, branch, adapter_ref, vec_ref, base, stage, aux, valid):
    down_t = adapter_ref[0, stage, :64]
    lift = adapter_ref[0, stage, 64:]
    branch_low = branch.astype(BF16)
    down = dot_nt(branch_low, down_t) + vec_ref[0, base + 4 : base + 5, :64]
    act, _ = gelu_both(down)
    lifted = dot(act.astype(BF16), lift) + vec_ref[0, base + 1 : base + 2]
    hidden_float = hidden.astype(F32)
    resid = hidden_float + branch + lifted
    mean = jnp.mean(resid, -1, keepdims=True)
    center = resid - mean
    inverse = lax.rsqrt(jnp.mean(center * center, -1, keepdims=True) + EPSILON)
    normed = center * inverse
    output = (normed * vec_ref[0, base + 2 : base + 3] + vec_ref[0, base + 3 : base + 4]).astype(BF16)
    sums = (
        jnp.sum(lifted * lifted * valid, 0, keepdims=True),
        jnp.sum(hidden_float * hidden_float * valid, 0, keepdims=True),
    )
    return branch_low, down, output, normed.astype(BF16), inverse, sums


def column_copies(weight, kind, chunk, held, sem):
    return pltpu.make_async_copy(weight.at[:, chunk, kind], held.at[chunk], sem)


def row_copies(weight, kind, chunk, held, sem):
    span = held.shape[1]
    return pltpu.make_async_copy(weight.at[pl.ds(chunk * span, span), :, kind], held.at[chunk], sem)


def start_copies(choice, sources, order, sems):
    made = []
    for which, source in enumerate(sources):
        copies = [make(source[matrix][0], source[matrix][1], chunk, held, sems.at[i])
                  for i, (make, matrix, chunk, held) in enumerate(order)]
        made.append(copies)

        @pl.when(choice == which)
        def _():
            for copy in copies:
                copy.start()

    return made[0]


def square(held, chunk):
    width = held.shape[-1]
    return held[chunk].reshape(width, width)


def attention_pair_forward(p, start, size, qkv, keyb, att, aux):
    rows = pl.ds(start, size)
    width = att.shape[1]
    col = pl.multiple_of(p * 128, 128)
    lane = lanes(size)
    query = qkv[rows, pl.ds(col, 128)]
    key = qkv[rows, pl.ds(width + col, 128)]
    value = qkv[rows, pl.ds(2 * width + col, 128)]
    bias = keyb[rows]
    place = start + lax.broadcasted_iota(jnp.int32, (size, 128), 0)
    hot = jnp.where(lane % 64 == place // SEG, 1.0, 0.0).astype(BF16)
    query = query * jnp.asarray(HD ** -0.5, BF16)
    total = None
    for half in range(2):
        mine = (lane < 64) if half == 0 else (lane >= 64)
        scores = dot_nt(jnp.where(mine, query, hot), jnp.where(mine, key, bias))
        peak = jnp.max(scores, -1, keepdims=True)
        expo = jnp.exp(scores - peak)
        norm = jnp.sum(expo, -1, keepdims=True)
        part = dot(expo.astype(BF16), jnp.where(mine, value, jnp.zeros_like(value))) * (1.0 / norm)
        log_total = peak + jnp.log(norm)
        aux[rows] = jnp.where(lane == 80 + 2 * p + half, log_total, aux[rows])
        total = part if total is None else total + part
    att[rows, pl.ds(col, 128)] = total.astype(BF16)


def forward_kernel(
    sources, idx, hidden_ref, keyb_ref, adapter_ref, vec_ref, in_bias_ref,
    h1_ref, h2_ref, qkv_ref, att_ref, br1_ref, nh1_ref, aux1_ref, slope_ref, br2_ref, nh2_ref, aux2_ref, sums_ref,
    attn_v, in_v, out_v, acc, sems,
):
    bucket = idx[1]
    length, width = hidden_ref.shape
    chunks = in_v.shape[0]
    cols = [pl.ds(c * width, width) for c in range(chunks)]
    order = [(column_copies, 0, c, attn_v) for c in range(4)]
    for c in range(chunks):
        order.append((column_copies, 1, c, in_v))
        order.append((row_copies, 2, c, out_v))
    copies = start_copies(idx[2], sources, order, sems)
    hidden = hidden_ref[...]
    valid = keyb_ref[:, 16:17].astype(F32)
    for part in range(3):
        copies[part].wait()
        mixed = dot(hidden, square(attn_v, part))
        if part == 0:
            mixed = mixed + vec_ref[0, 5:6]
        if part == 2:
            mixed = mixed + vec_ref[0, 6:7]
        qkv_ref[:, cols[part]] = mixed.astype(BF16)
    aux1_ref[...] = jnp.zeros_like(aux1_ref)

    def heads(size):
        blocks = length // size

        def body(step, carry):
            p = step // blocks
            start = pl.multiple_of((step % blocks) * size, size)
            attention_pair_forward(p, start, size, qkv_ref, keyb_ref, att_ref, aux1_ref)
            return carry

        lax.fori_loop(0, (HEADS // 2) * blocks, body, 0)

    @pl.when(bucket >= 3)
    def _():
        heads(length)

    @pl.when(bucket < 3)
    def _():
        heads(length // 2)

    copies[3].wait()
    branch = dot(att_ref[...], square(attn_v, 3)) + vec_ref[0, 0:1]
    branch_low, down, output, normed, inverse, sums = adapter_forward(
        hidden, branch, adapter_ref, vec_ref, 0, 0, None, valid
    )
    br1_ref[...] = branch_low
    nh1_ref[...] = normed
    h1_ref[...] = output
    lane = lanes(length)
    aux1_ref[:, :64] = down
    aux1_ref[...] = jnp.where(lane == 64, inverse, aux1_ref[...])
    sums_ref[0:1] = sums[0]
    sums_ref[1:2] = sums[1]
    hidden = h1_ref[...]
    for c in range(chunks):
        copies[4 + 2 * c].wait()
        pre = dot(hidden, square(in_v, c)) + in_bias_ref[0, :, c * width : (c + 1) * width]
        act, slope = gelu_both(pre)
        slope_ref[:, cols[c]] = slope.astype(BF16)
        copies[5 + 2 * c].wait()
        term = dot(act.astype(BF16), square(out_v, c))
        if c == 0:
            acc[...] = term + vec_ref[0, 8:9]
        else:
            acc[...] += term
    branch_low, down, output, normed, inverse, sums = adapter_forward(
        hidden, acc[...], adapter_ref, vec_ref, 8, 1, None, valid
    )
    br2_ref[...] = branch_low
    nh2_ref[...] = normed
    h2_ref[...] = output
    aux2_ref[...] = jnp.where(lane == 64, inverse, jnp.zeros((length, 128), F32))
    aux2_ref[:, :64] = down
    sums_ref[2:3] = sums[0]
    sums_ref[3:4] = sums[1]
    sums_ref[4:8] = jnp.zeros_like(sums_ref[4:8])


def weight_plan(weights):
    arrays, places = [], []
    for layer in weights:
        spots = []
        for array, kind in layer:
            found = [i for i, other in enumerate(arrays) if other is array]
            if not found:
                arrays.append(array)
                found = [len(arrays) - 1]
            spots.append((found[0], kind))
        places.append(spots)
    return arrays, places


def weight_scratch(weights):
    attn, inner, outer = [array.shape for array, _ in weights[0]]
    width = attn[-1]
    span = width // (4 * outer[3])
    return [
        pltpu.VMEM((4, attn[0], attn[3], width), BF16),
        pltpu.VMEM((4, inner[0], inner[3], width), BF16),
        pltpu.VMEM((outer[0] // span, span, 4, outer[3], width), BF16),
    ]


def whole(shape):
    return pl.BlockSpec(shape, lambda i, s: (0,) * len(shape))


def by_layer(shape):
    return pl.BlockSpec((1,) + shape, lambda i, s: (s[0],) + (0,) * len(shape))


def call_with_weights(kernel, weights, blocks, outs, scratch, flops, name):
    arrays, places = weight_plan(weights)
    fixed = len(blocks)
    idx, rest = blocks[0], blocks[1:]

    def body(*refs):
        held = refs[fixed : fixed + len(arrays)]
        sources = [[(held[i], kind) for i, kind in spots] for spots in places]
        kernel(sources, *refs[:fixed], *refs[fixed + len(arrays) :])

    copies = 12
    return pl.pallas_call(
        body,
        grid_spec=pltpu.PrefetchScalarGridSpec(
            num_scalar_prefetch=1,
            grid=(1,),
            in_specs=[spec for _, spec in rest] + [pl.BlockSpec(memory_space=pl.ANY)] * len(arrays),
            out_specs=[whole(shape) for shape, _ in outs],
            scratch_shapes=weight_scratch(weights) + scratch + [pltpu.SemaphoreType.DMA((copies,))],
        ),
        out_shape=[jax.ShapeDtypeStruct(shape, dtype) for shape, dtype in outs],
        compiler_params=pltpu.CompilerParams(vmem_limit_bytes=VMEM_BYTES),
        cost_estimate=pl.CostEstimate(flops=flops, bytes_accessed=24_000_000, transcendentals=0),
        name=name,
    )(idx, *[array for array, _ in rest], *arrays)


def forward_pair(layer, choice, bucket, hidden, keyb, weights, adapters, vecs, in_bias):
    length, width = hidden.shape
    ffn = in_bias.shape[-1]
    idx = jnp.stack([layer, bucket, choice]).astype(jnp.int32)
    outs = [
        ((length, width), BF16), ((length, width), BF16), ((length, 3 * width), BF16), ((length, width), BF16),
        ((length, width), BF16), ((length, width), BF16), ((length, 128), F32), ((length, ffn), BF16),
        ((length, width), BF16), ((length, width), BF16), ((length, 128), F32), ((8, width), F32),
    ]
    blocks = [
        idx, (hidden, whole((length, width))), (keyb, whole((length, 128))), (adapters, by_layer((2, 128, width))),
        (vecs, by_layer((16, width))), (in_bias, by_layer((1, ffn))),
    ]
    scratch = [pltpu.VMEM((length, width), F32)]
    return call_with_weights(forward_kernel, weights, blocks, outs, scratch, 12_000_000_000, "forward_pair")


def adapter_backward(grad, normed, branch_low, aux, adapter_ref, vec_ref, base, stage, grads_ref):
    down_t = adapter_ref[0, stage, :64]
    lift = adapter_ref[0, stage, 64:]
    grad = grad.astype(F32)
    normed = normed.astype(F32)
    inverse = aux[:, 64:65]
    down = aux[:, :64]
    scaled = grad * vec_ref[0, base + 2 : base + 3]
    resid = inverse * (
        scaled
        - jnp.mean(scaled, -1, keepdims=True)
        - normed * jnp.mean(scaled * normed, -1, keepdims=True)
    )
    lift_grad = resid.astype(BF16)
    act, slope = gelu_both(down)
    down_grad = (dot_nt(lift_grad, lift) * slope).astype(BF16)
    grads_ref[stage, 0:64] = dot_tn(act.astype(BF16), lift_grad)
    grads_ref[stage, 64:128] = dot_tn(down_grad, branch_low)
    grads_ref[stage, 128:136] = jnp.zeros_like(grads_ref[stage, 128:136])
    grads_ref[stage, 128:129] = jnp.sum(lift_grad.astype(F32), 0, keepdims=True)
    grads_ref[stage, 129:130] = jnp.sum(normed * grad, 0, keepdims=True)
    grads_ref[stage, 130:131] = jnp.sum(grad, 0, keepdims=True)
    grads_ref[stage, 131:132, :64] = jnp.sum(down_grad.astype(F32), 0, keepdims=True)
    branch_grad = (resid + dot(down_grad, down_t)).astype(BF16)
    return resid, branch_grad


def split_low(column):
    high = column.astype(BF16).astype(F32)
    rest = column - high
    middle = rest.astype(BF16).astype(F32)
    return high, middle, rest - middle


def attention_pair_backward(p, start, size, qkv, keyb, att, aux, att_grad, dqkv):
    rows = pl.ds(start, size)
    width = att.shape[1]
    col = pl.multiple_of(p * 128, 128)
    lane = lanes(size)
    query = qkv[rows, pl.ds(col, 128)] * jnp.asarray(HD ** -0.5, BF16)
    key = qkv[rows, pl.ds(width + col, 128)]
    value = qkv[rows, pl.ds(2 * width + col, 128)]
    grad = att_grad[rows, pl.ds(col, 128)]
    product = grad.astype(F32) * att[rows, pl.ds(col, 128)].astype(F32)
    bias = keyb[rows]
    place = start + lax.broadcasted_iota(jnp.int32, (size, 128), 0)
    spot = lane % 64
    hot = jnp.where(spot == place // SEG, 1.0, 0.0)
    aux_rows = aux[rows]
    zero = jnp.zeros((size, 128), BF16)
    sums = [None, None, None]
    for half in range(2):
        mine = (lane < 64) if half == 0 else (lane >= 64)
        log_total = jnp.sum(jnp.where(lane == 80 + 2 * p + half, aux_rows, 0.0), -1, keepdims=True)
        parts = split_low(-log_total)
        extra = jnp.where(spot == LOG_TOP, parts[0], jnp.where(spot == LOG_TOP + 1, parts[1], jnp.where(spot == LOG_TOP + 2, parts[2], hot)))
        row_dot = jnp.sum(jnp.where(mine, product, 0.0), -1, keepdims=True)
        dots = split_low(-row_dot)
        extra_grad = jnp.where(spot == LOG_TOP, dots[0], jnp.where(spot == LOG_TOP + 1, dots[1], jnp.where(spot == LOG_TOP + 2, dots[2], 0.0)))
        key_side = jnp.where(mine, key, bias)
        value_side = jnp.where(mine, value, bias)
        probs = jnp.exp(dot_nt(key_side, jnp.where(mine, query, extra.astype(BF16))))
        centred = dot_nt(value_side, jnp.where(mine, grad, extra_grad.astype(BF16)))
        score_grad = (probs * centred).astype(BF16)
        terms = (
            dot_tn(score_grad, jnp.where(mine, key, zero)),
            dot(score_grad, jnp.where(mine, query, zero)),
            dot(probs.astype(BF16), jnp.where(mine, grad, zero)),
        )
        sums = [t if s is None else s + t for s, t in zip(sums, terms)]
    dqkv[rows, pl.ds(col, 128)] = (sums[0] * HD ** -0.5).astype(BF16)
    dqkv[rows, pl.ds(width + col, 128)] = sums[1].astype(BF16)
    dqkv[rows, pl.ds(2 * width + col, 128)] = sums[2].astype(BF16)


def backward_kernel(
    sources, idx, grad_ref, keyb_ref, qkv_ref, att_ref, br1_ref, nh1_ref, aux1_ref, slope_ref, br2_ref, nh2_ref,
    aux2_ref, adapter_ref, vec_ref,
    g2_ref, g1_ref, grads_ref,
    attn_v, in_v, out_v, acc, low, dqkv, sems,
):
    bucket = idx[1]
    length, width = grad_ref.shape
    chunks = in_v.shape[0]
    cols = [pl.ds(c * width, width) for c in range(chunks)]
    order = []
    for c in range(chunks):
        order.append((row_copies, 2, c, out_v))
        order.append((column_copies, 1, c, in_v))
    order += [(column_copies, 0, c, attn_v) for c in (3, 0, 1, 2)]
    copies = start_copies(idx[2], sources, order, sems)
    resid, branch_grad = adapter_backward(
        grad_ref[...], nh2_ref[...], br2_ref[...], aux2_ref[...], adapter_ref, vec_ref, 8, 1, grads_ref
    )
    acc[...] = resid
    low[...] = branch_grad
    for c in range(chunks):
        copies[2 * c].wait()
        act_grad = dot_nt(low[...], square(out_v, c))
        pre_grad = (act_grad * slope_ref[:, cols[c]].astype(F32)).astype(BF16)
        copies[2 * c + 1].wait()
        acc[...] += dot_nt(pre_grad, square(in_v, c))
    g2_ref[...] = acc[...].astype(BF16)
    resid, branch_grad = adapter_backward(
        g2_ref[...], nh1_ref[...], br1_ref[...], aux1_ref[...], adapter_ref, vec_ref, 0, 0, grads_ref
    )
    acc[...] = resid
    copies[2 * chunks].wait()
    low[...] = dot_nt(branch_grad, square(attn_v, 3)).astype(BF16)

    def heads(size):
        blocks = length // size

        def body(step, carry):
            p = step // blocks
            start = pl.multiple_of((step % blocks) * size, size)
            attention_pair_backward(p, start, size, qkv_ref, keyb_ref, att_ref, aux1_ref, low, dqkv)
            return carry

        lax.fori_loop(0, (HEADS // 2) * blocks, body, 0)

    @pl.when(bucket >= 3)
    def _():
        heads(length)

    @pl.when(bucket < 3)
    def _():
        heads(length // 2)

    for part in range(3):
        copies[2 * chunks + 1 + part].wait()
        acc[...] += dot_nt(dqkv[:, cols[part]], square(attn_v, part))
    g1_ref[...] = acc[...].astype(BF16)


def backward_pair(layer, choice, bucket, grad, keyb, saved, weights, adapters, vecs):
    length, width = grad.shape
    idx = jnp.stack([layer, bucket, choice]).astype(jnp.int32)
    outs = [((length, width), BF16), ((length, width), BF16), ((2, 136, width), F32)]
    blocks = [idx, (grad, whole((length, width))), (keyb, whole((length, 128)))]
    blocks += [(member, whole(member.shape)) for member in saved]
    blocks += [(adapters, by_layer((2, 128, width))), (vecs, by_layer((16, width)))]
    scratch = [
        pltpu.VMEM((length, width), F32),
        pltpu.VMEM((length, width), BF16),
        pltpu.VMEM((length, 3 * width), BF16),
    ]
    return call_with_weights(backward_kernel, weights, blocks, outs, scratch, 16_000_000_000, "backward_pair")


def key_table(bucket, padding):
    rows, length = padding.shape
    spot = jnp.arange(128, dtype=jnp.int32) % 64
    shift = 6 + bucket[:, None, None]
    place = jnp.arange(length, dtype=jnp.int32)
    same = (spot[None, None, :] * SEG) >> shift == place[None, :, None] >> shift
    real = (padding == 1)[:, :, None]
    table = jnp.where(same & real, 0.0, MASKED)
    ones = (spot >= LOG_TOP) & (spot < LOG_TOP + 3)
    table = jnp.where(spot < 8, table, jnp.where(spot == 16, real.astype(F32), jnp.where(ones, 1.0, 0.0)))
    return table.astype(BF16)


MESH = pl.DeviceIdType.MESH
GRAD_ROWS = 144
MEGA_BYTES = 63 * 1024 * 1024


def when(condition, action):
    if condition is None:
        action()
    else:
        pl.when(condition)(action)


class Place:
    def __init__(self):
        self.section = lax.axis_index("section")
        self.dp = lax.axis_index("dp")
        self.count = lax.axis_size("dp") // 2
        self.z = self.dp // 2
        self.core = self.dp % 2
        self.side = self.section % 2
        self.early = self.section < 2
        self.late = self.section >= 2
        self.x_side = self.section + 1 - 2 * self.side
        self.y_side = lax.rem(self.section + 2, 4)
        self.corner = 3 - self.section
        self.to_x = (self.x_side, self.dp)
        self.to_y = (self.y_side, self.dp)
        self.to_corner = (self.corner, self.dp)
        self.to_core = (self.section, self.dp + 1 - 2 * self.core)

    def to_z(self, step):
        return (self.section, lax.rem(self.z + step, self.count) * 2 + self.core)

    def from_z(self, step):
        return lax.rem(self.z + self.count - step, self.count) * 2 + self.core

    def peers(self):
        return [self.to_z(d) for d in range(1, self.count)] + [self.to_x, self.to_y, self.to_corner, self.to_core]

    def barrier(self):
        entry = pltpu.get_barrier_semaphore()
        for peer in self.peers():
            pl.semaphore_signal(entry, inc=1, device_id=peer, device_id_type=MESH)
        pl.semaphore_wait(entry, len(self.peers()))


def remote(src, dst, send_sem, recv_sem, device):
    return pltpu.make_async_remote_copy(
        src_ref=src, dst_ref=dst, send_sem=send_sem, recv_sem=recv_sem, device_id=device, device_id_type=MESH
    )


class Gather:
    def __init__(self, full, sems, place):
        self.full = full
        self.sems = sems
        self.place = place
        self.steps = range(1, place.count)

    def copy(self, unit, shard, quarter, rows, name, spot, device):
        ref = self.full.at[unit // 3, shard, quarter, unit % 3]
        ref = ref if rows is None else ref.at[rows]
        spot = (unit,) + spot
        return remote(ref, ref, self.sems[name].at[(0,) + spot], self.sems[name].at[(1,) + spot], device)

    def z_copy(self, unit, step):
        at = self.place
        return self.copy(unit, at.dp, at.section, None, "z", (step - 1,), at.to_z(step))

    def side_copy(self, unit, step, way):
        at = self.place
        return self.copy(unit, at.from_z(step), at.section, None, "side", (step - 1, way), (at.to_x, at.to_y)[way])

    def corner_copy(self, unit, step, way):
        at = self.place
        half = self.full.shape[4] // 2
        quarter, target = (at.x_side, at.to_y) if way == 0 else (at.y_side, at.to_x)
        return self.copy(unit, at.from_z(step), quarter, pl.ds(way * half, half), "corner", (step - 1, way), target)

    def core_copy(self, unit, step, which):
        at = self.place
        quarter = (at.section, at.x_side, at.y_side, at.corner)[which]
        return self.copy(unit, at.from_z(step), quarter, None, "core", (step, which), at.to_core)

    def begin(self, unit):
        for step in self.steps:
            self.z_copy(unit, step).start()
        for which in range(4):
            self.core_copy(unit, 0, which).start()

    def spread(self, unit):
        for step in self.steps:
            self.z_copy(unit, step).wait_recv()
            for way in range(2):
                self.side_copy(unit, step, way).start()
            self.core_copy(unit, step, 0).start()

    def relay(self, unit):
        for step in self.steps:
            for way in range(2):
                self.side_copy(unit, step, way).wait_recv()
                self.corner_copy(unit, step, way).start()
                self.core_copy(unit, step, 1 + way).start()

    def close(self, unit):
        for step in self.steps:
            for way in range(2):
                self.corner_copy(unit, step, way).wait_recv()
            self.core_copy(unit, step, 3).start()

    def arrive(self, unit):
        for step in range(self.place.count):
            for which in range(4):
                self.core_copy(unit, step, which).wait_recv()

    def drain(self, unit):
        for step in self.steps:
            self.z_copy(unit, step).wait_send()
            for way in range(2):
                self.side_copy(unit, step, way).wait_send()
                self.corner_copy(unit, step, way).wait_send()
        for step in range(self.place.count):
            for which in range(4):
                self.core_copy(unit, step, which).wait_send()


class Rows:
    def __init__(self, place, done, results, mail, send_sems, recv_sems, local_sems):
        self.place = place
        self.done = done
        self.send_sems = send_sems
        self.recv_sems = recv_sems
        self.local_sems = local_sems
        self.moves = []
        self.locals = []
        at = place
        own = at.section
        shared = 4 + at.side
        other = 1 - at.side
        early, late = at.early, at.late
        for step in range(6):
            out = results[step // 3]
            kind = step if step < 3 else 5 - step
            if kind == 1:
                moves = [(None, None, other, out.at[own], at.to_x)]
                local = (None, out.at[own])
            elif kind == 0:
                moves = [
                    (early, early, other, out.at[shared], at.to_x),
                    (late, early, at.side, out.at[own], at.to_y),
                    (late, early, other, out.at[own], at.to_corner),
                ]
                local = (early, out.at[shared])
            else:
                moves = [
                    (late, late, other, out.at[shared], at.to_x),
                    (early, late, at.side, out.at[own], at.to_y),
                    (early, late, other, out.at[own], at.to_corner),
                ]
                local = (late, out.at[shared])
            if step == 0:
                moves.insert(0, (early, late, 1, mail.at[2], at.to_y))
            if step == 3:
                moves.insert(0, (late, early, 0, mail.at[3], at.to_y))
            self.moves.append(moves)
            self.locals.append(local)

    def make(self, step, number):
        _, _, pick, target, device = self.moves[step][number]
        src = self.done.at[2 * (step % 3) + pick]
        return remote(src, target, self.send_sems.at[step, number], self.recv_sems.at[step, number], device)

    def make_local(self, step):
        src = self.done.at[2 * (step % 3) + self.place.side]
        return pltpu.make_async_copy(src, self.locals[step][1], self.local_sems.at[step])

    def ready(self, step, which):
        for number, (sends, _, pick, _, _) in enumerate(self.moves[step]):
            if isinstance(pick, int):
                if pick == which:
                    when(sends, self.make(step, number).start)
            else:
                chosen = pick == which
                when(chosen if sends is None else sends & chosen, self.make(step, number).start)
        sends = self.locals[step][0]
        chosen = self.place.side == which
        when(chosen if sends is None else sends & chosen, self.make_local(step).start)

    def sent(self, step):
        for number, (sends, *_) in enumerate(self.moves[step]):
            when(sends, self.make(step, number).wait_send)
        when(self.locals[step][0], self.make_local(step).wait)

    def mail_here(self, step):
        when(self.moves[step][0][1], self.make(step, 0).wait_recv)

    def received(self, step):
        for number, (_, receives, *_) in enumerate(self.moves[step]):
            if step in (0, 3) and number == 0:
                continue
            when(receives, self.make(step, number).wait_recv)


def mega_kernel(
    inputs, cotangent, table, qkv_w, attn_w, in_w, out_w, own_adapter, own_vec, biases, in_bias,
    outputs, input_grads, full, spill, result,
    attn_v, in_v, out_v, qkv, att, branches, norms, aux, slope, hid, keyb, done, acc, low, dqkv,
    adapters, vecs, grads, parts, total, halves, final,
    z_sem, side_sem, corner_sem, core_sem, own_sem, small_sem, load_sem, row_send, row_recv, row_local, misc_sem,
    part_sem, half_sem,
):
    at = Place()
    length, width = hid.shape[1:]
    chunks = in_v.shape[0]
    cols = [pl.ds(c * width, width) for c in range(chunks)]
    gather = Gather(full, {"z": z_sem, "side": side_sem, "corner": corner_sem, "core": core_sem}, at)
    rows = Rows(at, done, (outputs, input_grads), hid, row_send, row_recv, row_local)
    own = at.section
    shared = 4 + at.side
    early_one = jnp.where(at.early, 1, 0)
    first_row = jnp.where(at.early, shared, own)
    third_row = jnp.where(at.early, own, shared)
    middle = 1 - early_one
    layer_of = [0, middle, 1, 1, middle, 0]

    local = [[], []]
    for layer in range(2):
        block_rows_ = full.shape[4]
        for quarter in range(4):
            first = qkv_w.at[layer, :, cols[quarter]] if quarter < 3 else attn_w.at[layer]
            slab = out_w.at[layer, pl.ds(quarter * block_rows_, block_rows_)]
            for kind, source in enumerate((first, in_w.at[layer, :, cols[quarter]], slab)):
                target = full.at[layer, at.dp, quarter, kind]
                local[layer].append(pltpu.make_async_copy(source, target, own_sem.at[layer, quarter, kind]))
    small = [
        pltpu.make_async_copy(own_adapter, adapters.at[own], misc_sem.at[0]),
        pltpu.make_async_copy(own_vec, vecs.at[own], misc_sem.at[1]),
    ]
    row_in = pltpu.make_async_copy(inputs.at[first_row], hid.at[0], misc_sem.at[2])
    row_own = pltpu.make_async_copy(inputs.at[own], hid.at[1], misc_sem.at[3])
    keys_in = [
        pltpu.make_async_copy(table.at[row], keyb.at[k], misc_sem.at[4 + k])
        for k, row in enumerate((first_row, own, third_row))
    ]
    cot_third = pltpu.make_async_copy(cotangent.at[third_row], hid.at[0], misc_sem.at[7])
    cot_own = pltpu.make_async_copy(cotangent.at[own], hid.at[1], misc_sem.at[8])
    spills = [pltpu.make_async_copy(slope, spill.at[k], misc_sem.at[9 + k]) for k in range(2)]
    returns = [pltpu.make_async_copy(spill.at[k], slope, misc_sem.at[11 + k]) for k in range(2)]
    for copy in local[0] + small + [row_in] + keys_in + local[1]:
        copy.start()
    pl.when(at.early)(row_own.start)
    grads[...] = jnp.zeros_like(grads)
    at.barrier()
    for copy in local[0]:
        copy.wait()
    gather.begin(0)
    for copy in small:
        copy.wait()
    shares = []
    for which, ref in enumerate((adapters, vecs)):
        for i, device in enumerate((at.to_x, at.to_y, at.to_corner)):
            spot = 3 * which + i
            shares.append(remote(ref.at[own], ref.at[own], small_sem.at[0, spot], small_sem.at[1, spot], device))
    for copy in shares:
        copy.start()
    for copy in local[1]:
        copy.wait()

    tasks = []
    for name, unit in (
        ("begin", 1), ("spread", 0), ("begin", 2), ("relay", 0), ("spread", 1), ("begin", 3), ("close", 0),
        ("relay", 1), ("spread", 2), ("begin", 4), ("close", 1), ("relay", 2), ("spread", 3), ("begin", 5), ("close", 2),
        ("relay", 3), ("spread", 4), ("close", 3), ("relay", 4), ("spread", 5), ("close", 4), ("relay", 5), ("close", 5),
    ):
        tasks.append((name, unit))

    def take(count):
        chosen = tasks[:count]
        del tasks[:count]

        def action():
            for name, unit in chosen:
                getattr(gather, name)(unit)

        return action

    def tasks_through(unit):
        if ("close", unit) in tasks:
            take(tasks.index(("close", unit)) + 1)()

    def load(kinds, layer, start=True):
        made = []
        for c in range(chunks):
            for kind in kinds:
                if kind < 2:
                    source, target = full.at[layer, :, c, kind], (attn_v, in_v)[kind].at[c]
                else:
                    span = out_v.shape[1]
                    source, target = full.at[layer, pl.ds(c * span, span), :, kind], out_v.at[c]
                made.append(pltpu.make_async_copy(source, target, load_sem.at[kind, c]))
        if start:
            for copy in made:
                copy.start()

    def loaded(kind, c):
        source = full.at[0, :, c, kind] if kind < 2 else full.at[0, pl.ds(0, out_v.shape[1]), :, kind]
        target = (attn_v, in_v, out_v)[kind].at[c]
        pltpu.make_async_copy(source, target, load_sem.at[kind, c]).wait()

    def vec(stage, row):
        return vecs[stage, row : row + 1]

    def bias(stage, row):
        return biases[stage, row : row + 1]

    def adapter_part(stage, k, sub, hidden, branch):
        down_t = adapters[stage, :64]
        lift = adapters[stage, 64:]
        branch_low = branch.astype(BF16)
        branches[k, sub] = branch_low
        down = dot_nt(branch_low, down_t) + vec(stage, 4)[:, :64]
        act, _ = gelu_both(down)
        lifted = dot(act.astype(BF16), lift) + vec(stage, 1)
        hidden_float = hidden.astype(F32)
        resid = hidden_float + branch + lifted
        center = resid - jnp.mean(resid, -1, keepdims=True)
        inverse = lax.rsqrt(jnp.mean(center * center, -1, keepdims=True) + EPSILON)
        normed = center * inverse
        norms[k, sub] = normed.astype(BF16)
        done[2 * k + sub] = (normed * vec(stage, 2) + vec(stage, 3)).astype(BF16)
        valid = keyb[k, :, 16:17].astype(F32)
        grads[stage, 132:133] += jnp.sum(lifted * lifted * valid, 0, keepdims=True)
        grads[stage, 133:134] += jnp.sum(hidden_float * hidden_float * valid, 0, keepdims=True)
        held = aux.at[k, sub]
        held[:, :64] = down
        held[...] = jnp.where(lanes(length) == 64, inverse, held[...])

    def heads(pair, hooks):
        def body(p, carry):
            pair(p)
            for i, hook in enumerate(hooks):
                pl.when(p == i)(hook)
            return carry

        lax.fori_loop(0, HEADS // 2, body, 0)

    def attention_forward(k, source, hooks):
        layer = layer_of[k]
        stage = 2 * layer
        hidden = hid[source]
        for part in range(3):
            loaded(0, part)
            mixed = dot(hidden, square(attn_v, part))
            if part != 1:
                mixed = mixed + bias(stage, 5 if part == 0 else 6)
            qkv[k, :, cols[part]] = mixed.astype(BF16)
        aux[k, 0] = jnp.zeros((length, 128), F32)

        def pair(p):
            attention_pair_forward(p, 0, length, qkv.at[k], keyb.at[k], att.at[k], aux.at[k, 0])

        heads(pair, hooks)
        loaded(0, 3)
        branch = dot(att[k], square(attn_v, 3)) + bias(stage, 0)
        adapter_part(stage, k, 0, hid[source], branch)
        rows.ready(k, 0)

    def ffn_forward(k, hooks):
        layer = layer_of[k]
        stage = 2 * layer + 1
        for c in range(chunks):
            loaded(1, c)
            pre = dot(done[2 * k], square(in_v, c)) + in_bias[layer, :, c * width : (c + 1) * width]
            act, steep = gelu_both(pre)
            slope[:, cols[c]] = steep.astype(BF16)
            loaded(2, c)
            term = dot(act.astype(BF16), square(out_v, c))
            if c == 0:
                acc[...] = term + bias(stage, 0)
            else:
                acc[...] += term
            if c < len(hooks):
                hooks[c]()
        aux[k, 1] = jnp.zeros((length, 128), F32)
        adapter_part(stage, k, 1, done[2 * k], acc[...])
        rows.ready(k, 1)

    def adapter_back(stage, k, sub, grad):
        down_t = adapters[stage, :64]
        lift = adapters[stage, 64:]
        grad = grad.astype(F32)
        normed = norms[k, sub].astype(F32)
        held = aux[k, sub]
        inverse = held[:, 64:65]
        down = held[:, :64]
        scaled = grad * vec(stage, 2)
        resid = inverse * (
            scaled
            - jnp.mean(scaled, -1, keepdims=True)
            - normed * jnp.mean(scaled * normed, -1, keepdims=True)
        )
        lift_grad = resid.astype(BF16)
        act, steep = gelu_both(down)
        down_grad = (dot_nt(lift_grad, lift) * steep).astype(BF16)
        grads[stage, 0:64] += dot_tn(act.astype(BF16), lift_grad)
        grads[stage, 64:128] += dot_tn(down_grad, branches[k, sub])
        grads[stage, 128:129] += jnp.sum(lift_grad.astype(F32), 0, keepdims=True)
        grads[stage, 129:130] += jnp.sum(normed * grad, 0, keepdims=True)
        grads[stage, 130:131] += jnp.sum(grad, 0, keepdims=True)
        grads[stage, 131:132, :64] += jnp.sum(down_grad.astype(F32), 0, keepdims=True)
        acc[...] = resid
        low[...] = (resid + dot(down_grad, down_t)).astype(BF16)

    def ffn_backward(step, source, after_adapter):
        k = 5 - step
        layer = layer_of[step]
        adapter_back(2 * layer + 1, k, 1, hid[source])
        after_adapter()
        for c in range(chunks):
            if step > 3:
                loaded(2, c)
            act_grad = dot_nt(low[...], square(out_v, c))
            pre_grad = (act_grad * slope[:, cols[c]].astype(F32)).astype(BF16)
            if step > 3:
                loaded(1, c)
            acc[...] += dot_nt(pre_grad, square(in_v, c))
        spot = 2 * (step - 3)
        done[spot + 1] = acc[...].astype(BF16)
        rows.ready(step, 1)

    def attention_backward(step, after_adapter, hooks):
        k = 5 - step
        layer = layer_of[step]
        spot = 2 * (step - 3)
        adapter_back(2 * layer, k, 0, done[spot + 1])
        after_adapter()
        if step > 3:
            loaded(0, 3)
        low[...] = dot_nt(low[...], square(attn_v, 3)).astype(BF16)

        def pair(p):
            attention_pair_backward(p, 0, length, qkv.at[k], keyb.at[k], att.at[k], aux.at[k, 0], low, dqkv)

        heads(pair, hooks)
        for part in range(3):
            if step > 3:
                loaded(0, part)
            acc[...] += dot_nt(dqkv[:, cols[part]], square(attn_v, part))
        done[spot] = acc[...].astype(BF16)
        rows.ready(step, 0)

    def part_copy(slot, stage, device):
        return remote(grads.at[stage], parts.at[slot], part_sem.at[0, slot], part_sem.at[1, slot], device)

    other = 1 - at.side
    upper = [(at.early, 1, 2 + at.side, at.to_y), (at.early, 2, 2 + other, at.to_corner), (at.late, 0, 2 + other, at.to_x)]
    lower = [(at.late, 1, at.side, at.to_y), (at.late, 2, other, at.to_corner), (at.early, 0, other, at.to_x)]

    def send_upper():
        for condition, slot, stage, device in upper:
            pl.when(condition)(part_copy(slot, stage, device).start)

    def send_lower(which):
        for condition, slot, stage, device in lower:
            pl.when(condition & (stage == which))(part_copy(slot, stage, device).start)

    span = GRAD_ROWS // 2
    mine = pl.ds(pl.multiple_of(at.core * span, 8), span)
    theirs = pl.ds(pl.multiple_of((1 - at.core) * span, 8), span)
    near = (at.section, (at.z + 1 - 2 * (at.z % 2)) * 2 + at.core)
    far = at.to_z(2)
    trades = [
        remote(total.at[theirs], halves.at[0], half_sem.at[0, 0], half_sem.at[1, 0], at.to_core),
        remote(total.at[mine], halves.at[1], half_sem.at[0, 1], half_sem.at[1, 1], near),
        remote(total.at[mine], halves.at[2], half_sem.at[0, 2], half_sem.at[1, 2], far),
        remote(final.at[mine], final.at[mine], half_sem.at[0, 3], half_sem.at[1, 3], at.to_core),
    ]

    def collect():
        for slot in range(3):
            part_copy(slot, 0, at.to_x).wait_recv()
        total[...] = grads[own] + parts[0] + parts[1] + parts[2]
        trades[0].start()

    def fold(number):
        def action():
            trades[number].wait()
            total[mine] += halves[number]
            if number < 2:
                trades[number + 1].start()
            else:
                final[mine] = total[mine]
                trades[3].start()

        return action

    def nothing():
        pass

    row_in.wait()
    for copy in keys_in:
        copy.wait()
    tasks_through(0)
    gather.arrive(0)
    load((0,), 0)
    for copy in shares:
        copy.wait()
    attention_forward(0, 0, [nothing, nothing, take(2)])
    cot_third.start()
    tasks_through(2)
    gather.arrive(1)
    gather.arrive(2)
    load((1, 2), 0)
    ffn_forward(0, [take(1) for _ in range(3)])
    spills[0].start()
    pl.when(at.early)(row_own.wait)

    @pl.when(at.late)
    def _():
        hid[1] = done[1]

    tasks_through(3)
    gather.arrive(3)
    load((0,), middle)
    attention_forward(1, 1, [take(1) for _ in range(5)])
    pl.when(at.late)(cot_own.start)
    load((0,), 1)
    tasks_through(5)
    gather.arrive(4)
    gather.arrive(5)
    load((1, 2), middle)
    spills[0].wait()
    ffn_forward(1, [])
    spills[1].start()
    load((1, 2), 1)
    rows.mail_here(0)

    @pl.when(at.early)
    def _():
        hid[2] = done[3]

    attention_forward(2, 2, [])
    spills[1].wait()
    ffn_forward(2, [])
    cot_third.wait()
    rows.sent(0)
    ffn_backward(3, 0, nothing)
    returns[1].start()
    load((1, 2), middle)
    attention_backward(3, nothing, [])
    load((0,), middle)
    pl.when(at.late)(cot_own.wait)

    @pl.when(at.early)
    def _():
        hid[1] = done[0]

    rows.sent(1)
    returns[1].wait()
    ffn_backward(4, 1, nothing)
    returns[0].start()
    load((1, 2), 0)
    attention_backward(4, send_upper, [])
    load((0,), 0)
    rows.mail_here(3)

    @pl.when(at.late)
    def _():
        hid[3] = done[2]

    rows.sent(2)
    returns[0].wait()
    ffn_backward(5, 3, lambda: send_lower(1))
    attention_backward(5, lambda: send_lower(0), [nothing, collect, fold(0), nothing, fold(1), fold(2)])
    trades[3].wait()
    result[...] = final[...]
    for slot in range(3):
        part_copy(slot, 0, at.to_x).wait_send()
    for step in range(6):
        if step >= 3:
            rows.sent(step)
        rows.received(step)
    for unit in range(6):
        gather.drain(unit)


def everything(inputs, cotangent, table, qkv_w, attn_w, in_w, out_w, own_adapter, own_vec, biases, in_bias):
    length, width = inputs.shape[1:]
    shard_rows = qkv_w.shape[1]
    shards = lax.axis_size("dp")
    count = shards // 2
    ffn = in_w.shape[2]
    anyspec = pl.BlockSpec(memory_space=pl.ANY)
    vmem = pl.BlockSpec(memory_space=pltpu.VMEM)
    dma = pltpu.SemaphoreType.DMA
    row = (length, width)
    scratch = [
        pltpu.VMEM((4, shards, shard_rows, width), BF16),
        pltpu.VMEM((4, shards, shard_rows, width), BF16),
        pltpu.VMEM((4, shards // 4, 4, shard_rows, width), BF16),
        pltpu.VMEM((3, length, 3 * width), BF16),
        pltpu.VMEM((3,) + row, BF16),
        pltpu.VMEM((3, 2) + row, BF16),
        pltpu.VMEM((3, 2) + row, BF16),
        pltpu.VMEM((3, 2, length, 128), F32),
        pltpu.VMEM((length, ffn), BF16),
        pltpu.VMEM((4,) + row, BF16),
        pltpu.VMEM((3, length, 128), BF16),
        pltpu.VMEM((6,) + row, BF16),
        pltpu.VMEM(row, F32),
        pltpu.VMEM(row, BF16),
        pltpu.VMEM((length, 3 * width), BF16),
        pltpu.VMEM((4, 128, width), BF16),
        pltpu.VMEM((4, 8, width), F32),
        pltpu.VMEM((4, GRAD_ROWS, width), F32),
        pltpu.VMEM((3, GRAD_ROWS, width), F32),
        pltpu.VMEM((GRAD_ROWS, width), F32),
        pltpu.VMEM((3, GRAD_ROWS // 2, width), F32),
        pltpu.VMEM((GRAD_ROWS, width), F32),
        dma((2, 6, count - 1)),
        dma((2, 6, count - 1, 2)),
        dma((2, 6, count - 1, 2)),
        dma((2, 6, count, 4)),
        dma((2, 4, 3)),
        dma((2, 6)),
        dma((3, 4)),
        dma((6, 4)),
        dma((6, 4)),
        dma((6,)),
        dma((13,)),
        dma((2, 3)),
        dma((2, 4)),
    ]
    outs = [
        (inputs.shape, BF16), (inputs.shape, BF16), ((2, shards, 4, 3, shard_rows, width), BF16),
        ((2, length, ffn), BF16), ((GRAD_ROWS, width), F32),
    ]
    return pl.pallas_call(
        mega_kernel,
        in_specs=[anyspec] * 9 + [vmem] * 2,
        out_specs=[anyspec] * 4 + [vmem],
        out_shape=[jax.ShapeDtypeStruct(shape, dtype) for shape, dtype in outs],
        scratch_shapes=scratch,
        compiler_params=pltpu.CompilerParams(
            collective_id=1, has_side_effects=True, vmem_limit_bytes=MEGA_BYTES
        ),
        cost_estimate=pl.CostEstimate(flops=90_000_000_000, bytes_accessed=200_000_000, transcendentals=0),
        name="everything",
    )(inputs, cotangent, table, qkv_w, attn_w, in_w, out_w, own_adapter, own_vec, biases, in_bias)


X_PAIRS = [(0, 1), (1, 0), (2, 3), (3, 2)]
Y_PAIRS = [(0, 2), (2, 0), (1, 3), (3, 1)]
CROSS = [(0, 3), (3, 0), (1, 2), (2, 1)]


def send(value, pairs, senders=(0, 1, 2, 3)):
    return lax.ppermute(value, "section", [pair for pair in pairs if pair[0] in senders])


def gather_weights(shards):
    section = lax.axis_index("section")
    quarter = lax.dynamic_index_in_dim(shards, section, 0, keepdims=False)
    full = lax.all_gather(quarter, ("dp", "section"), axis=0, tiled=False)
    count = lax.axis_size("dp")
    full = full.reshape((count, lax.axis_size("section")) + quarter.shape)
    return full


def in_quarters(matrix):
    rows, columns = matrix.shape
    return matrix.reshape(rows, 4, columns // 4).transpose(1, 0, 2)


def block_rows(full, kind, by_rows):
    if full.shape[3] % 16 == 0:
        return (full, kind)
    count, quarters, _, rows, width = full.shape
    one = full[:, :, kind]
    if by_rows:
        return (one.reshape(count * rows * quarters // width, quarters, 1, width // quarters, width), 0)
    return (one.transpose(1, 0, 2, 3).reshape(1, quarters, 1, count * rows, width), 0)


def on_device(
    inputs, bucket, padding, cotangent, down_weight, down_bias, up_weight, up_bias, ln_gain, ln_beta, qkv_weight,
    query_bias, value_bias, attn_out_weight, attn_out_bias, ffn_in_weight, ffn_in_bias, ffn_out_weight, ffn_out_bias,
):
    section = lax.axis_index("section")
    early = section < 2
    side = section % 2
    width = inputs.shape[2]
    adapter_width = down_weight.shape[2]
    layers = qkv_weight.shape[0]

    def layer_shards(layer):
        attn = jnp.concatenate([qkv_weight[layer], attn_out_weight[layer]], 1)
        outer = ffn_out_weight[layer]
        return (
            in_quarters(attn)[:, None],
            jnp.stack([in_quarters(ffn_in_weight[layer]), outer.reshape((4, -1) + outer.shape[1:])], 1),
        )

    zero_row = jnp.zeros((1, width), F32)
    own_vec = jnp.concatenate(
        [zero_row, up_bias, ln_gain, ln_beta, jnp.pad(down_bias, ((0, 0), (0, width - adapter_width))), zero_row, zero_row, zero_row], 0
    )
    own_adapter = jnp.concatenate([down_weight[0].T, up_weight[0]], 0)
    biases = jnp.zeros((layers, 2, 8, width), F32)
    biases = biases.at[:, 0, 0].set(attn_out_bias).at[:, 0, 5].set(query_bias).at[:, 0, 6].set(value_bias)
    biases = biases.at[:, 1, 0].set(ffn_out_bias)
    in_bias = ffn_in_bias[:, None, :]
    table = key_table(bucket, padding)

    def results(outputs, input_grads, total):
        ratios = jnp.sqrt(jnp.sum(total[132]) / jnp.sum(total[133]))[None]
        return (
            outputs[None],
            input_grads[None],
            total[64:128].T[None],
            total[131, :adapter_width][None],
            total[0:64][None],
            total[128][None],
            total[129][None],
            total[130][None],
            ratios,
        )

    if lax.axis_size("dp") == 8 and lax.axis_size("section") == 4 and inputs.shape[0] == 6:
        outputs, input_grads, _, _, total = everything(
            inputs, cotangent, table, qkv_weight, attn_out_weight, ffn_in_weight, ffn_out_weight, own_adapter, own_vec,
            biases.reshape(2 * layers, 8, width), in_bias,
        )
        return results(outputs, input_grads, total)

    weights = []
    for layer in range(layers):
        full = gather_weights(jnp.concatenate(layer_shards(layer), 1))
        weights.append([block_rows(full, 0, False), block_rows(full, 1, False), block_rows(full, 2, True)])
    adapters = lax.all_gather(own_adapter, "section", axis=0, tiled=False)
    vecs = lax.all_gather(own_vec, "section", axis=0, tiled=False)
    adapters = adapters.reshape(layers, 2, 128, width)
    vecs = vecs.reshape(layers, 2, 8, width)
    vecs = (vecs + biases).reshape(layers, 16, width)
    own = section
    shared = 4 + side

    def row_of(array, row):
        return lax.dynamic_index_in_dim(array, row, 0, keepdims=False)

    def forward(row, hidden, layer, weights_used, choice):
        return forward_pair(
            layer, choice, row_of(bucket, row), hidden, row_of(table, row), weights_used, adapters, vecs, in_bias
        )

    def backward(row, grad, saved, layer, weights_used, choice):
        return backward_pair(
            layer, choice, row_of(bucket, row), grad, row_of(table, row), saved, weights_used, adapters, vecs
        )

    zero = jnp.int32(0)
    one = jnp.int32(1)
    late = 1 - early.astype(jnp.int32)
    first_row = jnp.where(early, shared, own)
    third_row = jnp.where(early, own, shared)

    f0 = forward(first_row, row_of(inputs, first_row), zero, weights[:1], zero)
    x0 = send(jnp.where(side == 0, f0[1], f0[0]), X_PAIRS, (0, 1))
    y0 = send(jnp.where(early | (side == 1), f0[1], f0[0]), Y_PAIRS)
    z0 = send(jnp.where(side == 0, f0[1], f0[0]), CROSS, (2, 3))
    hidden = jnp.where(early, row_of(inputs, own), f0[1])
    f1 = forward(own, hidden, late, weights, late)
    x1 = send(jnp.where(side == 0, f1[1], f1[0]), X_PAIRS)
    hidden = jnp.where(early, f1[1], y0)
    f2 = forward(third_row, hidden, one, weights[1:], zero)
    x2 = send(jnp.where(side == 0, f2[1], f2[0]), X_PAIRS, (2, 3))
    y2 = send(jnp.where(side == 1, f2[1], f2[0]), Y_PAIRS, (0, 1))
    z2 = send(jnp.where(side == 0, f2[1], f2[0]), CROSS, (0, 1))

    b3 = backward(third_row, row_of(cotangent, third_row), f2[2:11], one, weights[1:], zero)
    x3 = send(jnp.where(side == 0, b3[0], b3[1]), X_PAIRS, (2, 3))
    y3 = send(jnp.where(early & (side == 1), b3[0], b3[1]), Y_PAIRS)
    z3 = send(jnp.where(side == 0, b3[0], b3[1]), CROSS, (0, 1))
    grad = jnp.where(early, b3[1], row_of(cotangent, own))
    b4 = backward(own, grad, f1[2:11], late, weights, late)
    x4 = send(jnp.where(side == 0, b4[0], b4[1]), X_PAIRS)
    grad = jnp.where(early, y3, b4[1])
    b5 = backward(first_row, grad, f0[2:11], zero, weights[:1], zero)
    x5 = send(jnp.where(side == 0, b5[0], b5[1]), X_PAIRS, (0, 1))
    y5 = send(jnp.where(side == 1, b5[0], b5[1]), Y_PAIRS, (2, 3))
    z5 = send(jnp.where(side == 0, b5[0], b5[1]), CROSS, (2, 3))

    def assemble(parts):
        result = jnp.zeros(inputs.shape, BF16)
        for row, part in parts:
            result = lax.dynamic_update_index_in_dim(result, part, row, 0)
        return result

    other = section + 1 - 2 * side
    across = jnp.where(early, section + 2, section - 2)
    corner = 3 - section
    other_shared = 4 + 1 - side
    outputs = assemble(
        [
            (own, jnp.where(side == 0, f1[0], f1[1])),
            (other, x1),
            (across, jnp.where(early, y0, y2)),
            (corner, jnp.where(early, z0, z2)),
            (shared, jnp.where(early, jnp.where(side == 0, f0[0], f0[1]), jnp.where(side == 0, f2[0], f2[1]))),
            (other_shared, jnp.where(early, x0, x2)),
        ]
    )
    input_grads = assemble(
        [
            (own, jnp.where(side == 0, b4[1], b4[0])),
            (other, x4),
            (across, jnp.where(early, y5, y3)),
            (corner, jnp.where(early, z5, z3)),
            (shared, jnp.where(early, jnp.where(side == 0, b5[1], b5[0]), jnp.where(side == 0, b3[1], b3[0]))),
            (other_shared, jnp.where(early, x5, x3)),
        ]
    )

    def with_sums(grads, sums):
        return grads.at[:, 132:134].set(sums[:4].reshape(2, 2, width))

    g3, g4, g5 = with_sums(b3[2], f2[11]), with_sums(b4[2], f1[11]), with_sums(b5[2], f0[11])
    low_layer = g5 + jnp.where(early, g4, 0.0)
    high_layer = g3 + jnp.where(early, 0.0, g4)
    mine = lax.psum_scatter(jnp.concatenate([low_layer, high_layer], 0), "section", scatter_dimension=0, tiled=False)
    return results(outputs, input_grads, lax.psum(mine, "dp"))


def solution(mesh):
    in_specs = (
        P("dp", None, None),
        P("dp"),
        P("dp", None),
        P("dp", None, None),
        P("section", None, None),
        P("section", None),
        P("section", None, None),
        P("section", None),
        P("section", None),
        P("section", None),
        P(None, "dp", None),
        P(),
        P(),
        P(None, "dp", None),
        P(),
        P(None, "dp", None),
        P(),
        P(None, "dp", None),
        P(),
    )
    out_specs = (
        P("section", "dp", None, None),
        P("section", "dp", None, None),
        P("section", None, None),
        P("section", None),
        P("section", None, None),
        P("section", None),
        P("section", None),
        P("section", None),
        P("section"),
    )
    return jax.shard_map(
        on_device, mesh=mesh, in_specs=in_specs, out_specs=out_specs, check_vma=False
    )
```

```python
import functools
import jax
import jax.numpy as jnp
from jax import lax
from jax.experimental import pallas as pl
from jax.experimental.pallas import tpu as pltpu
from jax.sharding import PartitionSpec as P

HEADS = 12
HD = 64
SEG = 64
EPSILON = 1e-05
MASKED = -1e30
LOG_TOP = 24
VMEM_BYTES = 56 * 1024 * 1024
F32 = jnp.float32
BF16 = jnp.bfloat16


def dot(left, right):
    return jnp.dot(left, right, preferred_element_type=F32)


def dot_nt(left, right):
    return lax.dot_general(left, right, (((1,), (1,)), ((), ())), preferred_element_type=F32)


def dot_tn(left, right):
    return lax.dot_general(left, right, (((0,), (0,)), ((), ())), preferred_element_type=F32)


def gelu_both(v):
    size = jnp.abs(v)
    bell = jnp.exp(v * v * -0.5)
    below = 1.0 + size * (0.3275911 * 0.7071067811865476)
    t = pl.reciprocal(below, approx=True)
    t = t * (2.0 - below * t)
    tail = t * (
        0.127414796
        + t * (-0.142248368 + t * (0.7107068705 + t * (-0.7265760135 + t * 0.5307027145)))
    )
    tail = tail * bell
    cdf = jnp.where(v >= 0, 1.0 - tail, tail)
    return (jnp.maximum(v, 0.0) - size * tail, cdf + v * (bell * 0.3989422804014327))


def lanes(rows):
    return lax.broadcasted_iota(jnp.int32, (rows, 128), 1)


def adapter_forward(hidden, branch, adapter_ref, vec_ref, base, stage, aux, valid):
    down_t = adapter_ref[0, stage, :64]
    lift = adapter_ref[0, stage, 64:]
    branch_low = branch.astype(BF16)
    down = dot_nt(branch_low, down_t) + vec_ref[0, base + 4 : base + 5, :64]
    act, _ = gelu_both(down)
    lifted = dot(act.astype(BF16), lift) + vec_ref[0, base + 1 : base + 2]
    hidden_float = hidden.astype(F32)
    resid = hidden_float + branch + lifted
    mean = jnp.mean(resid, -1, keepdims=True)
    center = resid - mean
    inverse = lax.rsqrt(jnp.mean(center * center, -1, keepdims=True) + EPSILON)
    normed = center * inverse
    output = (normed * vec_ref[0, base + 2 : base + 3] + vec_ref[0, base + 3 : base + 4]).astype(BF16)
    sums = (
        jnp.sum(lifted * lifted * valid, 0, keepdims=True),
        jnp.sum(hidden_float * hidden_float * valid, 0, keepdims=True),
    )
    return branch_low, down, output, normed.astype(BF16), inverse, sums


def column_copies(weight, kind, chunk, held, sem):
    return pltpu.make_async_copy(weight.at[:, chunk, kind], held.at[chunk], sem)


def row_copies(weight, kind, chunk, held, sem):
    span = held.shape[1]
    return pltpu.make_async_copy(weight.at[pl.ds(chunk * span, span), :, kind], held.at[chunk], sem)


def start_copies(choice, sources, order, sems):
    made = []
    for which, source in enumerate(sources):
        copies = [make(source[matrix][0], source[matrix][1], chunk, held, sems.at[i])
                  for i, (make, matrix, chunk, held) in enumerate(order)]
        made.append(copies)

        @pl.when(choice == which)
        def _():
            for copy in copies:
                copy.start()

    return made[0]


def square(held, chunk):
    width = held.shape[-1]
    return held[chunk].reshape(width, width)


def attention_pair_forward(p, start, size, qkv, keyb, att, aux):
    rows = pl.ds(start, size)
    width = att.shape[1]
    col = pl.multiple_of(p * 128, 128)
    lane = lanes(size)
    query = qkv[rows, pl.ds(col, 128)]
    key = qkv[rows, pl.ds(width + col, 128)]
    value = qkv[rows, pl.ds(2 * width + col, 128)]
    bias = keyb[rows]
    place = start + lax.broadcasted_iota(jnp.int32, (size, 128), 0)
    hot = jnp.where(lane % 64 == place // SEG, 1.0, 0.0).astype(BF16)
    query = query * jnp.asarray(HD ** -0.5, BF16)
    total = None
    for half in range(2):
        mine = (lane < 64) if half == 0 else (lane >= 64)
        scores = dot_nt(jnp.where(mine, query, hot), jnp.where(mine, key, bias))
        peak = jnp.max(scores, -1, keepdims=True)
        expo = jnp.exp(scores - peak)
        norm = jnp.sum(expo, -1, keepdims=True)
        part = dot(expo.astype(BF16), jnp.where(mine, value, jnp.zeros_like(value))) * (1.0 / norm)
        log_total = peak + jnp.log(norm)
        aux[rows] = jnp.where(lane == 80 + 2 * p + half, log_total, aux[rows])
        total = part if total is None else total + part
    att[rows, pl.ds(col, 128)] = total.astype(BF16)


def forward_kernel(
    sources, idx, hidden_ref, keyb_ref, adapter_ref, vec_ref, in_bias_ref,
    h1_ref, h2_ref, qkv_ref, att_ref, br1_ref, nh1_ref, aux1_ref, slope_ref, br2_ref, nh2_ref, aux2_ref, sums_ref,
    attn_v, in_v, out_v, acc, sems,
):
    bucket = idx[1]
    length, width = hidden_ref.shape
    chunks = in_v.shape[0]
    cols = [pl.ds(c * width, width) for c in range(chunks)]
    order = [(column_copies, 0, c, attn_v) for c in range(4)]
    for c in range(chunks):
        order.append((column_copies, 1, c, in_v))
        order.append((row_copies, 2, c, out_v))
    copies = start_copies(idx[2], sources, order, sems)
    hidden = hidden_ref[...]
    valid = keyb_ref[:, 16:17].astype(F32)
    for part in range(3):
        copies[part].wait()
        mixed = dot(hidden, square(attn_v, part))
        if part == 0:
            mixed = mixed + vec_ref[0, 5:6]
        if part == 2:
            mixed = mixed + vec_ref[0, 6:7]
        qkv_ref[:, cols[part]] = mixed.astype(BF16)
    aux1_ref[...] = jnp.zeros_like(aux1_ref)

    def heads(size):
        blocks = length // size

        def body(step, carry):
            p = step // blocks
            start = pl.multiple_of((step % blocks) * size, size)
            attention_pair_forward(p, start, size, qkv_ref, keyb_ref, att_ref, aux1_ref)
            return carry

        lax.fori_loop(0, (HEADS // 2) * blocks, body, 0)

    @pl.when(bucket >= 3)
    def _():
        heads(length)

    @pl.when(bucket < 3)
    def _():
        heads(length // 2)

    copies[3].wait()
    branch = dot(att_ref[...], square(attn_v, 3)) + vec_ref[0, 0:1]
    branch_low, down, output, normed, inverse, sums = adapter_forward(
        hidden, branch, adapter_ref, vec_ref, 0, 0, None, valid
    )
    br1_ref[...] = branch_low
    nh1_ref[...] = normed
    h1_ref[...] = output
    lane = lanes(length)
    aux1_ref[:, :64] = down
    aux1_ref[...] = jnp.where(lane == 64, inverse, aux1_ref[...])
    sums_ref[0:1] = sums[0]
    sums_ref[1:2] = sums[1]
    hidden = h1_ref[...]
    for c in range(chunks):
        copies[4 + 2 * c].wait()
        pre = dot(hidden, square(in_v, c)) + in_bias_ref[0, :, c * width : (c + 1) * width]
        act, slope = gelu_both(pre)
        slope_ref[:, cols[c]] = slope.astype(BF16)
        copies[5 + 2 * c].wait()
        term = dot(act.astype(BF16), square(out_v, c))
        if c == 0:
            acc[...] = term + vec_ref[0, 8:9]
        else:
            acc[...] += term
    branch_low, down, output, normed, inverse, sums = adapter_forward(
        hidden, acc[...], adapter_ref, vec_ref, 8, 1, None, valid
    )
    br2_ref[...] = branch_low
    nh2_ref[...] = normed
    h2_ref[...] = output
    aux2_ref[...] = jnp.where(lane == 64, inverse, jnp.zeros((length, 128), F32))
    aux2_ref[:, :64] = down
    sums_ref[2:3] = sums[0]
    sums_ref[3:4] = sums[1]
    sums_ref[4:8] = jnp.zeros_like(sums_ref[4:8])


def weight_plan(weights):
    arrays, places = [], []
    for layer in weights:
        spots = []
        for array, kind in layer:
            found = [i for i, other in enumerate(arrays) if other is array]
            if not found:
                arrays.append(array)
                found = [len(arrays) - 1]
            spots.append((found[0], kind))
        places.append(spots)
    return arrays, places


def weight_scratch(weights):
    attn, inner, outer = [array.shape for array, _ in weights[0]]
    width = attn[-1]
    span = width // (4 * outer[3])
    return [
        pltpu.VMEM((4, attn[0], attn[3], width), BF16),
        pltpu.VMEM((4, inner[0], inner[3], width), BF16),
        pltpu.VMEM((outer[0] // span, span, 4, outer[3], width), BF16),
    ]


def whole(shape):
    return pl.BlockSpec(shape, lambda i, s: (0,) * len(shape))


def by_layer(shape):
    return pl.BlockSpec((1,) + shape, lambda i, s: (s[0],) + (0,) * len(shape))


def call_with_weights(kernel, weights, blocks, outs, scratch, flops, name):
    arrays, places = weight_plan(weights)
    fixed = len(blocks)
    idx, rest = blocks[0], blocks[1:]

    def body(*refs):
        held = refs[fixed : fixed + len(arrays)]
        sources = [[(held[i], kind) for i, kind in spots] for spots in places]
        kernel(sources, *refs[:fixed], *refs[fixed + len(arrays) :])

    copies = 12
    return pl.pallas_call(
        body,
        grid_spec=pltpu.PrefetchScalarGridSpec(
            num_scalar_prefetch=1,
            grid=(1,),
            in_specs=[spec for _, spec in rest] + [pl.BlockSpec(memory_space=pl.ANY)] * len(arrays),
            out_specs=[whole(shape) for shape, _ in outs],
            scratch_shapes=weight_scratch(weights) + scratch + [pltpu.SemaphoreType.DMA((copies,))],
        ),
        out_shape=[jax.ShapeDtypeStruct(shape, dtype) for shape, dtype in outs],
        compiler_params=pltpu.CompilerParams(vmem_limit_bytes=VMEM_BYTES),
        cost_estimate=pl.CostEstimate(flops=flops, bytes_accessed=24_000_000, transcendentals=0),
        name=name,
    )(idx, *[array for array, _ in rest], *arrays)


def forward_pair(layer, choice, bucket, hidden, keyb, weights, adapters, vecs, in_bias):
    length, width = hidden.shape
    ffn = in_bias.shape[-1]
    idx = jnp.stack([layer, bucket, choice]).astype(jnp.int32)
    outs = [
        ((length, width), BF16), ((length, width), BF16), ((length, 3 * width), BF16), ((length, width), BF16),
        ((length, width), BF16), ((length, width), BF16), ((length, 128), F32), ((length, ffn), BF16),
        ((length, width), BF16), ((length, width), BF16), ((length, 128), F32), ((8, width), F32),
    ]
    blocks = [
        idx, (hidden, whole((length, width))), (keyb, whole((length, 128))), (adapters, by_layer((2, 128, width))),
        (vecs, by_layer((16, width))), (in_bias, by_layer((1, ffn))),
    ]
    scratch = [pltpu.VMEM((length, width), F32)]
    return call_with_weights(forward_kernel, weights, blocks, outs, scratch, 12_000_000_000, "forward_pair")


def adapter_backward(grad, normed, branch_low, aux, adapter_ref, vec_ref, base, stage, grads_ref):
    down_t = adapter_ref[0, stage, :64]
    lift = adapter_ref[0, stage, 64:]
    grad = grad.astype(F32)
    normed = normed.astype(F32)
    inverse = aux[:, 64:65]
    down = aux[:, :64]
    scaled = grad * vec_ref[0, base + 2 : base + 3]
    resid = inverse * (
        scaled
        - jnp.mean(scaled, -1, keepdims=True)
        - normed * jnp.mean(scaled * normed, -1, keepdims=True)
    )
    lift_grad = resid.astype(BF16)
    act, slope = gelu_both(down)
    down_grad = (dot_nt(lift_grad, lift) * slope).astype(BF16)
    grads_ref[stage, 0:64] = dot_tn(act.astype(BF16), lift_grad)
    grads_ref[stage, 64:128] = dot_tn(down_grad, branch_low)
    grads_ref[stage, 128:136] = jnp.zeros_like(grads_ref[stage, 128:136])
    grads_ref[stage, 128:129] = jnp.sum(lift_grad.astype(F32), 0, keepdims=True)
    grads_ref[stage, 129:130] = jnp.sum(normed * grad, 0, keepdims=True)
    grads_ref[stage, 130:131] = jnp.sum(grad, 0, keepdims=True)
    grads_ref[stage, 131:132, :64] = jnp.sum(down_grad.astype(F32), 0, keepdims=True)
    branch_grad = (resid + dot(down_grad, down_t)).astype(BF16)
    return resid, branch_grad


def split_low(column):
    high = column.astype(BF16).astype(F32)
    rest = column - high
    middle = rest.astype(BF16).astype(F32)
    return high, middle, rest - middle


def attention_pair_backward(p, start, size, qkv, keyb, att, aux, att_grad, dqkv):
    rows = pl.ds(start, size)
    width = att.shape[1]
    col = pl.multiple_of(p * 128, 128)
    lane = lanes(size)
    query = qkv[rows, pl.ds(col, 128)] * jnp.asarray(HD ** -0.5, BF16)
    key = qkv[rows, pl.ds(width + col, 128)]
    value = qkv[rows, pl.ds(2 * width + col, 128)]
    grad = att_grad[rows, pl.ds(col, 128)]
    product = grad.astype(F32) * att[rows, pl.ds(col, 128)].astype(F32)
    bias = keyb[rows]
    place = start + lax.broadcasted_iota(jnp.int32, (size, 128), 0)
    spot = lane % 64
    hot = jnp.where(spot == place // SEG, 1.0, 0.0)
    aux_rows = aux[rows]
    zero = jnp.zeros((size, 128), BF16)
    sums = [None, None, None]
    for half in range(2):
        mine = (lane < 64) if half == 0 else (lane >= 64)
        log_total = jnp.sum(jnp.where(lane == 80 + 2 * p + half, aux_rows, 0.0), -1, keepdims=True)
        parts = split_low(-log_total)
        extra = jnp.where(spot == LOG_TOP, parts[0], jnp.where(spot == LOG_TOP + 1, parts[1], jnp.where(spot == LOG_TOP + 2, parts[2], hot)))
        row_dot = jnp.sum(jnp.where(mine, product, 0.0), -1, keepdims=True)
        dots = split_low(-row_dot)
        extra_grad = jnp.where(spot == LOG_TOP, dots[0], jnp.where(spot == LOG_TOP + 1, dots[1], jnp.where(spot == LOG_TOP + 2, dots[2], 0.0)))
        key_side = jnp.where(mine, key, bias)
        value_side = jnp.where(mine, value, bias)
        probs = jnp.exp(dot_nt(key_side, jnp.where(mine, query, extra.astype(BF16))))
        centred = dot_nt(value_side, jnp.where(mine, grad, extra_grad.astype(BF16)))
        score_grad = (probs * centred).astype(BF16)
        terms = (
            dot_tn(score_grad, jnp.where(mine, key, zero)),
            dot(score_grad, jnp.where(mine, query, zero)),
            dot(probs.astype(BF16), jnp.where(mine, grad, zero)),
        )
        sums = [t if s is None else s + t for s, t in zip(sums, terms)]
    dqkv[rows, pl.ds(col, 128)] = (sums[0] * HD ** -0.5).astype(BF16)
    dqkv[rows, pl.ds(width + col, 128)] = sums[1].astype(BF16)
    dqkv[rows, pl.ds(2 * width + col, 128)] = sums[2].astype(BF16)


def backward_kernel(
    sources, idx, grad_ref, keyb_ref, qkv_ref, att_ref, br1_ref, nh1_ref, aux1_ref, slope_ref, br2_ref, nh2_ref,
    aux2_ref, adapter_ref, vec_ref,
    g2_ref, g1_ref, grads_ref,
    attn_v, in_v, out_v, acc, low, dqkv, sems,
):
    bucket = idx[1]
    length, width = grad_ref.shape
    chunks = in_v.shape[0]
    cols = [pl.ds(c * width, width) for c in range(chunks)]
    order = []
    for c in range(chunks):
        order.append((row_copies, 2, c, out_v))
        order.append((column_copies, 1, c, in_v))
    order += [(column_copies, 0, c, attn_v) for c in (3, 0, 1, 2)]
    copies = start_copies(idx[2], sources, order, sems)
    resid, branch_grad = adapter_backward(
        grad_ref[...], nh2_ref[...], br2_ref[...], aux2_ref[...], adapter_ref, vec_ref, 8, 1, grads_ref
    )
    acc[...] = resid
    low[...] = branch_grad
    for c in range(chunks):
        copies[2 * c].wait()
        act_grad = dot_nt(low[...], square(out_v, c))
        pre_grad = (act_grad * slope_ref[:, cols[c]].astype(F32)).astype(BF16)
        copies[2 * c + 1].wait()
        acc[...] += dot_nt(pre_grad, square(in_v, c))
    g2_ref[...] = acc[...].astype(BF16)
    resid, branch_grad = adapter_backward(
        g2_ref[...], nh1_ref[...], br1_ref[...], aux1_ref[...], adapter_ref, vec_ref, 0, 0, grads_ref
    )
    acc[...] = resid
    copies[2 * chunks].wait()
    low[...] = dot_nt(branch_grad, square(attn_v, 3)).astype(BF16)

    def heads(size):
        blocks = length // size

        def body(step, carry):
            p = step // blocks
            start = pl.multiple_of((step % blocks) * size, size)
            attention_pair_backward(p, start, size, qkv_ref, keyb_ref, att_ref, aux1_ref, low, dqkv)
            return carry

        lax.fori_loop(0, (HEADS // 2) * blocks, body, 0)

    @pl.when(bucket >= 3)
    def _():
        heads(length)

    @pl.when(bucket < 3)
    def _():
        heads(length // 2)

    for part in range(3):
        copies[2 * chunks + 1 + part].wait()
        acc[...] += dot_nt(dqkv[:, cols[part]], square(attn_v, part))
    g1_ref[...] = acc[...].astype(BF16)


def backward_pair(layer, choice, bucket, grad, keyb, saved, weights, adapters, vecs):
    length, width = grad.shape
    idx = jnp.stack([layer, bucket, choice]).astype(jnp.int32)
    outs = [((length, width), BF16), ((length, width), BF16), ((2, 136, width), F32)]
    blocks = [idx, (grad, whole((length, width))), (keyb, whole((length, 128)))]
    blocks += [(member, whole(member.shape)) for member in saved]
    blocks += [(adapters, by_layer((2, 128, width))), (vecs, by_layer((16, width)))]
    scratch = [
        pltpu.VMEM((length, width), F32),
        pltpu.VMEM((length, width), BF16),
        pltpu.VMEM((length, 3 * width), BF16),
    ]
    return call_with_weights(backward_kernel, weights, blocks, outs, scratch, 16_000_000_000, "backward_pair")


def key_table(bucket, padding):
    rows, length = padding.shape
    spot = jnp.arange(128, dtype=jnp.int32) % 64
    shift = 6 + bucket[:, None, None]
    place = jnp.arange(length, dtype=jnp.int32)
    same = (spot[None, None, :] * SEG) >> shift == place[None, :, None] >> shift
    real = (padding == 1)[:, :, None]
    table = jnp.where(same & real, 0.0, MASKED)
    ones = (spot >= LOG_TOP) & (spot < LOG_TOP + 3)
    table = jnp.where(spot < 8, table, jnp.where(spot == 16, real.astype(F32), jnp.where(ones, 1.0, 0.0)))
    return table.astype(BF16)


MESH = pl.DeviceIdType.MESH
GRAD_ROWS = 144
MEGA_BYTES = 63 * 1024 * 1024


def when(condition, action):
    if condition is None:
        action()
    else:
        pl.when(condition)(action)


class Place:
    def __init__(self):
        self.section = lax.axis_index("section")
        self.dp = lax.axis_index("dp")
        self.count = lax.axis_size("dp") // 2
        self.z = self.dp // 2
        self.core = self.dp % 2
        self.side = self.section % 2
        self.early = self.section < 2
        self.late = self.section >= 2
        self.x_side = self.section + 1 - 2 * self.side
        self.y_side = lax.rem(self.section + 2, 4)
        self.corner = 3 - self.section
        self.to_x = (self.x_side, self.dp)
        self.to_y = (self.y_side, self.dp)
        self.to_corner = (self.corner, self.dp)
        self.to_core = (self.section, self.dp + 1 - 2 * self.core)

    def to_z(self, step):
        return (self.section, lax.rem(self.z + step, self.count) * 2 + self.core)

    def from_z(self, step):
        return lax.rem(self.z + self.count - step, self.count) * 2 + self.core

    def peers(self):
        return [self.to_z(d) for d in range(1, self.count)] + [self.to_x, self.to_y, self.to_corner, self.to_core]

    def barrier(self):
        entry = pltpu.get_barrier_semaphore()
        for peer in self.peers():
            pl.semaphore_signal(entry, inc=1, device_id=peer, device_id_type=MESH)
        pl.semaphore_wait(entry, len(self.peers()))


def remote(src, dst, send_sem, recv_sem, device):
    return pltpu.make_async_remote_copy(
        src_ref=src, dst_ref=dst, send_sem=send_sem, recv_sem=recv_sem, device_id=device, device_id_type=MESH
    )


class Gather:
    def __init__(self, full, stage, sems, place):
        self.full = full
        self.stage = stage
        self.sems = sems
        self.place = place
        self.steps = range(1, place.count)

    def staged(self, unit, quarter):
        rows, width = self.full.shape[4:]
        kind = unit % 3
        last = quarter // 3
        line = (0 + last, 2 - last, 3 + last)[kind]
        column = quarter - 2 * last if kind == 1 else quarter - 3 * last
        if not isinstance(quarter, int):
            return self.stage[unit // 3].at[
                pl.ds(pl.multiple_of(line * rows, 16), rows), pl.ds(pl.multiple_of(column * width, 128), width)
            ]
        return self.stage[unit // 3].at[pl.ds(line * rows, rows), pl.ds(column * width, width)]

    def copy(self, unit, shard, quarter, rows, name, spot, device, source=None):
        ref = self.full.at[unit // 3, shard, quarter, unit % 3]
        ref = ref if rows is None else ref.at[rows]
        source = ref if source is None else source
        spot = (unit,) + spot
        return remote(source, ref, self.sems[name].at[(0,) + spot], self.sems[name].at[(1,) + spot], device)

    def z_copy(self, unit, step):
        at = self.place
        source = self.staged(unit, at.section)
        return self.copy(unit, at.dp, at.section, None, "z", (step - 1,), at.to_z(step), source)

    def side_copy(self, unit, step, way):
        at = self.place
        return self.copy(unit, at.from_z(step), at.section, None, "side", (step - 1, way), (at.to_x, at.to_y)[way])

    def corner_copy(self, unit, step, way):
        at = self.place
        half = self.full.shape[4] // 2
        quarter, target = (at.x_side, at.to_y) if way == 0 else (at.y_side, at.to_x)
        return self.copy(unit, at.from_z(step), quarter, pl.ds(way * half, half), "corner", (step - 1, way), target)

    def core_copy(self, unit, step, which):
        at = self.place
        if step == 0:
            return self.copy(unit, at.dp, which, None, "core", (0, which), at.to_core, self.staged(unit, which))
        quarter = (at.section, at.x_side, at.y_side, at.corner)[which]
        return self.copy(unit, at.from_z(step), quarter, None, "core", (step, which), at.to_core)

    def own_copy(self, unit, quarter):
        target = self.full.at[unit // 3, self.place.dp, quarter, unit % 3]
        return pltpu.make_async_copy(self.staged(unit, quarter), target, self.sems["own"].at[unit, quarter])

    def stage_copies(self, layer, qkv_w, attn_w, in_w, out_w):
        rows, width = self.full.shape[4:]
        pieces = [
            (qkv_w.at[layer], 0, 0, 3 * width),
            (attn_w.at[layer], 1, 0, width),
            (in_w.at[layer, :, pl.ds(0, 3 * width)], 2, 0, 3 * width),
            (in_w.at[layer, :, pl.ds(3 * width, width)], 1, 1, width),
        ]
        for quarter in range(4):
            pieces.append((out_w.at[layer, pl.ds(quarter * rows, rows)], 3 + quarter // 3, quarter % 3, width))
        made = []
        for i, (source, line, column, span) in enumerate(pieces):
            target = self.stage[layer].at[pl.ds(line * rows, rows), pl.ds(column * width, span)]
            made.append(pltpu.make_async_copy(source, target, self.sems["stage"].at[layer, i]))
        return made

    def release(self, layer):
        for unit in range(3 * layer, 3 * layer + 3):
            for step in self.steps:
                self.z_copy(unit, step).wait_send()
            for quarter in range(4):
                self.core_copy(unit, 0, quarter).wait_send()

    def begin(self, unit):
        for step in self.steps:
            self.z_copy(unit, step).start()
        for which in range(4):
            self.core_copy(unit, 0, which).start()
            self.own_copy(unit, which).start()

    def spread(self, unit):
        for step in self.steps:
            self.z_copy(unit, step).wait_recv()
            for way in range(2):
                self.side_copy(unit, step, way).start()
            self.core_copy(unit, step, 0).start()

    def relay(self, unit):
        for step in self.steps:
            for way in range(2):
                self.side_copy(unit, step, way).wait_recv()
                self.corner_copy(unit, step, way).start()
                self.core_copy(unit, step, 1 + way).start()

    def close(self, unit):
        for step in self.steps:
            for way in range(2):
                self.corner_copy(unit, step, way).wait_recv()
            self.core_copy(unit, step, 3).start()

    def arrive(self, unit):
        for quarter in range(4):
            self.own_copy(unit, quarter).wait()
        for step in range(self.place.count):
            for which in range(4):
                self.core_copy(unit, step, which).wait_recv()

    def drain(self, unit):
        for step in self.steps:
            for way in range(2):
                self.side_copy(unit, step, way).wait_send()
                self.corner_copy(unit, step, way).wait_send()
            for which in range(4):
                self.core_copy(unit, step, which).wait_send()


class Rows:
    def __init__(self, place, done, norms, slot_of, results, mail, send_sems, recv_sems, local_sems):
        self.place = place
        self.done = done
        self.norms = norms
        self.slot_of = slot_of
        self.send_sems = send_sems
        self.recv_sems = recv_sems
        self.local_sems = local_sems
        self.moves = []
        self.locals = []
        self.held = None
        at = place
        own = at.section
        shared = 4 + at.side
        other = 1 - at.side
        early, late = at.early, at.late
        self.base = (0, 2, 4, 2)
        for step in range(7):
            out = results[step // 4]
            if step in (0, 6):
                near = own if step == 0 else shared
                moves = [
                    (early, early, other, out.at[near], at.to_x),
                    (late, early, at.side, out.at[own], at.to_y),
                    (late, early, other, out.at[own], at.to_corner),
                ]
                local = (early, out.at[near])
            elif step in (2, 4):
                near = own if step == 2 else shared
                moves = [
                    (late, late, other, out.at[near], at.to_x),
                    (early, late, at.side, out.at[own], at.to_y),
                    (early, late, other, out.at[own], at.to_corner),
                ]
                local = (late, out.at[near])
            elif step == 5:
                moves = [(None, None, other, out.at[own], at.to_x)]
                local = (None, out.at[own])
            else:
                mine = early if step == 1 else late
                moves = [(mine, mine, other, out.at[shared], at.to_x)]
                local = (mine, out.at[shared])
            if step == 4:
                moves.insert(0, (late, early, 0, mail, at.to_y))
            self.moves.append(moves)
            self.locals.append(local)

    def source(self, step, pick):
        return self.done.at[self.base[step] + pick] if step < 4 else self.norms.at[self.slot_of[step], pick]

    def make(self, step, number):
        _, _, pick, target, device = self.moves[step][number]
        src = self.source(step, pick)
        return remote(src, target, self.send_sems.at[step, number], self.recv_sems.at[step, number], device)

    def make_local(self, step):
        src = self.source(step, self.place.side)
        return pltpu.make_async_copy(src, self.locals[step][1], self.local_sems.at[step])

    def hold(self):
        self.held = []

    def let_go(self):
        held, self.held = self.held, None
        for step, which in held:
            self.ready(step, which)

    def ready(self, step, which):
        if self.held is not None:
            self.held.append((step, which))
            return
        for number, (sends, _, pick, _, _) in enumerate(self.moves[step]):
            if isinstance(pick, int):
                if pick == which:
                    when(sends, self.make(step, number).start)
            else:
                chosen = pick == which
                when(chosen if sends is None else sends & chosen, self.make(step, number).start)
        sends = self.locals[step][0]
        chosen = self.place.side == which
        when(chosen if sends is None else sends & chosen, self.make_local(step).start)

    def sent(self, step):
        for number, (sends, *_) in enumerate(self.moves[step]):
            when(sends, self.make(step, number).wait_send)
        when(self.locals[step][0], self.make_local(step).wait)

    def mail_here(self, step):
        when(self.moves[step][0][1], self.make(step, 0).wait_recv)

    def received(self, step):
        for number, (_, receives, *_) in enumerate(self.moves[step]):
            if step == 4 and number == 0:
                continue
            when(receives, self.make(step, number).wait_recv)


def mega_kernel(
    bucket, inputs, cotangent, qkv_w, attn_w, in_w, out_w,
    padding, down_w, down_b, up_w, up_b, gain, beta, query_b, value_b, attn_b, in_b, out_b,
    outputs, input_grads, full, spill, grad_down_w, grad_down_b, grad_up_w, grad_up_b, grad_gain, grad_beta, ratio,
    attn_v, in_v, out_v, qkv, att, branches, norms, aux, slope, hid, keyb, done, acc, low, dqkv,
    adapters, vecs, grads, meet, parts, total, halves, final,
    z_sem, side_sem, corner_sem, core_sem, own_sem, stage_sem, small_sem, load_sem, row_send, row_recv, row_local, misc_sem,
    part_sem, half_sem,
):
    at = Place()
    length, width = hid.shape[1:]
    chunks = in_v.shape[0]
    cols = [pl.ds(c * width, width) for c in range(chunks)]
    sems = {"z": z_sem, "side": side_sem, "corner": corner_sem, "core": core_sem, "own": own_sem, "stage": stage_sem}
    gather = Gather(full, (qkv.at[1], dqkv), sems, at)
    own = at.section
    shared = 4 + at.side
    early_one = jnp.where(at.early, 1, 0)
    late_one = 1 - early_one
    third_row = jnp.where(at.early, own, shared)
    slot_of = {4: 1 + late_one, 5: late_one, 6: 2 * early_one}
    keys_of = {4: late_one, 5: 0, 6: early_one}
    layer_of = {4: 1, 5: late_one, 6: 0}
    rows = Rows(at, done, norms, slot_of, (outputs, input_grads), hid.at[2], row_send, row_recv, row_local)

    staging = [gather.stage_copies(layer, qkv_w, attn_w, in_w, out_w) for layer in range(2)]
    row_in = pltpu.make_async_copy(inputs.at[own], hid.at[0], misc_sem.at[2])
    row_shared = pltpu.make_async_copy(inputs.at[shared], hid.at[1], misc_sem.at[3])
    cot_third = pltpu.make_async_copy(cotangent.at[third_row], hid.at[0], misc_sem.at[7])
    cot_own = pltpu.make_async_copy(cotangent.at[own], hid.at[1], misc_sem.at[8])
    spills = [pltpu.make_async_copy(slope, spill.at[k], misc_sem.at[9 + k]) for k in range(3)]
    returns = {
        step: pltpu.make_async_copy(spill.at[slot_of[step]], slope, misc_sem.at[7 + step]) for step in (5, 6)
    }
    for copy in staging[0] + staging[1] + [row_in, row_shared]:
        copy.start()
    at.barrier()
    for copy in staging[0]:
        copy.wait()
    gather.begin(0)
    vecs[own] = jnp.zeros(vecs.shape[1:], F32)
    for place, ref in ((1, up_b), (2, gain), (3, beta)):
        vecs[own, place : place + 1] = ref[...]
    vecs[own, 4:5, : down_b.shape[1]] = down_b[...]
    adapters[own, :64] = down_w[0].astype(F32).T.astype(BF16)
    adapters[own, 64:] = up_w[0]
    shares = []
    passes = []
    part_of = pl.ds(pl.multiple_of(64 * at.core, 64), 64)
    for i, (device, whose) in enumerate(((at.to_x, at.x_side), (at.to_y, at.y_side), (at.to_corner, at.corner))):
        ref = adapters.at[own, part_of]
        shares.append(remote(ref, ref, small_sem.at[0, i], small_sem.at[1, i], device))
        ref = adapters.at[whose, part_of]
        passes.append(remote(ref, ref, small_sem.at[0, 6 + i], small_sem.at[1, 6 + i], at.to_core))
    for i, device in enumerate((at.to_x, at.to_y, at.to_corner)):
        shares.append(remote(vecs.at[own], vecs.at[own], small_sem.at[0, 3 + i], small_sem.at[1, 3 + i], device))
    for copy in shares:
        copy.start()
    for copy in staging[1]:
        copy.wait()
    grads[...] = jnp.zeros_like(grads)
    real_rows = jnp.concatenate([padding[...].astype(F32), jnp.zeros((8 - padding.shape[0], length), F32)], 0)
    spot = lanes(length) % 64
    place = lax.broadcasted_iota(jnp.int32, (length, 128), 0)
    for k, row in enumerate((own, shared)):
        chosen = jnp.where(lax.broadcasted_iota(jnp.int32, (8, 128), 0) == row, 1.0, 0.0)
        real = dot_tn(real_rows.astype(BF16), chosen.astype(BF16))
        shift = 6 + bucket[row]
        same = ((spot * SEG) >> shift) == (place >> shift)
        ones = jnp.where((spot >= LOG_TOP) & (spot < LOG_TOP + 3), 1.0, 0.0)
        held = jnp.where(spot < 8, jnp.where(same & (real > 0.5), 0.0, MASKED), jnp.where(spot == 16, real, ones))
        keyb[k] = held.astype(BF16)

    tasks = []
    for name, unit in (
        ("begin", 1), ("spread", 0), ("begin", 2), ("relay", 0),
        ("close", 0),
        ("spread", 1), ("begin", 3),
        ("relay", 1),
        ("spread", 2), ("begin", 4),
        ("close", 1),
        ("relay", 2),
        ("spread", 3), ("begin", 5),
        ("close", 2),
        ("spread", 4),
        ("relay", 3),
        ("close", 3),
        ("spread", 5),
        ("relay", 4),
        ("close", 4),
        ("relay", 5),
        ("close", 5),
    ):
        tasks.append((name, unit))

    def take(count):
        chosen = tasks[:count]
        del tasks[:count]

        def action():
            for name, unit in chosen:
                getattr(gather, name)(unit)

        return action

    def tasks_through(unit):
        if ("close", unit) in tasks:
            take(tasks.index(("close", unit)) + 1)()

    def load(kinds, layer, start=True):
        made = []
        for c in range(chunks):
            for kind in kinds:
                if kind < 2:
                    source, target = full.at[layer, :, c, kind], (attn_v, in_v)[kind].at[c]
                else:
                    span = out_v.shape[1]
                    source, target = full.at[layer, pl.ds(c * span, span), :, kind], out_v.at[c]
                made.append(pltpu.make_async_copy(source, target, load_sem.at[kind, c]))
        if start:
            for copy in made:
                copy.start()

    def loaded_all(kind):
        for c in range(chunks):
            loaded(kind, c)

    def loaded(kind, c):
        source = full.at[0, :, c, kind] if kind < 2 else full.at[0, pl.ds(0, out_v.shape[1]), :, kind]
        target = (attn_v, in_v, out_v)[kind].at[c]
        pltpu.make_async_copy(source, target, load_sem.at[kind, c]).wait()

    def vec(stage, row):
        return vecs[stage, row : row + 1]

    def adapter_part(stage, k, sub, hidden, branch, base, keys, counted):
        down_t = adapters[stage, :64]
        lift = adapters[stage, 64:]
        branch_low = branch.astype(BF16)
        branches[k, sub] = branch_low
        down = dot_nt(branch_low, down_t) + vec(stage, 4)[:, :64]
        act, _ = gelu_both(down)
        lifted = dot(act.astype(BF16), lift) + vec(stage, 1)
        hidden_float = hidden.astype(F32)
        resid = hidden_float + branch + lifted
        center = resid - jnp.mean(resid, -1, keepdims=True)
        inverse = lax.rsqrt(jnp.mean(center * center, -1, keepdims=True) + EPSILON)
        normed = center * inverse
        norms[k, sub] = normed.astype(BF16)
        done[base + sub] = (normed * vec(stage, 2) + vec(stage, 3)).astype(BF16)
        valid = keyb[keys, :, 16:17].astype(F32)
        if counted is not None:
            valid = valid * counted
        grads[stage, 132:133] += jnp.sum(lifted * lifted * valid, 0, keepdims=True)
        grads[stage, 133:134] += jnp.sum(hidden_float * hidden_float * valid, 0, keepdims=True)
        held = aux.at[k, sub]
        held[:, :64] = down
        held[...] = jnp.where(lanes(length) == 64, inverse, held[...])

    def heads(pair, hooks):
        def body(p, carry):
            pair(p)
            for i, hook in enumerate(hooks):
                pl.when(p == i)(hook)
            return carry

        lax.fori_loop(0, HEADS // 2, body, 0)

    def attention_forward(k, layer, hidden, base, keys, hooks, loads=0, counted=None, before_adapter=lambda: None):
        stage = 2 * layer
        if loads == 2:
            loaded_all(0)
        for part in range(3):
            if loads == 1:
                loaded(0, part)
            mixed = dot(hidden[...], square(attn_v, part))
            if part != 1:
                mixed = mixed + (query_b if part == 0 else value_b)[layer : layer + 1]
            qkv[k, :, cols[part]] = mixed.astype(BF16)
        aux[k, 0] = jnp.zeros((length, 128), F32)

        def pair(p):
            attention_pair_forward(p, 0, length, qkv.at[k], keyb.at[keys], att.at[k], aux.at[k, 0])

        heads(pair, hooks)
        if loads == 1:
            loaded(0, 3)
        branch = dot(att[k], square(attn_v, 3)) + attn_b[layer : layer + 1]
        before_adapter()
        adapter_part(stage, k, 0, hidden[...], branch, base, keys, counted)

    def ffn_forward(k, layer, base, keys, hooks, loads=True, counted=None):
        stage = 2 * layer + 1
        if loads:
            loaded_all(1)
            loaded_all(2)
        for c in range(chunks):
            pre = dot(done[base], square(in_v, c)) + in_b[layer : layer + 1, c * width : (c + 1) * width]
            act, steep = gelu_both(pre)
            slope[:, cols[c]] = steep.astype(BF16)
            term = dot(act.astype(BF16), square(out_v, c))
            if c == 0:
                acc[...] = term + out_b[layer : layer + 1]
            else:
                acc[...] += term
            if c < len(hooks):
                hooks[c]()
        aux[k, 1] = jnp.zeros((length, 128), F32)
        adapter_part(stage, k, 1, done[base], acc[...], base, keys, counted)

    def adapter_back(stage, k, sub, grad):
        down_t = adapters[stage, :64]
        lift = adapters[stage, 64:]
        grad = grad.astype(F32)
        normed = norms[k, sub].astype(F32)
        held = aux[k, sub]
        inverse = held[:, 64:65]
        down = held[:, :64]
        scaled = grad * vec(stage, 2)
        resid = inverse * (
            scaled
            - jnp.mean(scaled, -1, keepdims=True)
            - normed * jnp.mean(scaled * normed, -1, keepdims=True)
        )
        lift_grad = resid.astype(BF16)
        act, steep = gelu_both(down)
        down_grad = (dot_nt(lift_grad, lift) * steep).astype(BF16)
        grads[stage, 0:64] += dot_tn(act.astype(BF16), lift_grad)
        grads[stage, 64:128] += dot_tn(down_grad, branches[k, sub])
        grads[stage, 128:129] += jnp.sum(lift_grad.astype(F32), 0, keepdims=True)
        grads[stage, 129:130] += jnp.sum(normed * grad, 0, keepdims=True)
        grads[stage, 130:131] += jnp.sum(grad, 0, keepdims=True)
        grads[stage, 131:132, :64] += jnp.sum(down_grad.astype(F32), 0, keepdims=True)
        acc[...] = resid
        low[...] = (resid + dot(down_grad, down_t)).astype(BF16)

    def ffn_backward(step, source, after_adapter):
        k = slot_of[step]
        layer = layer_of[step]
        adapter_back(2 * layer + 1, k, 1, hid[source])
        after_adapter()
        if step > 4:
            loaded_all(1)
            loaded_all(2)
        for c in range(chunks):
            act_grad = dot_nt(low[...], square(out_v, c))
            pre_grad = (act_grad * slope[:, cols[c]].astype(F32)).astype(BF16)
            acc[...] += dot_nt(pre_grad, square(in_v, c))
        norms[k, 1] = acc[...].astype(BF16)
        rows.ready(step, 1)

    def attention_backward(step, after_adapter, hooks):
        k = slot_of[step]
        keys = keys_of[step]
        layer = layer_of[step]
        adapter_back(2 * layer, k, 0, norms[k, 1])
        after_adapter()
        if step > 4:
            loaded_all(0)
        low[...] = dot_nt(low[...], square(attn_v, 3)).astype(BF16)

        def pair(p):
            attention_pair_backward(p, 0, length, qkv.at[k], keyb.at[keys], att.at[k], aux.at[k, 0], low, dqkv)

        heads(pair, hooks)
        for part in range(3):
            acc[...] += dot_nt(dqkv[:, cols[part]], square(attn_v, part))
        norms[k, 0] = acc[...].astype(BF16)
        rows.ready(step, 0)

    span = GRAD_ROWS // 2
    mine = pl.ds(pl.multiple_of(at.core * span, 8), span)
    theirs = pl.ds(pl.multiple_of((1 - at.core) * span, 8), span)

    def meet_copy(stage):
        return remote(grads.at[stage, theirs], meet.at[stage], half_sem.at[0, stage], half_sem.at[1, stage], at.to_core)

    def met(stage):
        meet_copy(stage).wait()
        grads[stage, mine] += meet[stage]

    def part_copy(slot, stage, device):
        return remote(grads.at[stage, mine], parts.at[slot], part_sem.at[0, slot], part_sem.at[1, slot], device)

    other = 1 - at.side
    upper = [(at.early, 1, 2 + at.side, at.to_y), (at.early, 2, 2 + other, at.to_corner), (at.late, 0, 2 + other, at.to_x)]
    lower = [(at.late, 1, at.side, at.to_y), (at.late, 2, other, at.to_corner), (at.early, 0, other, at.to_x)]

    def meet_upper():
        meet_copy(2).start()
        meet_copy(3).start()

    def send_upper():
        met(2)
        met(3)
        for condition, slot, stage, device in upper:
            pl.when(condition)(part_copy(slot, stage, device).start)

    def send_lower(which):
        met(which)
        for condition, slot, stage, device in lower:
            pl.when(condition & (stage == which))(part_copy(slot, stage, device).start)

    near = (at.section, (at.z + 1 - 2 * (at.z % 2)) * 2 + at.core)
    far = at.to_z(2)
    trades = [
        remote(total, halves.at[0], half_sem.at[0, 4], half_sem.at[1, 4], near),
        remote(total, halves.at[1], half_sem.at[0, 5], half_sem.at[1, 5], far),
        remote(final.at[mine], final.at[mine], half_sem.at[0, 6], half_sem.at[1, 6], at.to_core),
    ]

    def collect():
        for slot in range(3):
            part_copy(slot, 0, at.to_x).wait_recv()
        total[...] = grads[own, mine] + parts[0] + parts[1] + parts[2]
        trades[0].start()

    def fold(number):
        def action():
            trades[number].wait()
            total[...] += halves[number]
            if number < 1:
                trades[1].start()
            else:
                final[mine] = total[...]
                trades[2].start()

        return action

    def nothing():
        pass

    counted = jnp.where(at.early, 1.0, 0.0)
    rows.hold()
    row_in.wait()
    take(4)()
    for copy in shares:
        copy.wait()
    for copy in passes:
        copy.start()
    take(1)()
    gather.arrive(0)
    load((0,), 0)
    take(2)()

    def adapters_here():
        for copy in passes:
            copy.wait()

    attention_forward(0, 0, hid.at[0], 0, 0, [nothing] * 4 + [take(1)], 1, None, adapters_here)
    take(2)()
    rows.ready(0, 0)
    cot_third.start()
    row_shared.wait()
    attention_forward(2, 0, hid.at[1], 2, 1, [take(1), nothing, nothing, nothing, nothing, take(1)], 0, counted)
    rows.ready(1, 0)
    pl.when(at.late)(cot_own.start)
    take(2)()
    gather.arrive(1)
    load((1,), 0)
    take(1)()
    gather.arrive(2)
    load((2,), 0)
    ffn_forward(0, 0, 0, 0, [nothing, take(1), take(1)])
    rows.ready(0, 1)
    spills[0].start()
    spills[0].wait()
    ffn_forward(2, 0, 2, 1, [take(1), take(1), take(1)], False, counted)
    rows.ready(1, 1)
    spills[2].start()
    gather.arrive(3)
    gather.release(0)
    load((0,), 1)
    attention_forward(1, 1, done.at[1], 4, 0, [nothing, nothing, take(1), nothing, nothing, take(1)], 2)
    rows.ready(2, 0)
    gather.arrive(4)
    load((1,), 1)
    last = take(1)

    @pl.when(at.late)
    def _():
        attention_forward(2, 1, done.at[3], 2, 1, [nothing] * 4 + [last])

    pl.when(at.early)(last)
    rows.ready(3, 0)
    rows.let_go()
    gather.arrive(5)
    load((2,), 1)
    spills[2].wait()
    ffn_forward(1, 1, 4, 0, [])
    rows.ready(2, 1)
    spills[1].start()
    spills[1].wait()

    @pl.when(at.late)
    def _():
        ffn_forward(2, 1, 2, 1, [], False)

    rows.ready(3, 1)
    gather.release(1)
    cot_third.wait()
    ffn_backward(4, 0, nothing)
    returns[5].start()
    load((1, 2), layer_of[5])
    attention_backward(4, nothing, [])
    load((0,), layer_of[5])
    pl.when(at.late)(cot_own.wait)

    @pl.when(at.early)
    def _():
        hid[1] = norms[slot_of[4], 0]

    returns[5].wait()
    ffn_backward(5, 1, nothing)
    returns[6].start()
    load((1, 2), 0)
    attention_backward(5, meet_upper, [nothing, nothing, nothing, send_upper])
    load((0,), 0)
    rows.mail_here(4)

    @pl.when(at.late)
    def _():
        hid[2] = norms[slot_of[5], 0]

    returns[6].wait()
    rows.hold()
    ffn_backward(6, 2, meet_copy(1).start)
    send_lower(1)

    def lower_and_rows():
        send_lower(0)
        rows.let_go()

    attention_backward(6, meet_copy(0).start, [nothing, lower_and_rows])
    collect()
    for unit in range(3):
        gather.drain(unit)
    fold(0)()
    for unit in range(3, 6):
        gather.drain(unit)
    fold(1)()
    trades[2].wait()
    grad_down_w[0] = final[64:128].T
    grad_down_b[...] = final[131:132, : down_b.shape[1]]
    grad_up_w[0] = final[0:64]
    for out, line in ((grad_up_b, 128), (grad_gain, 129), (grad_beta, 130)):
        out[...] = final[line : line + 1]
    squares = jnp.sum(final[132:134], -1, keepdims=True)
    ratio[...] = jnp.sqrt(squares[0:1] / squares[1:2])
    for slot in range(3):
        part_copy(slot, 0, at.to_x).wait_send()
    for step in range(7):
        rows.sent(step)
        rows.received(step)


def everything(bucket, inputs, cotangent, weights, small):
    length, width = inputs.shape[1:]
    shard_rows = weights[0].shape[1]
    shards = lax.axis_size("dp")
    count = shards // 2
    ffn = weights[2].shape[2]
    half = GRAD_ROWS // 2
    anyspec = pl.BlockSpec(memory_space=pl.ANY)
    vmem = pl.BlockSpec(memory_space=pltpu.VMEM)
    dma = pltpu.SemaphoreType.DMA
    row = (length, width)
    scratch = [
        pltpu.VMEM((4, shards, shard_rows, width), BF16),
        pltpu.VMEM((4, shards, shard_rows, width), BF16),
        pltpu.VMEM((4, shards // 4, 4, shard_rows, width), BF16),
        pltpu.VMEM((3, length, 3 * width), BF16),
        pltpu.VMEM((3,) + row, BF16),
        pltpu.VMEM((3, 2) + row, BF16),
        pltpu.VMEM((3, 2) + row, BF16),
        pltpu.VMEM((3, 2, length, 128), F32),
        pltpu.VMEM((length, ffn), BF16),
        pltpu.VMEM((3,) + row, BF16),
        pltpu.VMEM((2, length, 128), BF16),
        pltpu.VMEM((6,) + row, BF16),
        pltpu.VMEM(row, F32),
        pltpu.VMEM(row, BF16),
        pltpu.VMEM((length, 3 * width), BF16),
        pltpu.VMEM((4, 128, width), BF16),
        pltpu.VMEM((4, 8, width), F32),
        pltpu.VMEM((4, GRAD_ROWS, width), F32),
        pltpu.VMEM((4, half, width), F32),
        pltpu.VMEM((3, half, width), F32),
        pltpu.VMEM((half, width), F32),
        pltpu.VMEM((2, half, width), F32),
        pltpu.VMEM((GRAD_ROWS, width), F32),
        dma((2, 6, count - 1)),
        dma((2, 6, count - 1, 2)),
        dma((2, 6, count - 1, 2)),
        dma((2, 6, count, 4)),
        dma((6, 4)),
        dma((2, 8)),
        dma((2, 9)),
        dma((3, 4)),
        dma((7, 4)),
        dma((7, 4)),
        dma((7,)),
        dma((14,)),
        dma((2, 3)),
        dma((2, 7)),
    ]
    outs = [
        (inputs.shape, BF16), (inputs.shape, BF16), ((2, shards, 4, 3, shard_rows, width), BF16),
        ((3, length, ffn), BF16), ((1, width, 64), F32), ((1, 64), F32), ((1, 64, width), F32), ((1, width), F32),
        ((1, width), F32), ((1, width), F32), ((1, 1), F32),
    ]
    return pl.pallas_call(
        mega_kernel,
        in_specs=[pl.BlockSpec(memory_space=pltpu.SMEM)] + [anyspec] * 6 + [vmem] * len(small),
        out_specs=[anyspec] * 4 + [vmem] * 7,
        out_shape=[jax.ShapeDtypeStruct(shape, dtype) for shape, dtype in outs],
        scratch_shapes=scratch,
        compiler_params=pltpu.CompilerParams(
            collective_id=1, has_side_effects=True, vmem_limit_bytes=MEGA_BYTES
        ),
        cost_estimate=pl.CostEstimate(flops=90_000_000_000, bytes_accessed=200_000_000, transcendentals=0),
        name="everything",
    )(bucket, inputs, cotangent, *weights, *small)


X_PAIRS = [(0, 1), (1, 0), (2, 3), (3, 2)]
Y_PAIRS = [(0, 2), (2, 0), (1, 3), (3, 1)]
CROSS = [(0, 3), (3, 0), (1, 2), (2, 1)]


def send(value, pairs, senders=(0, 1, 2, 3)):
    return lax.ppermute(value, "section", [pair for pair in pairs if pair[0] in senders])


def gather_weights(shards):
    section = lax.axis_index("section")
    quarter = lax.dynamic_index_in_dim(shards, section, 0, keepdims=False)
    full = lax.all_gather(quarter, ("dp", "section"), axis=0, tiled=False)
    count = lax.axis_size("dp")
    full = full.reshape((count, lax.axis_size("section")) + quarter.shape)
    return full


def in_quarters(matrix):
    rows, columns = matrix.shape
    return matrix.reshape(rows, 4, columns // 4).transpose(1, 0, 2)


def block_rows(full, kind, by_rows):
    if full.shape[3] % 16 == 0:
        return (full, kind)
    count, quarters, _, rows, width = full.shape
    one = full[:, :, kind]
    if by_rows:
        return (one.reshape(count * rows * quarters // width, quarters, 1, width // quarters, width), 0)
    return (one.transpose(1, 0, 2, 3).reshape(1, quarters, 1, count * rows, width), 0)


def on_device(
    inputs, bucket, padding, cotangent, down_weight, down_bias, up_weight, up_bias, ln_gain, ln_beta, qkv_weight,
    query_bias, value_bias, attn_out_weight, attn_out_bias, ffn_in_weight, ffn_in_bias, ffn_out_weight, ffn_out_bias,
):
    section = lax.axis_index("section")
    early = section < 2
    side = section % 2
    width = inputs.shape[2]
    adapter_width = down_weight.shape[2]
    layers = qkv_weight.shape[0]

    def layer_shards(layer):
        attn = jnp.concatenate([qkv_weight[layer], attn_out_weight[layer]], 1)
        outer = ffn_out_weight[layer]
        return (
            in_quarters(attn)[:, None],
            jnp.stack([in_quarters(ffn_in_weight[layer]), outer.reshape((4, -1) + outer.shape[1:])], 1),
        )

    def results(outputs, input_grads, total):
        ratios = jnp.sqrt(jnp.sum(total[132]) / jnp.sum(total[133]))[None]
        return (
            outputs[None],
            input_grads[None],
            total[64:128].T[None],
            total[131, :adapter_width][None],
            total[0:64][None],
            total[128][None],
            total[129][None],
            total[130][None],
            ratios,
        )

    if lax.axis_size("dp") == 8 and lax.axis_size("section") == 4 and inputs.shape[0] == 6:
        found = everything(
            bucket, inputs, cotangent, (qkv_weight, attn_out_weight, ffn_in_weight, ffn_out_weight),
            (
                padding, down_weight, down_bias, up_weight, up_bias, ln_gain, ln_beta, query_bias, value_bias,
                attn_out_bias, ffn_in_bias, ffn_out_bias,
            ),
        )
        return (found[0][None], found[1][None]) + tuple(found[4:10]) + (found[10][0],)

    zero_row = jnp.zeros((1, width), F32)
    own_vec = jnp.concatenate(
        [zero_row, up_bias, ln_gain, ln_beta, jnp.pad(down_bias, ((0, 0), (0, width - adapter_width))), zero_row, zero_row, zero_row], 0
    )
    own_adapter = jnp.concatenate([down_weight[0].T, up_weight[0]], 0)
    biases = jnp.zeros((layers, 2, 8, width), F32)
    biases = biases.at[:, 0, 0].set(attn_out_bias).at[:, 0, 5].set(query_bias).at[:, 0, 6].set(value_bias)
    biases = biases.at[:, 1, 0].set(ffn_out_bias)
    in_bias = ffn_in_bias[:, None, :]
    table = key_table(bucket, padding)

    weights = []
    for layer in range(layers):
        full = gather_weights(jnp.concatenate(layer_shards(layer), 1))
        weights.append([block_rows(full, 0, False), block_rows(full, 1, False), block_rows(full, 2, True)])
    adapters = lax.all_gather(own_adapter, "section", axis=0, tiled=False)
    vecs = lax.all_gather(own_vec, "section", axis=0, tiled=False)
    adapters = adapters.reshape(layers, 2, 128, width)
    vecs = vecs.reshape(layers, 2, 8, width)
    vecs = (vecs + biases).reshape(layers, 16, width)
    own = section
    shared = 4 + side

    def row_of(array, row):
        return lax.dynamic_index_in_dim(array, row, 0, keepdims=False)

    def forward(row, hidden, layer, weights_used, choice):
        return forward_pair(
            layer, choice, row_of(bucket, row), hidden, row_of(table, row), weights_used, adapters, vecs, in_bias
        )

    def backward(row, grad, saved, layer, weights_used, choice):
        return backward_pair(
            layer, choice, row_of(bucket, row), grad, row_of(table, row), saved, weights_used, adapters, vecs
        )

    zero = jnp.int32(0)
    one = jnp.int32(1)
    late = 1 - early.astype(jnp.int32)
    first_row = jnp.where(early, shared, own)
    third_row = jnp.where(early, own, shared)

    f0 = forward(first_row, row_of(inputs, first_row), zero, weights[:1], zero)
    x0 = send(jnp.where(side == 0, f0[1], f0[0]), X_PAIRS, (0, 1))
    y0 = send(jnp.where(early | (side == 1), f0[1], f0[0]), Y_PAIRS)
    z0 = send(jnp.where(side == 0, f0[1], f0[0]), CROSS, (2, 3))
    hidden = jnp.where(early, row_of(inputs, own), f0[1])
    f1 = forward(own, hidden, late, weights, late)
    x1 = send(jnp.where(side == 0, f1[1], f1[0]), X_PAIRS)
    hidden = jnp.where(early, f1[1], y0)
    f2 = forward(third_row, hidden, one, weights[1:], zero)
    x2 = send(jnp.where(side == 0, f2[1], f2[0]), X_PAIRS, (2, 3))
    y2 = send(jnp.where(side == 1, f2[1], f2[0]), Y_PAIRS, (0, 1))
    z2 = send(jnp.where(side == 0, f2[1], f2[0]), CROSS, (0, 1))

    b3 = backward(third_row, row_of(cotangent, third_row), f2[2:11], one, weights[1:], zero)
    x3 = send(jnp.where(side == 0, b3[0], b3[1]), X_PAIRS, (2, 3))
    y3 = send(jnp.where(early & (side == 1), b3[0], b3[1]), Y_PAIRS)
    z3 = send(jnp.where(side == 0, b3[0], b3[1]), CROSS, (0, 1))
    grad = jnp.where(early, b3[1], row_of(cotangent, own))
    b4 = backward(own, grad, f1[2:11], late, weights, late)
    x4 = send(jnp.where(side == 0, b4[0], b4[1]), X_PAIRS)
    grad = jnp.where(early, y3, b4[1])
    b5 = backward(first_row, grad, f0[2:11], zero, weights[:1], zero)
    x5 = send(jnp.where(side == 0, b5[0], b5[1]), X_PAIRS, (0, 1))
    y5 = send(jnp.where(side == 1, b5[0], b5[1]), Y_PAIRS, (2, 3))
    z5 = send(jnp.where(side == 0, b5[0], b5[1]), CROSS, (2, 3))

    def assemble(parts):
        result = jnp.zeros(inputs.shape, BF16)
        for row, part in parts:
            result = lax.dynamic_update_index_in_dim(result, part, row, 0)
        return result

    other = section + 1 - 2 * side
    across = jnp.where(early, section + 2, section - 2)
    corner = 3 - section
    other_shared = 4 + 1 - side
    outputs = assemble(
        [
            (own, jnp.where(side == 0, f1[0], f1[1])),
            (other, x1),
            (across, jnp.where(early, y0, y2)),
            (corner, jnp.where(early, z0, z2)),
            (shared, jnp.where(early, jnp.where(side == 0, f0[0], f0[1]), jnp.where(side == 0, f2[0], f2[1]))),
            (other_shared, jnp.where(early, x0, x2)),
        ]
    )
    input_grads = assemble(
        [
            (own, jnp.where(side == 0, b4[1], b4[0])),
            (other, x4),
            (across, jnp.where(early, y5, y3)),
            (corner, jnp.where(early, z5, z3)),
            (shared, jnp.where(early, jnp.where(side == 0, b5[1], b5[0]), jnp.where(side == 0, b3[1], b3[0]))),
            (other_shared, jnp.where(early, x5, x3)),
        ]
    )

    def with_sums(grads, sums):
        return grads.at[:, 132:134].set(sums[:4].reshape(2, 2, width))

    g3, g4, g5 = with_sums(b3[2], f2[11]), with_sums(b4[2], f1[11]), with_sums(b5[2], f0[11])
    low_layer = g5 + jnp.where(early, g4, 0.0)
    high_layer = g3 + jnp.where(early, 0.0, g4)
    mine = lax.psum_scatter(jnp.concatenate([low_layer, high_layer], 0), "section", scatter_dimension=0, tiled=False)
    return results(outputs, input_grads, lax.psum(mine, "dp"))


def solution(mesh):
    in_specs = (
        P("dp", None, None),
        P("dp"),
        P("dp", None),
        P("dp", None, None),
        P("section", None, None),
        P("section", None),
        P("section", None, None),
        P("section", None),
        P("section", None),
        P("section", None),
        P(None, "dp", None),
        P(),
        P(),
        P(None, "dp", None),
        P(),
        P(None, "dp", None),
        P(),
        P(None, "dp", None),
        P(),
    )
    out_specs = (
        P("section", "dp", None, None),
        P("section", "dp", None, None),
        P("section", None, None),
        P("section", None),
        P("section", None, None),
        P("section", None),
        P("section", None),
        P("section", None),
        P("section"),
    )
    return jax.shard_map(
        on_device, mesh=mesh, in_specs=in_specs, out_specs=out_specs, check_vma=False
    )
```

```python
import functools
import jax
import jax.numpy as jnp
from jax import lax
from jax.experimental import pallas as pl
from jax.experimental.pallas import tpu as pltpu
from jax.sharding import PartitionSpec as P

HEADS = 12
HD = 64
SEG = 64
EPSILON = 1e-05
MASKED = -1e30
LOG_TOP = 24
VMEM_BYTES = 56 * 1024 * 1024
F32 = jnp.float32
BF16 = jnp.bfloat16


def dot(left, right):
    return jnp.dot(left, right, preferred_element_type=F32)


def dot_nt(left, right):
    return lax.dot_general(left, right, (((1,), (1,)), ((), ())), preferred_element_type=F32)


def dot_tn(left, right):
    return lax.dot_general(left, right, (((0,), (0,)), ((), ())), preferred_element_type=F32)


def gelu_both(v):
    size = jnp.abs(v)
    bell = jnp.exp(v * v * -0.5)
    below = 1.0 + size * (0.3275911 * 0.7071067811865476)
    t = pl.reciprocal(below, approx=True)
    t = t * (2.0 - below * t)
    tail = t * (
        0.127414796
        + t * (-0.142248368 + t * (0.7107068705 + t * (-0.7265760135 + t * 0.5307027145)))
    )
    tail = tail * bell
    cdf = jnp.where(v >= 0, 1.0 - tail, tail)
    return (jnp.maximum(v, 0.0) - size * tail, cdf + v * (bell * 0.3989422804014327))


def lanes(rows):
    return lax.broadcasted_iota(jnp.int32, (rows, 128), 1)


def adapter_forward(hidden, branch, adapter_ref, vec_ref, base, stage, aux, valid):
    down_t = adapter_ref[0, stage, :64]
    lift = adapter_ref[0, stage, 64:]
    branch_low = branch.astype(BF16)
    down = dot_nt(branch_low, down_t) + vec_ref[0, base + 4 : base + 5, :64]
    act, _ = gelu_both(down)
    lifted = dot(act.astype(BF16), lift) + vec_ref[0, base + 1 : base + 2]
    hidden_float = hidden.astype(F32)
    resid = hidden_float + branch + lifted
    mean = jnp.mean(resid, -1, keepdims=True)
    center = resid - mean
    inverse = lax.rsqrt(jnp.mean(center * center, -1, keepdims=True) + EPSILON)
    normed = center * inverse
    output = (normed * vec_ref[0, base + 2 : base + 3] + vec_ref[0, base + 3 : base + 4]).astype(BF16)
    sums = (
        jnp.sum(lifted * lifted * valid, 0, keepdims=True),
        jnp.sum(hidden_float * hidden_float * valid, 0, keepdims=True),
    )
    return branch_low, down, output, normed.astype(BF16), inverse, sums


def column_copies(weight, kind, chunk, held, sem):
    return pltpu.make_async_copy(weight.at[:, chunk, kind], held.at[chunk], sem)


def row_copies(weight, kind, chunk, held, sem):
    span = held.shape[1]
    return pltpu.make_async_copy(weight.at[pl.ds(chunk * span, span), :, kind], held.at[chunk], sem)


def start_copies(choice, sources, order, sems):
    made = []
    for which, source in enumerate(sources):
        copies = [make(source[matrix][0], source[matrix][1], chunk, held, sems.at[i])
                  for i, (make, matrix, chunk, held) in enumerate(order)]
        made.append(copies)

        @pl.when(choice == which)
        def _():
            for copy in copies:
                copy.start()

    return made[0]


def square(held, chunk):
    width = held.shape[-1]
    return held[chunk].reshape(width, width)


def attention_pair_forward(p, start, size, qkv, keyb, att, aux):
    rows = pl.ds(start, size)
    width = att.shape[1]
    col = pl.multiple_of(p * 128, 128)
    lane = lanes(size)
    query = qkv[rows, pl.ds(col, 128)]
    key = qkv[rows, pl.ds(width + col, 128)]
    value = qkv[rows, pl.ds(2 * width + col, 128)]
    bias = keyb[rows]
    place = start + lax.broadcasted_iota(jnp.int32, (size, 128), 0)
    hot = jnp.where(lane % 64 == place // SEG, 1.0, 0.0).astype(BF16)
    query = query * jnp.asarray(HD ** -0.5, BF16)
    total = None
    for half in range(2):
        mine = (lane < 64) if half == 0 else (lane >= 64)
        scores = dot_nt(jnp.where(mine, query, hot), jnp.where(mine, key, bias))
        peak = jnp.max(scores, -1, keepdims=True)
        expo = jnp.exp(scores - peak)
        norm = jnp.sum(expo, -1, keepdims=True)
        part = dot(expo.astype(BF16), jnp.where(mine, value, jnp.zeros_like(value))) * (1.0 / norm)
        log_total = peak + jnp.log(norm)
        aux[rows] = jnp.where(lane == 80 + 2 * p + half, log_total, aux[rows])
        total = part if total is None else total + part
    att[rows, pl.ds(col, 128)] = total.astype(BF16)


def forward_kernel(
    sources, idx, hidden_ref, keyb_ref, adapter_ref, vec_ref, in_bias_ref,
    h1_ref, h2_ref, qkv_ref, att_ref, br1_ref, nh1_ref, aux1_ref, slope_ref, br2_ref, nh2_ref, aux2_ref, sums_ref,
    attn_v, in_v, out_v, acc, sems,
):
    bucket = idx[1]
    length, width = hidden_ref.shape
    chunks = in_v.shape[0]
    cols = [pl.ds(c * width, width) for c in range(chunks)]
    order = [(column_copies, 0, c, attn_v) for c in range(4)]
    for c in range(chunks):
        order.append((column_copies, 1, c, in_v))
        order.append((row_copies, 2, c, out_v))
    copies = start_copies(idx[2], sources, order, sems)
    hidden = hidden_ref[...]
    valid = keyb_ref[:, 16:17].astype(F32)
    for part in range(3):
        copies[part].wait()
        mixed = dot(hidden, square(attn_v, part))
        if part == 0:
            mixed = mixed + vec_ref[0, 5:6]
        if part == 2:
            mixed = mixed + vec_ref[0, 6:7]
        qkv_ref[:, cols[part]] = mixed.astype(BF16)
    aux1_ref[...] = jnp.zeros_like(aux1_ref)

    def heads(size):
        blocks = length // size

        def body(step, carry):
            p = step // blocks
            start = pl.multiple_of((step % blocks) * size, size)
            attention_pair_forward(p, start, size, qkv_ref, keyb_ref, att_ref, aux1_ref)
            return carry

        lax.fori_loop(0, (HEADS // 2) * blocks, body, 0)

    @pl.when(bucket >= 3)
    def _():
        heads(length)

    @pl.when(bucket < 3)
    def _():
        heads(length // 2)

    copies[3].wait()
    branch = dot(att_ref[...], square(attn_v, 3)) + vec_ref[0, 0:1]
    branch_low, down, output, normed, inverse, sums = adapter_forward(
        hidden, branch, adapter_ref, vec_ref, 0, 0, None, valid
    )
    br1_ref[...] = branch_low
    nh1_ref[...] = normed
    h1_ref[...] = output
    lane = lanes(length)
    aux1_ref[:, :64] = down
    aux1_ref[...] = jnp.where(lane == 64, inverse, aux1_ref[...])
    sums_ref[0:1] = sums[0]
    sums_ref[1:2] = sums[1]
    hidden = h1_ref[...]
    for c in range(chunks):
        copies[4 + 2 * c].wait()
        pre = dot(hidden, square(in_v, c)) + in_bias_ref[0, :, c * width : (c + 1) * width]
        act, slope = gelu_both(pre)
        slope_ref[:, cols[c]] = slope.astype(BF16)
        copies[5 + 2 * c].wait()
        term = dot(act.astype(BF16), square(out_v, c))
        if c == 0:
            acc[...] = term + vec_ref[0, 8:9]
        else:
            acc[...] += term
    branch_low, down, output, normed, inverse, sums = adapter_forward(
        hidden, acc[...], adapter_ref, vec_ref, 8, 1, None, valid
    )
    br2_ref[...] = branch_low
    nh2_ref[...] = normed
    h2_ref[...] = output
    aux2_ref[...] = jnp.where(lane == 64, inverse, jnp.zeros((length, 128), F32))
    aux2_ref[:, :64] = down
    sums_ref[2:3] = sums[0]
    sums_ref[3:4] = sums[1]
    sums_ref[4:8] = jnp.zeros_like(sums_ref[4:8])


def weight_plan(weights):
    arrays, places = [], []
    for layer in weights:
        spots = []
        for array, kind in layer:
            found = [i for i, other in enumerate(arrays) if other is array]
            if not found:
                arrays.append(array)
                found = [len(arrays) - 1]
            spots.append((found[0], kind))
        places.append(spots)
    return arrays, places


def weight_scratch(weights):
    attn, inner, outer = [array.shape for array, _ in weights[0]]
    width = attn[-1]
    span = width // (4 * outer[3])
    return [
        pltpu.VMEM((4, attn[0], attn[3], width), BF16),
        pltpu.VMEM((4, inner[0], inner[3], width), BF16),
        pltpu.VMEM((outer[0] // span, span, 4, outer[3], width), BF16),
    ]


def whole(shape):
    return pl.BlockSpec(shape, lambda i, s: (0,) * len(shape))


def by_layer(shape):
    return pl.BlockSpec((1,) + shape, lambda i, s: (s[0],) + (0,) * len(shape))


def call_with_weights(kernel, weights, blocks, outs, scratch, flops, name):
    arrays, places = weight_plan(weights)
    fixed = len(blocks)
    idx, rest = blocks[0], blocks[1:]

    def body(*refs):
        held = refs[fixed : fixed + len(arrays)]
        sources = [[(held[i], kind) for i, kind in spots] for spots in places]
        kernel(sources, *refs[:fixed], *refs[fixed + len(arrays) :])

    copies = 12
    return pl.pallas_call(
        body,
        grid_spec=pltpu.PrefetchScalarGridSpec(
            num_scalar_prefetch=1,
            grid=(1,),
            in_specs=[spec for _, spec in rest] + [pl.BlockSpec(memory_space=pl.ANY)] * len(arrays),
            out_specs=[whole(shape) for shape, _ in outs],
            scratch_shapes=weight_scratch(weights) + scratch + [pltpu.SemaphoreType.DMA((copies,))],
        ),
        out_shape=[jax.ShapeDtypeStruct(shape, dtype) for shape, dtype in outs],
        compiler_params=pltpu.CompilerParams(vmem_limit_bytes=VMEM_BYTES),
        cost_estimate=pl.CostEstimate(flops=flops, bytes_accessed=24_000_000, transcendentals=0),
        name=name,
    )(idx, *[array for array, _ in rest], *arrays)


def forward_pair(layer, choice, bucket, hidden, keyb, weights, adapters, vecs, in_bias):
    length, width = hidden.shape
    ffn = in_bias.shape[-1]
    idx = jnp.stack([layer, bucket, choice]).astype(jnp.int32)
    outs = [
        ((length, width), BF16), ((length, width), BF16), ((length, 3 * width), BF16), ((length, width), BF16),
        ((length, width), BF16), ((length, width), BF16), ((length, 128), F32), ((length, ffn), BF16),
        ((length, width), BF16), ((length, width), BF16), ((length, 128), F32), ((8, width), F32),
    ]
    blocks = [
        idx, (hidden, whole((length, width))), (keyb, whole((length, 128))), (adapters, by_layer((2, 128, width))),
        (vecs, by_layer((16, width))), (in_bias, by_layer((1, ffn))),
    ]
    scratch = [pltpu.VMEM((length, width), F32)]
    return call_with_weights(forward_kernel, weights, blocks, outs, scratch, 12_000_000_000, "forward_pair")


def adapter_backward(grad, normed, branch_low, aux, adapter_ref, vec_ref, base, stage, grads_ref):
    down_t = adapter_ref[0, stage, :64]
    lift = adapter_ref[0, stage, 64:]
    grad = grad.astype(F32)
    normed = normed.astype(F32)
    inverse = aux[:, 64:65]
    down = aux[:, :64]
    scaled = grad * vec_ref[0, base + 2 : base + 3]
    resid = inverse * (
        scaled
        - jnp.mean(scaled, -1, keepdims=True)
        - normed * jnp.mean(scaled * normed, -1, keepdims=True)
    )
    lift_grad = resid.astype(BF16)
    act, slope = gelu_both(down)
    down_grad = (dot_nt(lift_grad, lift) * slope).astype(BF16)
    grads_ref[stage, 0:64] = dot_tn(act.astype(BF16), lift_grad)
    grads_ref[stage, 64:128] = dot_tn(down_grad, branch_low)
    grads_ref[stage, 128:136] = jnp.zeros_like(grads_ref[stage, 128:136])
    grads_ref[stage, 128:129] = jnp.sum(lift_grad.astype(F32), 0, keepdims=True)
    grads_ref[stage, 129:130] = jnp.sum(normed * grad, 0, keepdims=True)
    grads_ref[stage, 130:131] = jnp.sum(grad, 0, keepdims=True)
    grads_ref[stage, 131:132, :64] = jnp.sum(down_grad.astype(F32), 0, keepdims=True)
    branch_grad = (resid + dot(down_grad, down_t)).astype(BF16)
    return resid, branch_grad


def split_low(column):
    high = column.astype(BF16).astype(F32)
    rest = column - high
    middle = rest.astype(BF16).astype(F32)
    return high, middle, rest - middle


def attention_pair_backward(p, start, size, qkv, keyb, att, aux, att_grad, dqkv):
    rows = pl.ds(start, size)
    width = att.shape[1]
    col = pl.multiple_of(p * 128, 128)
    lane = lanes(size)
    query = qkv[rows, pl.ds(col, 128)] * jnp.asarray(HD ** -0.5, BF16)
    key = qkv[rows, pl.ds(width + col, 128)]
    value = qkv[rows, pl.ds(2 * width + col, 128)]
    grad = att_grad[rows, pl.ds(col, 128)]
    product = grad.astype(F32) * att[rows, pl.ds(col, 128)].astype(F32)
    bias = keyb[rows]
    place = start + lax.broadcasted_iota(jnp.int32, (size, 128), 0)
    spot = lane % 64
    hot = jnp.where(spot == place // SEG, 1.0, 0.0)
    aux_rows = aux[rows]
    zero = jnp.zeros((size, 128), BF16)
    query_t = query.astype(F32).T.astype(BF16)
    grad_t = grad.astype(F32).T.astype(BF16)
    query_grad = None
    key_grads = []
    value_grads = []
    for half in range(2):
        mine = (lane < 64) if half == 0 else (lane >= 64)
        log_total = jnp.sum(jnp.where(lane == 80 + 2 * p + half, aux_rows, 0.0), -1, keepdims=True)
        parts = split_low(-log_total)
        extra = jnp.where(spot == LOG_TOP, parts[0], jnp.where(spot == LOG_TOP + 1, parts[1], jnp.where(spot == LOG_TOP + 2, parts[2], hot)))
        row_dot = jnp.sum(jnp.where(mine, product, 0.0), -1, keepdims=True)
        dots = split_low(-row_dot)
        extra_grad = jnp.where(spot == LOG_TOP, dots[0], jnp.where(spot == LOG_TOP + 1, dots[1], jnp.where(spot == LOG_TOP + 2, dots[2], 0.0)))
        key_side = jnp.where(mine, key, bias)
        value_side = jnp.where(mine, value, bias)
        probs = jnp.exp(dot_nt(jnp.where(mine, query, extra.astype(BF16)), key_side))
        centred = dot_nt(jnp.where(mine, grad, extra_grad.astype(BF16)), value_side)
        score_grad = (probs * centred).astype(BF16)
        term = dot(score_grad, jnp.where(mine, key, zero))
        query_grad = term if query_grad is None else query_grad + term
        part = slice(64 * half, 64 * half + 64)
        key_grads.append(dot(query_t[part], score_grad))
        value_grads.append(dot(grad_t[part], probs.astype(BF16)))
    dqkv[rows, pl.ds(col, 128)] = (query_grad * HD ** -0.5).astype(BF16)
    dqkv[rows, pl.ds(width + col, 128)] = jnp.concatenate(key_grads, 0).T.astype(BF16)
    dqkv[rows, pl.ds(2 * width + col, 128)] = jnp.concatenate(value_grads, 0).T.astype(BF16)


def backward_kernel(
    sources, idx, grad_ref, keyb_ref, qkv_ref, att_ref, br1_ref, nh1_ref, aux1_ref, slope_ref, br2_ref, nh2_ref,
    aux2_ref, adapter_ref, vec_ref,
    g2_ref, g1_ref, grads_ref,
    attn_v, in_v, out_v, acc, low, dqkv, sems,
):
    bucket = idx[1]
    length, width = grad_ref.shape
    chunks = in_v.shape[0]
    cols = [pl.ds(c * width, width) for c in range(chunks)]
    order = []
    for c in range(chunks):
        order.append((row_copies, 2, c, out_v))
        order.append((column_copies, 1, c, in_v))
    order += [(column_copies, 0, c, attn_v) for c in (3, 0, 1, 2)]
    copies = start_copies(idx[2], sources, order, sems)
    resid, branch_grad = adapter_backward(
        grad_ref[...], nh2_ref[...], br2_ref[...], aux2_ref[...], adapter_ref, vec_ref, 8, 1, grads_ref
    )
    acc[...] = resid
    low[...] = branch_grad
    for c in range(chunks):
        copies[2 * c].wait()
        act_grad = dot_nt(low[...], square(out_v, c))
        pre_grad = (act_grad * slope_ref[:, cols[c]].astype(F32)).astype(BF16)
        copies[2 * c + 1].wait()
        acc[...] += dot_nt(pre_grad, square(in_v, c))
    g2_ref[...] = acc[...].astype(BF16)
    resid, branch_grad = adapter_backward(
        g2_ref[...], nh1_ref[...], br1_ref[...], aux1_ref[...], adapter_ref, vec_ref, 0, 0, grads_ref
    )
    acc[...] = resid
    copies[2 * chunks].wait()
    low[...] = dot_nt(branch_grad, square(attn_v, 3)).astype(BF16)

    def heads(size):
        blocks = length // size

        def body(step, carry):
            p = step // blocks
            start = pl.multiple_of((step % blocks) * size, size)
            attention_pair_backward(p, start, size, qkv_ref, keyb_ref, att_ref, aux1_ref, low, dqkv)
            return carry

        lax.fori_loop(0, (HEADS // 2) * blocks, body, 0)

    @pl.when(bucket >= 3)
    def _():
        heads(length)

    @pl.when(bucket < 3)
    def _():
        heads(length // 2)

    for part in range(3):
        copies[2 * chunks + 1 + part].wait()
        acc[...] += dot_nt(dqkv[:, cols[part]], square(attn_v, part))
    g1_ref[...] = acc[...].astype(BF16)


def backward_pair(layer, choice, bucket, grad, keyb, saved, weights, adapters, vecs):
    length, width = grad.shape
    idx = jnp.stack([layer, bucket, choice]).astype(jnp.int32)
    outs = [((length, width), BF16), ((length, width), BF16), ((2, 136, width), F32)]
    blocks = [idx, (grad, whole((length, width))), (keyb, whole((length, 128)))]
    blocks += [(member, whole(member.shape)) for member in saved]
    blocks += [(adapters, by_layer((2, 128, width))), (vecs, by_layer((16, width)))]
    scratch = [
        pltpu.VMEM((length, width), F32),
        pltpu.VMEM((length, width), BF16),
        pltpu.VMEM((length, 3 * width), BF16),
    ]
    return call_with_weights(backward_kernel, weights, blocks, outs, scratch, 16_000_000_000, "backward_pair")


def key_table(bucket, padding):
    rows, length = padding.shape
    spot = jnp.arange(128, dtype=jnp.int32) % 64
    shift = 6 + bucket[:, None, None]
    place = jnp.arange(length, dtype=jnp.int32)
    same = (spot[None, None, :] * SEG) >> shift == place[None, :, None] >> shift
    real = (padding == 1)[:, :, None]
    table = jnp.where(same & real, 0.0, MASKED)
    ones = (spot >= LOG_TOP) & (spot < LOG_TOP + 3)
    table = jnp.where(spot < 8, table, jnp.where(spot == 16, real.astype(F32), jnp.where(ones, 1.0, 0.0)))
    return table.astype(BF16)


MESH = pl.DeviceIdType.MESH
GRAD_ROWS = 160
MEET = (0, 2, 0, 1)
MEGA_BYTES = 63 * 1024 * 1024


def when(condition, action):
    if condition is None:
        action()
    else:
        pl.when(condition)(action)


class Place:
    def __init__(self):
        self.section = lax.axis_index("section")
        self.dp = lax.axis_index("dp")
        self.count = lax.axis_size("dp") // 2
        self.z = self.dp // 2
        self.core = self.dp % 2
        self.side = self.section % 2
        self.early = self.section < 2
        self.late = self.section >= 2
        self.x_side = self.section + 1 - 2 * self.side
        self.y_side = lax.rem(self.section + 2, 4)
        self.corner = 3 - self.section
        self.to_x = (self.x_side, self.dp)
        self.to_y = (self.y_side, self.dp)
        self.to_corner = (self.corner, self.dp)
        self.to_core = (self.section, self.dp + 1 - 2 * self.core)

    def to_z(self, step):
        return (self.section, lax.rem(self.z + step, self.count) * 2 + self.core)

    def from_z(self, step):
        return lax.rem(self.z + self.count - step, self.count) * 2 + self.core

    def peers(self):
        return [self.to_z(d) for d in range(1, self.count)] + [self.to_x, self.to_y, self.to_corner, self.to_core]

    def barrier(self):
        entry = pltpu.get_barrier_semaphore()
        for peer in self.peers():
            pl.semaphore_signal(entry, inc=1, device_id=peer, device_id_type=MESH)
        pl.semaphore_wait(entry, len(self.peers()))


def remote(src, dst, send_sem, recv_sem, device):
    return pltpu.make_async_remote_copy(
        src_ref=src, dst_ref=dst, send_sem=send_sem, recv_sem=recv_sem, device_id=device, device_id_type=MESH
    )


class Gather:
    def __init__(self, full, stage, sems, place):
        self.full = full
        self.stage = stage
        self.sems = sems
        self.place = place
        self.steps = range(1, place.count)

    def staged(self, unit, quarter):
        rows, width = self.full.shape[4:]
        kind = unit % 3
        last = quarter // 3
        line = (0 + last, 2 - last, 3 + last)[kind]
        column = quarter - 2 * last if kind == 1 else quarter - 3 * last
        if not isinstance(quarter, int):
            return self.stage[unit // 3].at[
                pl.ds(pl.multiple_of(line * rows, 16), rows), pl.ds(pl.multiple_of(column * width, 128), width)
            ]
        return self.stage[unit // 3].at[pl.ds(line * rows, rows), pl.ds(column * width, width)]

    def copy(self, unit, shard, quarter, rows, name, spot, device, source=None):
        ref = self.full.at[unit // 3, shard, quarter, unit % 3]
        ref = ref if rows is None else ref.at[rows]
        source = ref if source is None else source
        spot = (unit,) + spot
        return remote(source, ref, self.sems[name].at[(0,) + spot], self.sems[name].at[(1,) + spot], device)

    def z_copy(self, unit, step):
        at = self.place
        source = self.staged(unit, at.section)
        return self.copy(unit, at.dp, at.section, None, "z", (step - 1,), at.to_z(step), source)

    def side_copy(self, unit, step, way):
        at = self.place
        return self.copy(unit, at.from_z(step), at.section, None, "side", (step - 1, way), (at.to_x, at.to_y)[way])

    def corner_copy(self, unit, step, way):
        at = self.place
        half = self.full.shape[4] // 2
        quarter, target = (at.x_side, at.to_y) if way == 0 else (at.y_side, at.to_x)
        return self.copy(unit, at.from_z(step), quarter, pl.ds(way * half, half), "corner", (step - 1, way), target)

    def core_copy(self, unit, step, which):
        at = self.place
        if step == 0:
            return self.copy(unit, at.dp, which, None, "core", (0, which), at.to_core, self.staged(unit, which))
        quarter = (at.section, at.x_side, at.y_side, at.corner)[which]
        return self.copy(unit, at.from_z(step), quarter, None, "core", (step, which), at.to_core)

    def own_copy(self, unit, quarter):
        target = self.full.at[unit // 3, self.place.dp, quarter, unit % 3]
        return pltpu.make_async_copy(self.staged(unit, quarter), target, self.sems["own"].at[unit, quarter])

    def stage_copies(self, layer, qkv_w, attn_w, in_w, out_w):
        rows, width = self.full.shape[4:]
        pieces = [
            (qkv_w.at[layer], 0, 0, 3 * width),
            (attn_w.at[layer], 1, 0, width),
            (in_w.at[layer, :, pl.ds(0, 3 * width)], 2, 0, 3 * width),
            (in_w.at[layer, :, pl.ds(3 * width, width)], 1, 1, width),
        ]
        for quarter in range(4):
            pieces.append((out_w.at[layer, pl.ds(quarter * rows, rows)], 3 + quarter // 3, quarter % 3, width))
        made = []
        for i, (source, line, column, span) in enumerate(pieces):
            target = self.stage[layer].at[pl.ds(line * rows, rows), pl.ds(column * width, span)]
            made.append(pltpu.make_async_copy(source, target, self.sems["stage"].at[layer, i]))
        return made

    def release(self, layer):
        for unit in range(3 * layer, 3 * layer + 3):
            for step in self.steps:
                self.z_copy(unit, step).wait_send()
            for quarter in range(4):
                self.core_copy(unit, 0, quarter).wait_send()

    def begin(self, unit):
        for step in self.steps:
            self.z_copy(unit, step).start()
        for which in range(4):
            self.core_copy(unit, 0, which).start()
            self.own_copy(unit, which).start()

    def spread(self, unit):
        for step in self.steps:
            self.z_copy(unit, step).wait_recv()
            for way in range(2):
                self.side_copy(unit, step, way).start()
            self.core_copy(unit, step, 0).start()

    def relay(self, unit):
        for step in self.steps:
            for way in range(2):
                self.side_copy(unit, step, way).wait_recv()
                self.corner_copy(unit, step, way).start()
                self.core_copy(unit, step, 1 + way).start()

    def close(self, unit):
        for step in self.steps:
            for way in range(2):
                self.corner_copy(unit, step, way).wait_recv()
            self.core_copy(unit, step, 3).start()

    def arrive(self, unit):
        for quarter in range(4):
            self.own_copy(unit, quarter).wait()
        for step in range(self.place.count):
            for which in range(4):
                self.core_copy(unit, step, which).wait_recv()

    def drain(self, unit):
        for step in self.steps:
            for way in range(2):
                self.side_copy(unit, step, way).wait_send()
                self.corner_copy(unit, step, way).wait_send()
            for which in range(4):
                self.core_copy(unit, step, which).wait_send()


class Rows:
    def __init__(self, place, done, norms, slot_of, results, mail, send_sems, recv_sems, local_sems):
        self.place = place
        self.done = done
        self.norms = norms
        self.slot_of = slot_of
        self.send_sems = send_sems
        self.recv_sems = recv_sems
        self.local_sems = local_sems
        self.moves = []
        self.locals = []
        self.held = None
        at = place
        own = at.section
        shared = 4 + at.side
        other = 1 - at.side
        early, late = at.early, at.late
        self.base = (0, 2, 4, 2)
        for step in range(7):
            out = results[step // 4]
            if step in (0, 6):
                near = own if step == 0 else shared
                moves = [
                    (early, early, other, out.at[near], at.to_x),
                    (late, early, at.side, out.at[own], at.to_y),
                    (late, early, other, out.at[own], at.to_corner),
                ]
                if step == 6:
                    moves.pop()
                local = (early, out.at[near])
            elif step in (2, 4):
                near = own if step == 2 else shared
                moves = [
                    (late, late, other, out.at[near], at.to_x),
                    (early, late, at.side, out.at[own], at.to_y),
                    (early, late, other, out.at[own], at.to_corner),
                ]
                local = (late, out.at[near])
            elif step == 5:
                moves = [(None, None, other, out.at[own], at.to_x)]
                local = (None, out.at[own])
            else:
                mine = early if step == 1 else late
                moves = [(mine, mine, other, out.at[shared], at.to_x)]
                local = (mine, out.at[shared])
            if step == 4:
                moves.insert(0, (late, early, 0, mail, at.to_y))
            self.moves.append(moves)
            self.locals.append(local)

    def source(self, step, pick):
        return self.done.at[self.base[step] + pick] if step < 4 else self.norms.at[self.slot_of[step], pick]

    def make(self, step, number):
        _, _, pick, target, device = self.moves[step][number]
        src = self.source(step, pick)
        return remote(src, target, self.send_sems.at[step, number], self.recv_sems.at[step, number], device)

    def make_local(self, step):
        src = self.source(step, self.place.side)
        return pltpu.make_async_copy(src, self.locals[step][1], self.local_sems.at[step])

    def hold(self):
        self.held = []

    def let_go(self):
        held, self.held = self.held, None
        for step, which in held:
            self.ready(step, which)

    def ready(self, step, which):
        if self.held is not None:
            self.held.append((step, which))
            return
        for number, (sends, _, pick, _, _) in enumerate(self.moves[step]):
            if isinstance(pick, int):
                if pick == which:
                    when(sends, self.make(step, number).start)
            else:
                chosen = pick == which
                when(chosen if sends is None else sends & chosen, self.make(step, number).start)
        sends = self.locals[step][0]
        chosen = self.place.side == which
        when(chosen if sends is None else sends & chosen, self.make_local(step).start)

    def sent(self, step):
        for number, (sends, *_) in enumerate(self.moves[step]):
            when(sends, self.make(step, number).wait_send)
        when(self.locals[step][0], self.make_local(step).wait)

    def mail_here(self, step):
        when(self.moves[step][0][1], self.make(step, 0).wait_recv)

    def received(self, step):
        for number, (_, receives, *_) in enumerate(self.moves[step]):
            if step == 4 and number == 0:
                continue
            when(receives, self.make(step, number).wait_recv)


def mega_kernel(
    bucket, inputs, cotangent, qkv_w, attn_w, in_w, out_w,
    padding, down_w, down_b, up_w, up_b, gain, beta, query_b, value_b, attn_b, in_b, out_b,
    outputs, input_grads, full, spill, passing, grad_down_w, grad_down_b, grad_up_w, grad_up_b, grad_gain, grad_beta, ratio,
    attn_v, in_v, out_v, qkv, att, branches, norms, aux, slope, hid, keyb, done, acc, dqkv,
    adapters, vecs, grads, meet, shared_sums, parts, offers, halves,
    z_sem, side_sem, corner_sem, core_sem, own_sem, stage_sem, small_sem, load_sem, row_send, row_recv, row_local, misc_sem,
    part_sem, half_sem, pass_sem,
):
    at = Place()
    length, width = hid.shape[1:]
    chunks = in_v.shape[0]
    cols = [pl.ds(c * width, width) for c in range(chunks)]
    sems = {"z": z_sem, "side": side_sem, "corner": corner_sem, "core": core_sem, "own": own_sem, "stage": stage_sem}
    gather = Gather(full, (qkv.at[1], dqkv), sems, at)
    own = at.section
    shared = 4 + at.side
    early_one = jnp.where(at.early, 1, 0)
    late_one = 1 - early_one
    third_row = jnp.where(at.early, own, shared)
    slot_of = {4: 1 + late_one, 5: late_one, 6: 2 * early_one}
    keys_of = {4: late_one, 5: 0, 6: early_one}
    layer_of = {4: 1, 5: late_one, 6: 0}
    rows = Rows(at, done, norms, slot_of, (outputs, input_grads), hid.at[1], row_send, row_recv, row_local)

    low = hid.at[0]

    staging = [gather.stage_copies(layer, qkv_w, attn_w, in_w, out_w) for layer in range(2)]
    row_in = pltpu.make_async_copy(inputs.at[own], hid.at[0], misc_sem.at[2])
    row_shared = pltpu.make_async_copy(inputs.at[shared], branches.at[1, 0], misc_sem.at[3])
    cot_third = pltpu.make_async_copy(cotangent.at[third_row], hid.at[0], misc_sem.at[7])
    cot_own = pltpu.make_async_copy(cotangent.at[own], done.at[0], misc_sem.at[8])
    spills = [pltpu.make_async_copy(slope, spill.at[k], misc_sem.at[9 + k]) for k in range(3)]
    returns = {
        step: pltpu.make_async_copy(spill.at[slot_of[step]], slope, misc_sem.at[7 + step]) for step in (5, 6)
    }
    for copy in staging[0] + staging[1] + [row_in, row_shared]:
        copy.start()
    at.barrier()
    for copy in staging[0]:
        copy.wait()
    gather.begin(0)
    vecs[own] = jnp.zeros(vecs.shape[1:], F32)
    for place, ref in ((1, up_b), (2, gain), (3, beta)):
        vecs[own, place : place + 1] = ref[...]
    vecs[own, 4:5, : down_b.shape[1]] = down_b[...]
    adapters[own, :64] = down_w[0].astype(F32).T.astype(BF16)
    adapters[own, 64:] = up_w[0]
    shares = []
    passes = []
    part_of = pl.ds(pl.multiple_of(64 * at.core, 64), 64)
    for i, (device, whose) in enumerate(((at.to_x, at.x_side), (at.to_y, at.y_side), (at.to_corner, at.corner))):
        ref = adapters.at[own, part_of]
        shares.append(remote(ref, ref, small_sem.at[0, i], small_sem.at[1, i], device))
        ref = adapters.at[whose, part_of]
        passes.append(remote(ref, ref, small_sem.at[0, 6 + i], small_sem.at[1, 6 + i], at.to_core))
    for i, device in enumerate((at.to_x, at.to_y, at.to_corner)):
        shares.append(remote(vecs.at[own], vecs.at[own], small_sem.at[0, 3 + i], small_sem.at[1, 3 + i], device))
    for copy in shares:
        copy.start()
    for copy in staging[1]:
        copy.wait()
    grads[...] = jnp.zeros_like(grads)
    real_rows = jnp.concatenate([padding[...].astype(F32), jnp.zeros((8 - padding.shape[0], length), F32)], 0)
    spot = lanes(length) % 64
    place = lax.broadcasted_iota(jnp.int32, (length, 128), 0)
    for k, row in enumerate((own, shared)):
        chosen = jnp.where(lax.broadcasted_iota(jnp.int32, (8, 128), 0) == row, 1.0, 0.0)
        real = dot_tn(real_rows.astype(BF16), chosen.astype(BF16))
        shift = 6 + bucket[row]
        same = ((spot * SEG) >> shift) == (place >> shift)
        ones = jnp.where((spot >= LOG_TOP) & (spot < LOG_TOP + 3), 1.0, 0.0)
        held = jnp.where(spot < 8, jnp.where(same & (real > 0.5), 0.0, MASKED), jnp.where(spot == 16, real, ones))
        keyb[k] = held.astype(BF16)

    tasks = []
    for name, unit in (
        ("begin", 1), ("spread", 0), ("begin", 2), ("relay", 0),
        ("close", 0),
        ("spread", 1), ("begin", 3),
        ("relay", 1),
        ("spread", 2), ("begin", 4),
        ("close", 1),
        ("relay", 2),
        ("spread", 3), ("begin", 5),
        ("close", 2),
        ("spread", 4),
        ("relay", 3),
        ("spread", 5),
        ("close", 3),
        ("relay", 4),
        ("close", 4),
        ("relay", 5),
        ("close", 5),
    ):
        tasks.append((name, unit))

    def take(count):
        chosen = tasks[:count]
        del tasks[:count]

        def action():
            for name, unit in chosen:
                getattr(gather, name)(unit)

        return action

    def tasks_through(unit):
        if ("close", unit) in tasks:
            take(tasks.index(("close", unit)) + 1)()

    def load(kinds, layer, start=True):
        made = []
        for c in range(chunks):
            for kind in kinds:
                if kind < 2:
                    source, target = full.at[layer, :, c, kind], (attn_v, in_v)[kind].at[c]
                else:
                    span = out_v.shape[1]
                    source, target = full.at[layer, pl.ds(c * span, span), :, kind], out_v.at[c]
                made.append(pltpu.make_async_copy(source, target, load_sem.at[kind, c]))
        if start:
            for copy in made:
                copy.start()

    def loaded_all(kind):
        for c in range(chunks):
            loaded(kind, c)

    def loaded(kind, c):
        source = full.at[0, :, c, kind] if kind < 2 else full.at[0, pl.ds(0, out_v.shape[1]), :, kind]
        target = (attn_v, in_v, out_v)[kind].at[c]
        pltpu.make_async_copy(source, target, load_sem.at[kind, c]).wait()

    def vec(stage, row):
        return vecs[stage, row : row + 1]

    def adapter_part(stage, k, sub, hidden, branch, base, keys, counted):
        down_t = adapters[stage, :64]
        lift = adapters[stage, 64:]
        branch_low = branch.astype(BF16)
        branches[k, sub] = branch_low
        down = dot_nt(branch_low, down_t) + vec(stage, 4)[:, :64]
        act, _ = gelu_both(down)
        lifted = dot(act.astype(BF16), lift) + vec(stage, 1)
        hidden_float = hidden.astype(F32)
        resid = hidden_float + branch + lifted
        center = resid - jnp.mean(resid, -1, keepdims=True)
        inverse = lax.rsqrt(jnp.mean(center * center, -1, keepdims=True) + EPSILON)
        normed = center * inverse
        norms[k, sub] = normed.astype(BF16)
        done[base + sub] = (normed * vec(stage, 2) + vec(stage, 3)).astype(BF16)
        valid = keyb[keys, :, 16:17].astype(F32)
        if counted is not None:
            valid = valid * counted
        grads[stage, 132:133] += jnp.sum(lifted * lifted * valid, 0, keepdims=True)
        grads[stage, 133:134] += jnp.sum(hidden_float * hidden_float * valid, 0, keepdims=True)
        held = aux.at[k, sub]
        held[:, :64] = down
        held[...] = jnp.where(lanes(length) == 64, inverse, held[...])

    def heads(pair, hooks):
        def body(p, carry):
            pair(p)
            for i, hook in enumerate(hooks):
                pl.when(p == i)(hook)
            return carry

        lax.fori_loop(0, HEADS // 2, body, 0)

    def attention_forward(k, layer, hidden, base, keys, hooks, loads=0, counted=None, before_adapter=lambda: None):
        stage = 2 * layer
        if loads == 2:
            loaded_all(0)
        for part in range(3):
            if loads == 1:
                loaded(0, part)
            mixed = dot(hidden[...], square(attn_v, part))
            if part != 1:
                mixed = mixed + (query_b if part == 0 else value_b)[layer : layer + 1]
            qkv[k, :, cols[part]] = mixed.astype(BF16)
        aux[k, 0] = jnp.zeros((length, 128), F32)

        def pair(p):
            attention_pair_forward(p, 0, length, qkv.at[k], keyb.at[keys], att.at[k], aux.at[k, 0])

        heads(pair, hooks)
        if loads == 1:
            loaded(0, 3)
        branch = dot(att[k], square(attn_v, 3)) + attn_b[layer : layer + 1]
        before_adapter()
        adapter_part(stage, k, 0, hidden[...], branch, base, keys, counted)

    def ffn_forward(k, layer, base, keys, hooks, bank, loads=True, counted=None):
        stage = 2 * layer + 1
        if loads:
            loaded_all(1)
        for c in range(chunks):
            pre = dot(done[base], square(in_v, c)) + in_b[layer : layer + 1, c * width : (c + 1) * width]
            act, steep = gelu_both(pre)
            slope[:, cols[c]] = steep.astype(BF16)
            if loads and c == 0:
                loaded_all(2)
            term = dot(act.astype(BF16), square(out_v, c))
            if c == 0:
                acc[...] = term + out_b[layer : layer + 1]
            else:
                acc[...] += term
            if c < len(hooks):
                hooks[c]()
        aux[k, 1] = jnp.zeros((length, 128), F32)
        adapter_part(stage, k, 1, done[base], acc[...], base, keys, counted)

    def adapter_back(stage, k, sub, grad):
        down_t = adapters[stage, :64]
        lift = adapters[stage, 64:]
        grad = grad.astype(F32)
        normed = norms[k, sub].astype(F32)
        held = aux[k, sub]
        inverse = held[:, 64:65]
        down = held[:, :64]
        scaled = grad * vec(stage, 2)
        resid = inverse * (
            scaled
            - jnp.mean(scaled, -1, keepdims=True)
            - normed * jnp.mean(scaled * normed, -1, keepdims=True)
        )
        lift_grad = resid.astype(BF16)
        act, steep = gelu_both(down)
        down_grad = (dot_nt(lift_grad, lift) * steep).astype(BF16)
        grads[stage, 0:64] += dot_tn(act.astype(BF16), lift_grad)
        grads[stage, 64:128] += dot_tn(down_grad, branches[k, sub])
        grads[stage, 128:129] += jnp.sum(lift_grad.astype(F32), 0, keepdims=True)
        grads[stage, 129:130] += jnp.sum(normed * grad, 0, keepdims=True)
        grads[stage, 130:131] += jnp.sum(grad, 0, keepdims=True)
        grads[stage, 131:132, :64] += jnp.sum(down_grad.astype(F32), 0, keepdims=True)
        acc[...] = resid
        low[...] = (resid + dot(down_grad, down_t)).astype(BF16)

    def ffn_backward(step, source, after_adapter):
        k = slot_of[step]
        layer = layer_of[step]
        adapter_back(2 * layer + 1, k, 1, source[...])
        after_adapter()
        if step > 4:
            loaded_all(1)
            loaded_all(2)
        for c in range(chunks):
            act_grad = dot_nt(low[...], square(out_v, c))
            pre_grad = (act_grad * slope[:, cols[c]].astype(F32)).astype(BF16)
            acc[...] += dot_nt(pre_grad, square(in_v, c))
        norms[k, 1] = acc[...].astype(BF16)
        rows.ready(step, 1)

    def attention_backward(step, after_adapter, hooks):
        k = slot_of[step]
        keys = keys_of[step]
        layer = layer_of[step]
        adapter_back(2 * layer, k, 0, norms[k, 1])
        after_adapter()
        if step > 4:
            loaded_all(0)
        low[...] = dot_nt(low[...], square(attn_v, 3)).astype(BF16)

        def pair(p):
            attention_pair_backward(p, 0, length, qkv.at[k], keyb.at[keys], att.at[k], aux.at[k, 0], low, dqkv)

        heads(pair, hooks)
        for part in range(3):
            acc[...] += dot_nt(dqkv[:, cols[part]], square(attn_v, part))
        norms[k, 0] = acc[...].astype(BF16)
        rows.ready(step, 0)

    other = 1 - at.side
    half_rows = length // 2
    first_half, second_half = pl.ds(0, half_rows), pl.ds(half_rows, half_rows)
    row_src = norms.at[slot_of[6], other]
    straight = remote(
        row_src.at[first_half], input_grads.at[own, first_half], pass_sem.at[0, 0], pass_sem.at[1, 0], at.to_corner
    )
    half_in = remote(row_src.at[second_half], passing, pass_sem.at[0, 1], pass_sem.at[1, 1], at.to_y)
    half_out = remote(passing, input_grads.at[at.y_side, second_half], pass_sem.at[0, 2], pass_sem.at[1, 2], at.to_x)

    def corner_rows(which):
        @pl.when(at.late & (other == which))
        def _():
            straight.start()
            half_in.start()

    def pass_on(side):
        @pl.when(at.early & (at.side == side))
        def _():
            half_in.wait_recv()
            half_out.start()

    def passed():
        @pl.when(at.late)
        def _():
            straight.wait_send()
            half_in.wait_send()

        @pl.when(at.early)
        def _():
            straight.wait_recv()
            half_out.wait()

    span = GRAD_ROWS // 2
    mine = pl.ds(pl.multiple_of(at.core * span, 8), span)
    theirs = pl.ds(pl.multiple_of((1 - at.core) * span, 8), span)

    def meet_copy(stage):
        return remote(grads.at[stage, theirs], meet.at[MEET[stage]], half_sem.at[0, stage], half_sem.at[1, stage], at.to_core)

    def met(stage):
        meet_copy(stage).wait()
        grads[stage, mine] += meet[MEET[stage]]
        shared_sums[stage] = grads[stage, mine].astype(BF16)

    def part_copy(slot, stage, device):
        return remote(shared_sums.at[stage], parts.at[slot], part_sem.at[0, slot], part_sem.at[1, slot], device)

    other = 1 - at.side
    upper = [(at.early, 1, 2 + at.side, at.to_y), (at.early, 2, 2 + other, at.to_corner), (at.late, 0, 2 + other, at.to_x)]
    lower = [(at.late, 1, at.side, at.to_y), (at.late, 2, other, at.to_corner), (at.early, 0, other, at.to_x)]

    def meet_upper():
        meet_copy(2).start()
        meet_copy(3).start()

    def send_upper():
        met(2)
        met(3)
        for condition, slot, stage, device in upper:
            pl.when(condition)(part_copy(slot, stage, device).start)

    def send_lower(which):
        met(which)
        for condition, slot, stage, device in lower:
            pl.when(condition & (stage == which))(part_copy(slot, stage, device).start)

    near = (at.section, (at.z + 1 - 2 * (at.z % 2)) * 2 + at.core)
    far = at.to_z(2)
    total = grads.at[own, mine]
    trades = [
        remote(offers.at[0], halves.at[0], half_sem.at[0, 4], half_sem.at[1, 4], near),
        remote(offers.at[1], halves.at[1], half_sem.at[0, 5], half_sem.at[1, 5], far),
        remote(total, meet.at[2], half_sem.at[0, 6], half_sem.at[1, 6], at.to_core),
    ]

    def collect():
        for slot in range(3):
            part_copy(slot, 0, at.to_x).wait_recv()
        found = grads[own, mine] + parts[0].astype(F32) + parts[1].astype(F32) + parts[2].astype(F32)
        offers[0] = found.astype(BF16)
        trades[0].start()

    def fold(number):
        def action():
            trades[number].wait()
            found = offers[number].astype(F32) + halves[number].astype(F32)
            if number < 1:
                offers[1] = found.astype(BF16)
                trades[1].start()
            else:
                grads[own, mine] = found
                trades[2].start()

        return action

    def nothing():
        pass

    counted = jnp.where(at.early, 1.0, 0.0)
    rows.hold()
    row_in.wait()
    take(4)()
    for copy in shares:
        copy.wait()
    for copy in passes:
        copy.start()
    take(1)()
    gather.arrive(0)
    load((0,), 0)
    take(2)()

    def adapters_here():
        for copy in passes:
            copy.wait()

    attention_forward(0, 0, hid.at[0], 0, 0, [nothing] * 4 + [take(1)], 1, None, adapters_here)
    take(2)()
    rows.ready(0, 0)
    cot_third.start()
    row_shared.wait()
    attention_forward(2, 0, branches.at[1, 0], 2, 1, [take(1), nothing, nothing, nothing, nothing, take(1)], 0, counted)
    rows.ready(1, 0)
    take(2)()
    gather.arrive(1)
    load((1,), 0)
    take(1)()
    gather.arrive(2)
    load((2,), 0)
    ffn_forward(0, 0, 0, 0, [nothing, nothing, take(1), take(1)], 0)
    rows.ready(0, 1)
    spills[0].start()
    spills[0].wait()
    spread_last = take(1)
    relay_two = take(2)

    def attention_next():
        relay_two()
        gather.arrive(3)
        load((0,), 1)

    ffn_forward(2, 0, 2, 1, [nothing, nothing, spread_last, attention_next], 1, False, counted)
    rows.ready(1, 1)
    spills[2].start()
    gather.release(0)
    attention_forward(1, 1, done.at[1], 4, 0, [nothing] * 5 + [take(1)], 2)
    take(1)()
    rows.ready(2, 0)
    gather.arrive(4)
    load((1,), 1)
    last = take(1)

    @pl.when(at.late)
    def _():
        attention_forward(2, 1, done.at[3], 2, 1, [nothing] * 4 + [last])

    pl.when(at.early)(last)
    rows.ready(3, 0)
    rows.let_go()
    gather.arrive(5)
    load((2,), 1)
    spills[2].wait()
    ffn_forward(1, 1, 4, 0, [], 0)
    rows.ready(2, 1)
    spills[1].start()
    spills[1].wait()

    @pl.when(at.late)
    def _():
        ffn_forward(2, 1, 2, 1, [], 1, False)

    rows.ready(3, 1)
    gather.release(1)
    cot_third.wait()
    ffn_backward(4, hid.at[0], nothing)
    returns[5].start()
    load((1, 2), layer_of[5])

    def own_grad_in():
        rows.sent(0)
        pl.when(at.late)(cot_own.start)

    attention_backward(4, nothing, [nothing] * 5 + [own_grad_in])
    load((0,), layer_of[5])
    pl.when(at.late)(cot_own.wait)

    @pl.when(at.early)
    def _():
        done[0] = norms[slot_of[4], 0]

    returns[5].wait()
    ffn_backward(5, done.at[0], nothing)
    returns[6].start()
    load((1, 2), 0)
    attention_backward(5, meet_upper, [nothing, nothing, nothing, send_upper])
    load((0,), 0)
    rows.mail_here(4)

    @pl.when(at.late)
    def _():
        hid[1] = norms[slot_of[5], 0]

    returns[6].wait()
    rows.hold()
    ffn_backward(6, hid.at[1], meet_copy(1).start)
    send_lower(1)
    rows.let_go()
    corner_rows(1)
    attention_backward(6, meet_copy(0).start, [nothing, lambda: send_lower(0)])
    corner_rows(0)
    pass_on(0)
    collect()
    pass_on(1)
    for unit in range(3):
        gather.drain(unit)
    fold(0)()
    for unit in range(3, 6):
        gather.drain(unit)
    fold(1)()
    trades[2].wait()
    grads[own, theirs] = meet[2]
    grad_down_w[0] = grads[own, 64:128].T
    grad_down_b[...] = grads[own, 131:132, : down_b.shape[1]]
    grad_up_w[0] = grads[own, 0:64]
    for out, line in ((grad_up_b, 128), (grad_gain, 129), (grad_beta, 130)):
        out[...] = grads[own, line : line + 1]
    squares = jnp.sum(grads[own, 132:134], -1, keepdims=True)
    ratio[...] = jnp.sqrt(squares[0:1] / squares[1:2])
    for slot in range(3):
        part_copy(slot, 0, at.to_x).wait_send()
    for step in range(7):
        if step > 0:
            rows.sent(step)
        rows.received(step)
    passed()


def everything(bucket, inputs, cotangent, weights, small):
    length, width = inputs.shape[1:]
    shard_rows = weights[0].shape[1]
    shards = lax.axis_size("dp")
    count = shards // 2
    ffn = weights[2].shape[2]
    half = GRAD_ROWS // 2
    anyspec = pl.BlockSpec(memory_space=pl.ANY)
    vmem = pl.BlockSpec(memory_space=pltpu.VMEM)
    dma = pltpu.SemaphoreType.DMA
    row = (length, width)
    scratch = [
        pltpu.VMEM((4, shards, shard_rows, width), BF16),
        pltpu.VMEM((4, shards, shard_rows, width), BF16),
        pltpu.VMEM((4, shards // 4, 4, shard_rows, width), BF16),
        pltpu.VMEM((3, length, 3 * width), BF16),
        pltpu.VMEM((3,) + row, BF16),
        pltpu.VMEM((3, 2) + row, BF16),
        pltpu.VMEM((3, 2) + row, BF16),
        pltpu.VMEM((3, 2, length, 128), F32),
        pltpu.VMEM((length, ffn), BF16),
        pltpu.VMEM((2,) + row, BF16),
        pltpu.VMEM((2, length, 128), BF16),
        pltpu.VMEM((6,) + row, BF16),
        pltpu.VMEM(row, F32),
        pltpu.VMEM((length, 3 * width), BF16),
        pltpu.VMEM((4, 128, width), BF16),
        pltpu.VMEM((4, 8, width), F32),
        pltpu.VMEM((4, GRAD_ROWS, width), F32),
        pltpu.VMEM((3, half, width), F32),
        pltpu.VMEM((4, half, width), BF16),
        pltpu.VMEM((3, half, width), BF16),
        pltpu.VMEM((2, half, width), BF16),
        pltpu.VMEM((2, half, width), BF16),
        dma((2, 6, count - 1)),
        dma((2, 6, count - 1, 2)),
        dma((2, 6, count - 1, 2)),
        dma((2, 6, count, 4)),
        dma((6, 4)),
        dma((2, 8)),
        dma((2, 9)),
        dma((3, 4)),
        dma((7, 4)),
        dma((7, 4)),
        dma((7,)),
        dma((14,)),
        dma((2, 3)),
        dma((2, 7)),
        dma((2, 3)),
    ]
    outs = [
        (inputs.shape, BF16), (inputs.shape, BF16), ((2, shards, 4, 3, shard_rows, width), BF16),
        ((3, length, ffn), BF16), ((length // 2, width), BF16), ((1, width, 64), F32), ((1, 64), F32), ((1, 64, width), F32), ((1, width), F32),
        ((1, width), F32), ((1, width), F32), ((1, 1), F32),
    ]
    return pl.pallas_call(
        mega_kernel,
        in_specs=[pl.BlockSpec(memory_space=pltpu.SMEM)] + [anyspec] * 6 + [vmem] * len(small),
        out_specs=[anyspec] * 5 + [vmem] * 7,
        out_shape=[jax.ShapeDtypeStruct(shape, dtype) for shape, dtype in outs],
        scratch_shapes=scratch,
        compiler_params=pltpu.CompilerParams(
            collective_id=1, has_side_effects=True, vmem_limit_bytes=MEGA_BYTES
        ),
        cost_estimate=pl.CostEstimate(flops=90_000_000_000, bytes_accessed=200_000_000, transcendentals=0),
        name="everything",
    )(bucket, inputs, cotangent, *weights, *small)


X_PAIRS = [(0, 1), (1, 0), (2, 3), (3, 2)]
Y_PAIRS = [(0, 2), (2, 0), (1, 3), (3, 1)]
CROSS = [(0, 3), (3, 0), (1, 2), (2, 1)]


def send(value, pairs, senders=(0, 1, 2, 3)):
    return lax.ppermute(value, "section", [pair for pair in pairs if pair[0] in senders])


def gather_weights(shards):
    section = lax.axis_index("section")
    quarter = lax.dynamic_index_in_dim(shards, section, 0, keepdims=False)
    full = lax.all_gather(quarter, ("dp", "section"), axis=0, tiled=False)
    count = lax.axis_size("dp")
    full = full.reshape((count, lax.axis_size("section")) + quarter.shape)
    return full


def in_quarters(matrix):
    rows, columns = matrix.shape
    return matrix.reshape(rows, 4, columns // 4).transpose(1, 0, 2)


def block_rows(full, kind, by_rows):
    if full.shape[3] % 16 == 0:
        return (full, kind)
    count, quarters, _, rows, width = full.shape
    one = full[:, :, kind]
    if by_rows:
        return (one.reshape(count * rows * quarters // width, quarters, 1, width // quarters, width), 0)
    return (one.transpose(1, 0, 2, 3).reshape(1, quarters, 1, count * rows, width), 0)


def on_device(
    inputs, bucket, padding, cotangent, down_weight, down_bias, up_weight, up_bias, ln_gain, ln_beta, qkv_weight,
    query_bias, value_bias, attn_out_weight, attn_out_bias, ffn_in_weight, ffn_in_bias, ffn_out_weight, ffn_out_bias,
):
    section = lax.axis_index("section")
    early = section < 2
    side = section % 2
    width = inputs.shape[2]
    adapter_width = down_weight.shape[2]
    layers = qkv_weight.shape[0]

    def layer_shards(layer):
        attn = jnp.concatenate([qkv_weight[layer], attn_out_weight[layer]], 1)
        outer = ffn_out_weight[layer]
        return (
            in_quarters(attn)[:, None],
            jnp.stack([in_quarters(ffn_in_weight[layer]), outer.reshape((4, -1) + outer.shape[1:])], 1),
        )

    def results(outputs, input_grads, total):
        ratios = jnp.sqrt(jnp.sum(total[132]) / jnp.sum(total[133]))[None]
        return (
            outputs[None],
            input_grads[None],
            total[64:128].T[None],
            total[131, :adapter_width][None],
            total[0:64][None],
            total[128][None],
            total[129][None],
            total[130][None],
            ratios,
        )

    if lax.axis_size("dp") == 8 and lax.axis_size("section") == 4 and inputs.shape[0] == 6:
        found = everything(
            bucket, inputs, cotangent, (qkv_weight, attn_out_weight, ffn_in_weight, ffn_out_weight),
            (
                padding, down_weight, down_bias, up_weight, up_bias, ln_gain, ln_beta, query_bias, value_bias,
                attn_out_bias, ffn_in_bias, ffn_out_bias,
            ),
        )
        return (found[0][None], found[1][None]) + tuple(found[5:11]) + (found[11][0],)

    zero_row = jnp.zeros((1, width), F32)
    own_vec = jnp.concatenate(
        [zero_row, up_bias, ln_gain, ln_beta, jnp.pad(down_bias, ((0, 0), (0, width - adapter_width))), zero_row, zero_row, zero_row], 0
    )
    own_adapter = jnp.concatenate([down_weight[0].T, up_weight[0]], 0)
    biases = jnp.zeros((layers, 2, 8, width), F32)
    biases = biases.at[:, 0, 0].set(attn_out_bias).at[:, 0, 5].set(query_bias).at[:, 0, 6].set(value_bias)
    biases = biases.at[:, 1, 0].set(ffn_out_bias)
    in_bias = ffn_in_bias[:, None, :]
    table = key_table(bucket, padding)

    weights = []
    for layer in range(layers):
        full = gather_weights(jnp.concatenate(layer_shards(layer), 1))
        weights.append([block_rows(full, 0, False), block_rows(full, 1, False), block_rows(full, 2, True)])
    adapters = lax.all_gather(own_adapter, "section", axis=0, tiled=False)
    vecs = lax.all_gather(own_vec, "section", axis=0, tiled=False)
    adapters = adapters.reshape(layers, 2, 128, width)
    vecs = vecs.reshape(layers, 2, 8, width)
    vecs = (vecs + biases).reshape(layers, 16, width)
    own = section
    shared = 4 + side

    def row_of(array, row):
        return lax.dynamic_index_in_dim(array, row, 0, keepdims=False)

    def forward(row, hidden, layer, weights_used, choice):
        return forward_pair(
            layer, choice, row_of(bucket, row), hidden, row_of(table, row), weights_used, adapters, vecs, in_bias
        )

    def backward(row, grad, saved, layer, weights_used, choice):
        return backward_pair(
            layer, choice, row_of(bucket, row), grad, row_of(table, row), saved, weights_used, adapters, vecs
        )

    zero = jnp.int32(0)
    one = jnp.int32(1)
    late = 1 - early.astype(jnp.int32)
    first_row = jnp.where(early, shared, own)
    third_row = jnp.where(early, own, shared)

    f0 = forward(first_row, row_of(inputs, first_row), zero, weights[:1], zero)
    x0 = send(jnp.where(side == 0, f0[1], f0[0]), X_PAIRS, (0, 1))
    y0 = send(jnp.where(early | (side == 1), f0[1], f0[0]), Y_PAIRS)
    z0 = send(jnp.where(side == 0, f0[1], f0[0]), CROSS, (2, 3))
    hidden = jnp.where(early, row_of(inputs, own), f0[1])
    f1 = forward(own, hidden, late, weights, late)
    x1 = send(jnp.where(side == 0, f1[1], f1[0]), X_PAIRS)
    hidden = jnp.where(early, f1[1], y0)
    f2 = forward(third_row, hidden, one, weights[1:], zero)
    x2 = send(jnp.where(side == 0, f2[1], f2[0]), X_PAIRS, (2, 3))
    y2 = send(jnp.where(side == 1, f2[1], f2[0]), Y_PAIRS, (0, 1))
    z2 = send(jnp.where(side == 0, f2[1], f2[0]), CROSS, (0, 1))

    b3 = backward(third_row, row_of(cotangent, third_row), f2[2:11], one, weights[1:], zero)
    x3 = send(jnp.where(side == 0, b3[0], b3[1]), X_PAIRS, (2, 3))
    y3 = send(jnp.where(early & (side == 1), b3[0], b3[1]), Y_PAIRS)
    z3 = send(jnp.where(side == 0, b3[0], b3[1]), CROSS, (0, 1))
    grad = jnp.where(early, b3[1], row_of(cotangent, own))
    b4 = backward(own, grad, f1[2:11], late, weights, late)
    x4 = send(jnp.where(side == 0, b4[0], b4[1]), X_PAIRS)
    grad = jnp.where(early, y3, b4[1])
    b5 = backward(first_row, grad, f0[2:11], zero, weights[:1], zero)
    x5 = send(jnp.where(side == 0, b5[0], b5[1]), X_PAIRS, (0, 1))
    y5 = send(jnp.where(side == 1, b5[0], b5[1]), Y_PAIRS, (2, 3))
    z5 = send(jnp.where(side == 0, b5[0], b5[1]), CROSS, (2, 3))

    def assemble(parts):
        result = jnp.zeros(inputs.shape, BF16)
        for row, part in parts:
            result = lax.dynamic_update_index_in_dim(result, part, row, 0)
        return result

    other = section + 1 - 2 * side
    across = jnp.where(early, section + 2, section - 2)
    corner = 3 - section
    other_shared = 4 + 1 - side
    outputs = assemble(
        [
            (own, jnp.where(side == 0, f1[0], f1[1])),
            (other, x1),
            (across, jnp.where(early, y0, y2)),
            (corner, jnp.where(early, z0, z2)),
            (shared, jnp.where(early, jnp.where(side == 0, f0[0], f0[1]), jnp.where(side == 0, f2[0], f2[1]))),
            (other_shared, jnp.where(early, x0, x2)),
        ]
    )
    input_grads = assemble(
        [
            (own, jnp.where(side == 0, b4[1], b4[0])),
            (other, x4),
            (across, jnp.where(early, y5, y3)),
            (corner, jnp.where(early, z5, z3)),
            (shared, jnp.where(early, jnp.where(side == 0, b5[1], b5[0]), jnp.where(side == 0, b3[1], b3[0]))),
            (other_shared, jnp.where(early, x5, x3)),
        ]
    )

    def with_sums(grads, sums):
        return grads.at[:, 132:134].set(sums[:4].reshape(2, 2, width))

    g3, g4, g5 = with_sums(b3[2], f2[11]), with_sums(b4[2], f1[11]), with_sums(b5[2], f0[11])
    low_layer = g5 + jnp.where(early, g4, 0.0)
    high_layer = g3 + jnp.where(early, 0.0, g4)
    mine = lax.psum_scatter(jnp.concatenate([low_layer, high_layer], 0), "section", scatter_dimension=0, tiled=False)
    return results(outputs, input_grads, lax.psum(mine, "dp"))


def solution(mesh):
    in_specs = (
        P("dp", None, None),
        P("dp"),
        P("dp", None),
        P("dp", None, None),
        P("section", None, None),
        P("section", None),
        P("section", None, None),
        P("section", None),
        P("section", None),
        P("section", None),
        P(None, "dp", None),
        P(),
        P(),
        P(None, "dp", None),
        P(),
        P(None, "dp", None),
        P(),
        P(None, "dp", None),
        P(),
    )
    out_specs = (
        P("section", "dp", None, None),
        P("section", "dp", None, None),
        P("section", None, None),
        P("section", None),
        P("section", None, None),
        P("section", None),
        P("section", None),
        P("section", None),
        P("section"),
    )
    return jax.shard_map(
        on_device, mesh=mesh, in_specs=in_specs, out_specs=out_specs, check_vma=False
    )
```
